32 devices in a mesh: dp: 2 (over core), hid: 4 (over y, x), mod: 4 (over z).
Axes of the slice: x: 2, y: 2, z: 4, core: 2. Of those that a mesh axis runs over, the one named last changes fastest.
Arguments:
- patches: bfloat16 [4, 1625088], P('mod', ('dp', 'hid')), may hold values from -6 to 6
- visible: int32 [16], P(('dp', 'hid')), may hold values from 265 to 529, as said below
- project_in: bfloat16 [3, 768, 768], P(None, ('dp', 'hid'), 'mod'), may hold values from -0.21875 to 0.21875
- project_out: bfloat16 [768, 768], P('mod', ('dp', 'hid')), may hold values from -1.5 to 1.5
- expand: bfloat16 [768, 3072], P('mod', ('dp', 'hid')), may hold values from -0.21875 to 0.21875
- contract: bfloat16 [3072, 768], P(('dp', 'hid'), 'mod'), may hold values from -0.109375 to 0.109375
- expand_bias: bfloat16 [3072], P(('dp', 'hid')), may hold values from -1.5 to 1.5
- vectors: float32 [8, 768], P(None, 'mod'), may hold values from -1.2 to 1.8, as said below
- cotangent: bfloat16 [4, 1625088], P('mod', ('dp', 'hid')), may hold values from -6 to 6
Outputs:
- output: bfloat16 [4, 1625088], P('mod', ('dp', 'hid'))
- input_grad: float32 [4, 1625088], P('mod', ('dp', 'hid'))
- project_in_grad: float32 [3, 768, 768], P(None, ('dp', 'hid'), 'mod')
- project_out_grad: float32 [768, 768], P('mod', ('dp', 'hid'))
- expand_grad: float32 [768, 3072], P('mod', ('dp', 'hid'))
- contract_grad: float32 [3072, 768], P(('dp', 'hid'), 'mod')
- expand_bias_grad: float32 [3072], P(('dp', 'hid'))
- vectors_grad: float32 [8, 768], P(None, 'mod')
The draws below stay inside these ranges and needn't reach their ends.
Inputs may be any that keep to these rules, and one draw needn't show every extreme that they name: visible patches of each strip; in every draw some strip keeps all 529. `vectors`: rows 0 and 5 are gains, the other rows biases.
All inputs are finite; a program needn't handle non-finite values.
Results may differ from the reference program's by a relative error of at most 0.019.
Values may be sent and summed in bfloat16 or wider, within the bound.
No kernel may reach another device: no remote copies, remote signals or barrier semaphores. Data moves between devices by JAX's collectives and lax.ppermute only.
A program may use at most 128 MiB of HBM per device.

```python
import jax
import jax.numpy as jnp
from jax import lax

D = 768
HEADS = 12
HEAD_DIM = 64
FF = 3072
L = 529
SH = 2
STRIPS = 16
FEAT = 192
N_MOD = 4


def draw_visible(key, part):
    key = jax.random.fold_in(key, 11)
    first, second = jax.random.split(key)
    masked = jax.random.randint(first, (STRIPS,), 0, L // 2 + 1)
    whole = jax.random.randint(second, (), 0, STRIPS)
    counts = L - masked
    return jnp.where(jnp.arange(STRIPS) == whole, L, counts).astype(jnp.int32)


def draw_vectors(key, part):
    key = jax.random.fold_in(key, 23)
    noise = jnp.clip(jax.random.normal(key, (8, D), jnp.float32), -4.0, 4.0)
    order = jnp.arange(8)[:, None]
    gains = (order == 0) | (order == 5)
    return jnp.where(gains, 1.0 + 0.2 * noise, 0.3 * noise).astype(jnp.float32)


def block_scale(own_key, dims, cuts, least, high):
    def one(position, shards_of):
        draws = jax.random.uniform(jax.random.fold_in(jax.random.fold_in(own_key, 6), position), (shards_of,), jnp.float32, least / len(cuts), high / len(cuts))
        return jnp.repeat(jnp.exp(draws), dims[position] // shards_of).reshape((-1,) + (1,) * (len(dims) - position - 1))

    factor_of = one(*cuts[0])
    for cut in cuts[1:]:
        factor_of = factor_of * one(*cut)
    return factor_of


def centred(key, shape, scale, most, pieces=(), kind=jnp.bfloat16):
    level = block_scale(key, shape, pieces, -0.22, 0.18) if pieces else 1.0
    drawn = jax.random.normal(key, shape, jnp.float32) * scale * level
    return jnp.minimum(jnp.maximum(drawn, -most), most).astype(kind)


def setup_inputs(seed: int = 0) -> dict:
    key_of = jax.random.split(jax.random.key(seed), 10)
    return {
        "patches": centred(key_of[0], (N_MOD, STRIPS * L * FEAT), 1.0, 6.0, ((0, 4), (1, 8))),
        "visible": draw_visible(jax.random.fold_in(key_of[9], 71), 0),
        "project_in": centred(key_of[2], (3, D, D), D ** -0.5, 0.21875, ((1, 8), (2, 4))),
        "project_out": centred(key_of[3], (D, D), (D // 48) ** -0.5, 1.5, ((0, 4), (1, 8))),
        "expand": centred(key_of[4], (D, FF), D ** -0.5, 0.21875, ((0, 4), (1, 8))),
        "contract": centred(key_of[5], (FF, D), FF ** -0.5, 0.109375, ((0, 8), (1, 4))),
        "expand_bias": centred(key_of[6], (FF,), 0.3, 1.5, ((0, 8),)),
        "vectors": draw_vectors(jax.random.fold_in(key_of[9], 71), 0),
        "cotangent": centred(key_of[8], (N_MOD, STRIPS * L * FEAT), 1.0, 6.0, ((0, 4), (1, 8))),
    }


eps = 1e-06
highest = lax.Precision.HIGHEST

@jax.custom_vjp
def low(v):
    return lax.optimization_barrier(v.astype(jnp.bfloat16)).astype(jnp.float32)

@jax.custom_vjp
def low_back(v):
    return v

def low_keep(v):
    return (low(v), None)

def low_pass(kept, grad):
    return (grad,)

def back_keep(v):
    return (v, None)

def back_low(kept, grad):
    return (low(grad),)
low.defvjp(low_keep, low_pass)
low_back.defvjp(back_keep, back_low)

def norm_rows(values, gain, shift):
    center = lax.optimization_barrier(jnp.mean(values, axis=-1, keepdims=True))
    moved = values - center
    spread = lax.optimization_barrier(jnp.mean(moved * moved, axis=-1, keepdims=True))
    return moved * lax.rsqrt(spread + eps) * gain + shift

def unpack_rows(flat):
    return flat.reshape(N_MOD, STRIPS, L, FEAT).transpose(1, 2, 0, 3).reshape(STRIPS, L, D)

def pack_rows(whole):
    return whole.reshape(STRIPS, L, N_MOD, FEAT).transpose(2, 0, 1, 3).reshape(N_MOD, STRIPS * L * FEAT)

def strip_layer(params, block, counts):
    project_in, project_out, expand, contract, expand_bias, vectors = params
    number = block.shape[0]
    places = jnp.arange(L)
    valid = (places[None, :] < counts[:, None]).astype(jnp.float32)
    normed = low(norm_rows(block, vectors[0], vectors[1]))
    projected = jnp.einsum('gld,tdc->tglc', normed, project_in, precision=highest)
    queries = low(low_back(projected[0] + vectors[2])).reshape(number, L, HEADS, HEAD_DIM)
    keys = low(low_back(projected[1])).reshape(number, L, HEADS, HEAD_DIM)
    values = low(low_back(projected[2] + vectors[3])).reshape(number, L, HEADS, HEAD_DIM)
    logits = low_back(jnp.einsum('gqhc,gkhc->ghqk', queries, keys, precision=highest) * HEAD_DIM ** (-0.5))
    logits = jnp.where(valid[:, None, None, :] > 0.5, logits, -1e+30)
    top = lax.optimization_barrier(jnp.max(logits, axis=-1, keepdims=True))
    expo = jnp.exp(logits - top)
    weights = expo / lax.optimization_barrier(jnp.sum(expo, axis=-1, keepdims=True))
    mixed = jnp.einsum('ghqk,gkhc->gqhc', low(weights), values, precision=highest).reshape(number, L, D)
    mixed = low(low_back(mixed))
    branch = low_back(jnp.einsum('gle,ed->gld', mixed, project_out, precision=highest) + vectors[4])
    resid = block + branch
    normed_mlp = low(norm_rows(resid, vectors[5], vectors[6]))
    pre = low_back(jnp.einsum('gld,df->glf', normed_mlp, expand, precision=highest) + expand_bias)
    hidden = low(jax.nn.gelu(pre, approximate=False))
    mlp_out = low_back(jnp.einsum('glf,fd->gld', hidden, contract, precision=highest) + vectors[7])
    return valid[:, :, None] * (resid + mlp_out)

def reference(patches, visible, project_in, project_out, expand, contract, expand_bias, vectors, cotangent):
    params = tuple((item.astype(jnp.float32) for item in (project_in, project_out, expand, contract, expand_bias, vectors)))
    stream = unpack_rows(patches.astype(jnp.float32))
    groups = visible.reshape(-1, SH)

    def forward(inputs, weights_all):
        blocks = inputs.reshape(-1, SH, L, D)
        layer = jax.checkpoint(lambda block, counts: strip_layer(weights_all, block, counts))
        result = lax.map(lambda pair: layer(pair[0], pair[1]), (blocks, groups))
        return result.reshape(STRIPS, L, D)
    final, backward = jax.vjp(forward, stream, params)
    input_grad, grads = backward(unpack_rows(cotangent.astype(jnp.float32)))
    return (pack_rows(final).astype(jnp.bfloat16), pack_rows(input_grad), grads[0], grads[1], grads[2], grads[3], grads[4], grads[5])
```

```python
from functools import partial

import jax
import jax.numpy as jnp
from jax import lax
from jax.sharding import PartitionSpec as P

D = 768
HEAD_DIM = 64
L = 529
FEAT = 192
HALF = 265
PAD = 272
ROWS = 2 * PAD
WIDE = 2 * FEAT
UNITS = D // 8
eps = 1e-06
bf16 = jnp.bfloat16
f32 = jnp.float32

X = [(0, 1), (1, 0), (2, 3), (3, 2)]
Y = [(0, 2), (2, 0), (1, 3), (3, 1)]


def dot(a, b, ca=1, cb=0):
    return lax.dot_general(a, b, (((ca,), (cb,)), ((), ())), preferred_element_type=f32)


def over_x(v):
    return lax.ppermute(v, "hid", X)


def over_y(v):
    return lax.ppermute(v, "hid", Y)


def over_core(v):
    n = lax.axis_size("dp")
    return lax.ppermute(v, "dp", [(i, i ^ 1) for i in range(n)])


def over_z(v, shift):
    n = lax.axis_size("mod")
    return lax.ppermute(v, "mod", [(i, (i + shift) % n) for i in range(n)])


def row_pairs(second, back):
    pairs = []
    for dp in range(lax.axis_size("dp")):
        for z in range(4):
            core = dp % 2
            parity = 1 - z % 2 if second else z % 2
            src, dst = dp * 4 + z, (dp - core + z // 2) * 4 + 2 * core + parity
            pairs.append((dst, src) if back else (src, dst))
    return pairs


def rows_there(v, second):
    return lax.ppermute(v, ("dp", "mod"), row_pairs(second, False))


def rows_back(v, second):
    return lax.ppermute(v, ("dp", "mod"), row_pairs(second, True))


def pack(pin, pout, ex, con, bias, vec):
    top = jnp.concatenate([pin[0], pin[1]], 1)
    low = jnp.concatenate([pin[2], pout.T], 1)
    hi = lax.reduce_precision(vec, 8, 7)
    lo = vec - hi
    vecs = jnp.pad(jnp.concatenate([hi, lo], 1).astype(bf16), ((0, 8), (0, 0)))
    attn = jnp.concatenate([top, low, vecs], 0)
    ffn = jnp.concatenate([ex, con.T, jnp.pad(bias[None], ((0, 15), (0, 0)))], 0)
    return attn, ffn


def natural(parts, z):
    order = (z - jnp.arange(4)) % 4
    return jnp.take(jnp.stack(parts), order, axis=0)


def norm(v, gain, shift):
    center = jnp.mean(v, 1, keepdims=True)
    moved = v - center
    inverse = lax.rsqrt(jnp.mean(moved * moved, 1, keepdims=True) + eps)
    normed = moved * inverse
    return normed, inverse, normed * gain + shift


def norm_back(grad, normed, inverse, gain):
    t = grad * gain
    return inverse * (t - jnp.mean(t, 1, keepdims=True) - normed * jnp.mean(t * normed, 1, keepdims=True))


def unflat(own1, own2, oth1, oth2, core, parity):
    def arrange(a, b):
        return jnp.where(parity == 0, a, b), jnp.where(parity == 0, b, a)

    own = arrange(own1, own2)
    oth = arrange(oth1, oth2)
    quarters = [jnp.where(core == 0, own[0], oth[0]), jnp.where(core == 0, own[1], oth[1]),
                jnp.where(core == 0, oth[0], own[0]), jnp.where(core == 0, oth[1], own[1])]
    quarters = [q.reshape(HALF, WIDE) for q in quarters]
    left = jnp.concatenate([q[:, :FEAT] for q in quarters], 1)
    right = jnp.concatenate([q[:, FEAT:] for q in quarters], 1)
    gap = ((0, PAD - HALF), (0, 0))
    return jnp.concatenate([jnp.pad(left, gap), jnp.pad(right, gap)], 0)


def reflat(v, core, parity):
    half = lax.dynamic_slice_in_dim(v, core * WIDE, WIDE, 1)
    q = []
    for i in range(2):
        part = half[:, i * FEAT : (i + 1) * FEAT]
        q.append(jnp.concatenate([part[:HALF], part[PAD : PAD + HALF]], 1).reshape(1, -1))
    return jnp.where(parity == 0, q[0], q[1]), jnp.where(parity == 0, q[1], q[0])


def heads_of(v, j):
    return [v[:, j * FEAT + h * HEAD_DIM : j * FEAT + (h + 1) * HEAD_DIM] for h in range(3)]


def attend(q, k, v, keep):
    logits = jnp.where(keep, dot(q, k, 1, 1) * 0.125, -1e30)
    top = jnp.max(logits, -1, keepdims=True)
    expo = jnp.exp(logits - top)
    total = jnp.sum(expo, -1, keepdims=True)
    mixed = dot((expo / total).astype(bf16), v)
    return mixed.astype(bf16), top + jnp.log(total)


def attend_back(q, k, v, keep, lse, grad):
    logits = jnp.where(keep, dot(q, k, 1, 1) * 0.125, -1e30)
    chance = jnp.exp(logits - lse)
    gchance = dot(grad, v, 1, 1)
    gv = dot(chance.astype(bf16), grad, 0, 0)
    inner = jnp.sum(chance * gchance, -1, keepdims=True)
    gl = (chance * (gchance - inner)).astype(bf16)
    gq = dot(gl, k) * 0.125
    gk = dot(gl, q, 0, 0) * 0.125
    return gq.astype(bf16), gk.astype(bf16), gv.astype(bf16)


def body(patches, visible, project_in, project_out, expand, contract, expand_bias, vectors, cotangent):
    n_dp = lax.axis_size("dp")
    more = n_dp // 2
    dp, hid, z = lax.axis_index("dp"), lax.axis_index("hid"), lax.axis_index("mod")
    core, parity = dp % 2, z % 2
    place = 4 * core + hid
    if more > 1:
        def mine_of(v, dim):
            whole = lax.all_gather(v, ("dp", "hid"), axis=dim, tiled=True)
            size = whole.shape[dim] // 8
            return lax.dynamic_slice_in_dim(whole, place * size, size, dim)

        project_in, project_out = mine_of(project_in, 1), mine_of(project_out, 1)
        expand, contract = mine_of(expand, 1), mine_of(contract, 0)
        expand_bias = mine_of(expand_bias, 0)

    a0, f0 = pack(project_in, project_out, expand, contract, expand_bias, vectors)
    a = [a0] + [over_z(a0, k) for k in (1, 2, 3)]
    size = HALF * WIDE
    jump = (HALF - 1) * WIDE

    def blocks(v):
        return (lax.dynamic_slice(v, (0, parity * jump), (1, size)),
                lax.dynamic_slice(v, (0, (1 - parity) * jump), (1, size)))

    pb, cb = blocks(patches), blocks(cotangent)
    first = rows_there(jnp.concatenate([pb[0], cb[0]], 0), False)
    second = rows_there(jnp.concatenate([pb[1], cb[1]], 0), True)
    both = jnp.concatenate([first, second], 0)
    other = over_core(both)
    counts = jnp.stack([visible, over_core(visible)])
    counts = jnp.where(core == 0, counts, counts[::-1]).reshape(4)
    count = counts[z]
    f = [f0] + [over_z(f0, k) for k in (1, 3, 2)]
    f = [f[0], f[1], f[3], f[2]]

    slot = jnp.arange(PAD)
    ids = jnp.concatenate([2 * slot - parity, 2 * slot + 1 - parity])
    real = (slot < HALF)
    real = jnp.concatenate([real, real]) & (ids >= 0) & (ids < L)
    keep = (real & (ids < count))
    keep_row, keep_col = keep[:, None], keep[None, :]

    x = unflat(both[0:1], both[2:3], other[0:1], other[2:3], core, parity)
    x = jnp.where(real[:, None], x, 0).astype(f32)
    grad_out = unflat(both[1:2], both[3:4], other[1:2], other[3:4], core, parity)
    grad_mlp = jnp.where(keep_row, grad_out, 0).astype(bf16)
    grad_out = grad_mlp.astype(f32)

    low = jnp.stack([a[0][:192], a[1][:192]])
    high = jnp.stack([a[2][:192], a[3][:192]])
    keeps, gives = jnp.where(core == 0, low, high), jnp.where(core == 0, high, low)
    got = over_core(gives)
    here = jnp.concatenate([keeps, got], 0)
    from_x, from_y = over_x(here), over_y(here)
    diag_a, diag_b = over_x(from_y[:2]), over_y(from_x[2:])
    fx, fy = over_x(f0), over_y(f0)
    f3 = jnp.stack(f[1:])
    fx3, fy3 = over_x(f3), over_y(f3)
    fd_a, fd_b = over_x(jnp.stack([fy, fy3[0]])), over_y(fx3[1:])
    by_hid = [here, from_x, from_y, jnp.concatenate([diag_a, diag_b], 0)]
    stacked = jnp.stack(by_hid)
    order_hid = jnp.arange(4) ^ hid
    stacked = jnp.take(stacked, order_hid, axis=0).reshape(4, 2, 2, 2, UNITS, WIDE)
    stacked = jnp.take(stacked, jnp.stack([core, 1 - core]), axis=1)
    w = stacked.transpose(2, 3, 1, 0, 4, 5).reshape(2, 2, D, WIDE)

    vq = natural([v[192:200] for v in a], z).astype(f32)
    vec = (vq[:, :, :FEAT] + vq[:, :, FEAT:]).transpose(1, 0, 2).reshape(8, D)
    slots = [(z - 2 * core - j) % 4 for j in range(2)]
    vec_slot = [(vq[s] if False else jnp.take(vq, s, axis=0)) for s in slots]
    vec_slot = [v[:, :FEAT] + v[:, FEAT:] for v in vec_slot]

    normed1, inv1, shifted1 = norm(x, vec[0:1], vec[1:2])
    attn_in = shifted1.astype(bf16)
    qs, ks, vs = [], [], []
    for j in range(2):
        qk = dot(attn_in, w[j, 0])
        vv = dot(attn_in, w[j, 1][:, :FEAT])
        qs += heads_of((qk[:, :FEAT] + vec_slot[j][2:3]).astype(bf16), 0)
        ks += heads_of(qk[:, FEAT:].astype(bf16), 0)
        vs += heads_of((vv + vec_slot[j][3:4]).astype(bf16), 0)
    outs = [attend(q, k, v, keep_col) for q, k, v in zip(qs, ks, vs)]
    mixed = [jnp.concatenate([o[0] for o in outs[3 * j : 3 * j + 3]], 1) for j in range(2)]
    part = sum(dot(mixed[j], w[j, 1][:, FEAT:], 1, 1) for j in range(2))
    resid = x + part + over_core(part.astype(bf16)).astype(f32) + vec[4:5]

    normed2, inv2, shifted2 = norm(resid, vec[5:6], vec[6:7])
    mlp_in = shifted2.astype(bf16)

    f_own = jnp.stack(f)
    f_x, f_y = jnp.concatenate([fx[None], fx3]), jnp.concatenate([fy[None], fy3])
    f_d = jnp.concatenate([fd_a, fd_b])
    mlp_out, gnm = 0.0, 0.0
    grads = []
    for piece in (f_own, f_x, f_y, f_d):
        nat = jnp.take(piece, (z - jnp.arange(4)) % 4, axis=0)
        ein, cout = nat[:, :FEAT].reshape(D, WIDE), nat[:, FEAT : 2 * FEAT].reshape(D, WIDE)
        bias = piece[0, 2 * FEAT : 2 * FEAT + 1].astype(f32)
        pre = dot(mlp_in, ein) + bias
        hidden = jax.nn.gelu(pre, approximate=False).astype(bf16)
        mlp_out += dot(hidden, cout, 1, 1)
        ghid = dot(grad_mlp, cout)
        gpre = jax.vjp(partial(jax.nn.gelu, approximate=False), pre)[1](ghid)[0].astype(bf16)
        gnm += dot(gpre, ein, 1, 1)
        g_in = dot(mlp_in, gpre, 0, 0)
        g_out = dot(grad_mlp, hidden, 0, 0)
        gb = jnp.pad(jnp.sum(gpre.astype(f32), 0, keepdims=True), ((0, 15), (0, 0)))
        grads.append((g_in.astype(bf16), g_out.astype(bf16), gb.astype(bf16)))

    mlp_sum = mlp_out + over_core(mlp_out.astype(bf16)).astype(f32)
    result = (keep_row * (resid + mlp_sum + vec[7:8])).astype(bf16)

    def add(u, v):
        return (u.astype(f32) + v.astype(f32)).astype(bf16)

    own, gx, gy, gd = [(jnp.concatenate([g[0], g[2]], 0), g[1]) for g in grads]
    rx, ry = over_x(gd[0]), over_y(gd[1])
    sx, sy = over_x(jnp.concatenate([gx[0], add(gx[1], ry)], 0)), over_y(jnp.concatenate([add(gy[0], rx), gy[1]], 0))
    total = jnp.concatenate(own, 0).astype(f32) + sx.astype(f32) + sy.astype(f32)

    def ffn_part(k):
        q = (z + k) % 4
        return jnp.concatenate([lax.dynamic_slice_in_dim(total, q * FEAT, FEAT, 0),
                                lax.dynamic_slice_in_dim(total, D + 16 + q * FEAT, FEAT, 0), total[D : D + 16]], 0)

    fsum = ffn_part(0)
    for k in (1, 2, 3):
        fsum += over_z(ffn_part(k).astype(bf16), k).astype(f32)
    expand_grad, contract_grad, bias_grad = fsum[:FEAT], fsum[FEAT : 2 * FEAT].T, fsum[2 * FEAT]

    gnm = gnm + over_core(gnm.astype(bf16)).astype(f32)
    grad_resid = grad_out + norm_back(gnm, normed2, inv2, vec[5:6])
    grad_branch = grad_resid.astype(bf16)
    gw, part, colsums = [], 0.0, []
    for j in range(2):
        gm = dot(grad_branch, w[j, 1][:, FEAT:]).astype(bf16)
        res = [attend_back(qs[3 * j + h], ks[3 * j + h], vs[3 * j + h], keep_col, outs[3 * j + h][1],
                           gm[:, h * HEAD_DIM : (h + 1) * HEAD_DIM]) for h in range(3)]
        gq, gk, gv = (jnp.concatenate([r[i] for r in res], 1) for i in range(3))
        gqk = jnp.concatenate([gq, gk], 1)
        part += dot(gqk, w[j, 0], 1, 1) + dot(gv, w[j, 1][:, :FEAT], 1, 1)
        gw.append((dot(attn_in, gqk, 0, 0),
                   jnp.concatenate([dot(attn_in, gv, 0, 0), dot(grad_branch, mixed[j], 0, 0)], 1)))
        colsums.append((jnp.sum(gq.astype(f32), 0), jnp.sum(gv.astype(f32), 0)))
    gna = part + over_core(part.astype(bf16)).astype(f32)
    grad_in = grad_resid + norm_back(gna, normed1, inv1, vec[0:1])

    zero = jnp.zeros((D,), f32)
    vg = jnp.stack([jnp.sum(gna * normed1, 0), jnp.sum(gna, 0), zero, zero, jnp.sum(grad_branch.astype(f32), 0),
                    jnp.sum(gnm * normed2, 0), jnp.sum(gnm, 0), jnp.sum(grad_out, 0)])
    vg = vg.reshape(8, 4, FEAT).transpose(1, 0, 2)
    pieces = []
    for j in range(2):
        v = jnp.take(vg, slots[j], axis=0)
        v = v.at[2].set(colsums[j][0]).at[3].set(colsums[j][1])
        v = jnp.pad(v, ((0, 8), (0, FEAT))).astype(bf16)
        pieces.append(v)
    blocks_of = []
    for i in range(4):
        four = []
        for p in range(2):
            for j in range(2):
                at = (4 * (core ^ p) + (hid ^ i)) * UNITS
                four.append(jnp.concatenate([lax.dynamic_slice_in_dim(g, at, UNITS, 0).astype(bf16) for g in gw[j]]
                                            + [pieces[j]], 0))
        blocks_of.append(jnp.stack(four))
    own, gx, gy, gd = blocks_of
    rx, ry = over_x(gd[:2]), over_y(gd[2:])
    sx = over_x(jnp.concatenate([gx[:2], add(gx[2:], ry)], 0))
    sy = over_y(jnp.concatenate([add(gy[:2], rx), gy[2:]], 0))
    total = own.astype(f32) + sx.astype(f32) + sy.astype(f32)
    got = over_core(total[2:].astype(bf16)).astype(f32)
    keeps = total[:2]
    slot_all = jnp.where(core == 0, jnp.concatenate([keeps, got], 0), jnp.concatenate([got, keeps], 0))
    asum = slot_all[0]
    for k in (1, 2, 3):
        asum += over_z(slot_all[k].astype(bf16), -k).astype(f32)
    in_grad = jnp.stack([asum[:UNITS, :FEAT], asum[:UNITS, FEAT:], asum[UNITS : 2 * UNITS, :FEAT]])
    out_grad = asum[UNITS : 2 * UNITS, FEAT:].T
    vector_grad = asum[2 * UNITS : 2 * UNITS + 8, :FEAT]

    def home(v):
        u1, u2 = reflat(v, core, parity)
        b1, b2 = rows_back(u1, False), rows_back(u2, True)
        s0, s1 = jnp.where(parity == 0, b1, b2), jnp.where(parity == 0, b2, b1)
        edge = HALF * WIDE - FEAT
        return jnp.concatenate([s0[:, :edge], s1[:, FEAT:]], 1)

    result = home(result)
    grad_input = home(grad_in.astype(bf16)).astype(f32)

    if more > 1:
        def spread(v, dim):
            whole = jnp.zeros(v.shape[:dim] + (8 * v.shape[dim],) + v.shape[dim + 1 :], f32)
            whole = lax.dynamic_update_slice_in_dim(whole, v, place * v.shape[dim], dim)
            return lax.psum_scatter(whole, ("dp", "hid"), scatter_dimension=dim, tiled=True)

        in_grad, out_grad = spread(in_grad, 1), spread(out_grad, 1)
        expand_grad, contract_grad, bias_grad = spread(expand_grad, 1), spread(contract_grad, 0), spread(bias_grad, 0)
        vector_grad = lax.psum(vector_grad, "dp") / 2
    return result, grad_input, in_grad, out_grad, expand_grad, contract_grad, bias_grad, vector_grad


def solution(mesh):
    rows = P("mod", ("dp", "hid"))
    in_specs = (rows, P(("dp", "hid")), P(None, ("dp", "hid"), "mod"), rows, rows, P(("dp", "hid"), "mod"),
                P(("dp", "hid")), P(None, "mod"), rows)
    out_specs = (rows, rows, P(None, ("dp", "hid"), "mod"), rows, rows, P(("dp", "hid"), "mod"),
                 P(("dp", "hid")), P(None, "mod"))
    return jax.shard_map(body, mesh=mesh, in_specs=in_specs, out_specs=out_specs, check_vma=False)
```

```python
import jax
import jax.numpy as jnp
from jax import lax
from jax.experimental import pallas as pl
from jax.experimental.pallas import tpu as pltpu
from jax.sharding import PartitionSpec as P

D = 768
HEAD_DIM = 64
L = 529
FEAT = 192
HALF = 265
PAD = 272
ROWS = 2 * PAD
WIDE = 2 * FEAT
UNITS = D // 8
APIECE = 2 * UNITS + 16
FPIECE = 2 * FEAT + 16
eps = 1e-06
bf16 = jnp.bfloat16
f32 = jnp.float32

X = [(0, 1), (1, 0), (2, 3), (3, 2)]
Y = [(0, 2), (2, 0), (1, 3), (3, 1)]


def dot(a, b, ca=1, cb=0):
    return lax.dot_general(a, b, (((ca,), (cb,)), ((), ())), preferred_element_type=f32)


def over_x(v):
    return lax.ppermute(v, "hid", X)


def over_y(v):
    return lax.ppermute(v, "hid", Y)


def over_core(v):
    n = lax.axis_size("dp")
    return lax.ppermute(v, "dp", [(i, i ^ 1) for i in range(n)])


def over_z(v, shift):
    n = lax.axis_size("mod")
    return lax.ppermute(v, "mod", [(i, (i + shift) % n) for i in range(n)])


def row_pairs(second, back):
    pairs = []
    for dp in range(lax.axis_size("dp")):
        for z in range(4):
            core = dp % 2
            parity = 1 - z % 2 if second else z % 2
            src, dst = dp * 4 + z, (dp - core + z // 2) * 4 + 2 * core + parity
            pairs.append((dst, src) if back else (src, dst))
    return pairs


def rows_there(v, second):
    return lax.ppermute(v, ("dp", "mod"), row_pairs(second, False))


def rows_back(v, second):
    return lax.ppermute(v, ("dp", "mod"), row_pairs(second, True))


VM = pl.BlockSpec(memory_space=pltpu.VMEM)
SM = pl.BlockSpec(memory_space=pltpu.SMEM)


def call(kernel, outs, scal, *args, flops=0, limit=48, scratch=(), name=None):
    outs = [jax.ShapeDtypeStruct(s, t) for s, t in outs]
    size = sum(a.size * a.dtype.itemsize for a in args) + sum(o.size * o.dtype.itemsize for o in outs)
    single = len(outs) == 1
    ins = ([] if scal is None else [SM]) + [VM] * len(args)
    if scal is not None:
        args = (scal,) + args
    return pl.pallas_call(
        kernel,
        out_shape=outs[0] if single else outs,
        in_specs=ins,
        out_specs=VM if single else [VM] * len(outs),
        scratch_shapes=list(scratch),
        cost_estimate=pl.CostEstimate(flops=int(flops), bytes_accessed=int(size), transcendentals=0),
        compiler_params=pltpu.CompilerParams(vmem_limit_bytes=limit * 2**20),
        name=name,
    )(*args)


def k_pack(pin, pout, ex, con, bias, vec, attn, ffn):
    u = UNITS
    attn[0:u, 0:FEAT] = pin[0]
    attn[0:u, FEAT:WIDE] = pin[1]
    attn[u : 2 * u, 0:FEAT] = pin[2]
    attn[u : 2 * u, FEAT:WIDE] = pout[...].astype(f32).T.astype(bf16)
    v = vec[...]
    hi = v.astype(bf16)
    lo = (v - hi.astype(f32)).astype(bf16)
    both = jnp.concatenate([hi.astype(f32), lo.astype(f32)], 1)
    attn[2 * u : APIECE, :] = jnp.concatenate([both, jnp.zeros_like(both)], 0).astype(bf16)
    ffn[0:FEAT, :] = ex[...]
    ffn[FEAT:WIDE, :] = con[...].astype(f32).T.astype(bf16)
    ffn[WIDE:FPIECE, :] = jnp.broadcast_to(bias[...].astype(f32), (16, WIDE)).astype(bf16)


def k_in(scal, p, c, p1, p2, c1, c2):
    even = scal[2] % 2 == 0

    @pl.when(even)
    def _():
        p1[...] = p[0:HALF, 0, :]
        p2[...] = p[HALF - 1 : L, 0, :]
        c1[...] = c[0:HALF, 0, :]
        c2[...] = c[HALF - 1 : L, 0, :]

    @pl.when(jnp.logical_not(even))
    def _():
        p2[...] = p[0:HALF, 0, :]
        p1[...] = p[HALF - 1 : L, 0, :]
        c2[...] = c[0:HALF, 0, :]
        c1[...] = c[HALF - 1 : L, 0, :]


def row_ids(parity, shape, dim):
    place = lax.broadcasted_iota(jnp.int32, shape, dim)
    right = place >= PAD
    slot = jnp.where(right, place - PAD, place)
    ids = 2 * slot - parity + jnp.where(right, 1, 0)
    real = (slot < HALF) & (ids >= 0) & (ids < L)
    return real, ids


def kept_rows(scal, shape=(ROWS, 1), dim=0):
    real, ids = row_ids(scal[2] % 2, shape, dim)
    return real & (ids < scal[3])


def assemble(scal, own1, own2, oth1, oth2, out):
    core, even = scal[0], scal[2] % 2 == 0
    a, b, c, d = (r[...].astype(f32) for r in (own1, own2, oth1, oth2))
    own = jnp.where(even, a, b), jnp.where(even, b, a)
    oth = jnp.where(even, c, d), jnp.where(even, d, c)
    first = core == 0
    for q in range(4):
        mine, theirs = (own, oth) if q < 2 else (oth, own)
        v = jnp.where(first, mine[q % 2], theirs[q % 2])
        out[0:HALF, q * FEAT : (q + 1) * FEAT] = v[:, :FEAT]
        out[PAD : PAD + HALF, q * FEAT : (q + 1) * FEAT] = v[:, FEAT:]


def norm(v, gain, shift):
    moved = v - jnp.mean(v, 1, keepdims=True)
    inverse = lax.rsqrt(jnp.mean(moved * moved, 1, keepdims=True) + eps)
    normed = moved * inverse
    return normed, inverse, normed * gain + shift


def norm_back(grad, normed, inverse, gain):
    t = grad * gain
    return inverse * (t - jnp.mean(t, 1, keepdims=True) - normed * jnp.mean(t * normed, 1, keepdims=True))


def vec_block(refs, k):
    v = refs[0][2 * UNITS : APIECE, :].astype(f32)
    for i in (1, 2, 3):
        v = jnp.where(k == i, refs[i][2 * UNITS : APIECE, :].astype(f32), v)
    return v[0:8, :FEAT] + v[0:8, FEAT:]


def k_norm1(scal, own1, own2, oth1, oth2, a0, a1, a2, a3, x, ain, ain_t, vec, slots, buf):
    core, z = scal[0], scal[2]
    refs = (a0, a1, a2, a3)
    for q in range(4):
        vec[:, q * FEAT : (q + 1) * FEAT] = vec_block(refs, (z - q + 4) % 4)
    for j in range(2):
        slots[j] = vec_block(refs, 2 * core + j)
    assemble(scal, own1, own2, oth1, oth2, buf)
    real, _ = row_ids(z % 2, (ROWS, 1), 0)
    v = jnp.where(real, buf[...], 0.0)
    x[...] = v.astype(bf16)
    low = norm(v, vec[0:1, :], vec[1:2, :])[2].astype(bf16)
    ain[...] = low
    ain_t[...] = low.T


def k_give(scal, a0, a1, a2, a3, keeps, gives):
    first = scal[0] == 0
    for j, (lo, hi) in enumerate(((a0, a2), (a1, a3))):
        u, v = lo[0 : 2 * UNITS, :], hi[0 : 2 * UNITS, :]
        keeps[j] = jnp.where(first, u, v)
        gives[j] = jnp.where(first, v, u)


def k_attn(scal, ain, h_own, h_got, fx, fy, da, db, slots, w, q, k, v, lse, mixed, part, part_low, qt, vt, mt):
    core, hid = scal[0], scal[1]
    for i in range(4):
        for p in range(2):
            for j in range(2):
                src = ((h_own, h_got)[p], None, None, None)[i]
                if i == 0:
                    src = (h_own, h_got)[p][j]
                elif i == 3:
                    src = (da, db)[p][j]
                else:
                    src = (fx, fy)[i - 1][2 * p + j]
                at = pl.multiple_of((4 * (core ^ p) + (hid ^ i)) * UNITS, 32)
                w[j, 0, pl.ds(at, UNITS), :] = src[0:UNITS]
                w[j, 1, pl.ds(at, UNITS), :] = src[UNITS : 2 * UNITS]
    keep = kept_rows(scal)
    lane = lax.broadcasted_iota(jnp.int32, (1, FEAT), 1) // HEAD_DIM
    for j in range(2):
        qk = dot(ain[...], w[j, 0])
        qj = (qk[:, :FEAT] + slots[j, 2:3, :]).astype(bf16) * jnp.asarray(0.125, bf16)
        q[j] = qj
        qt[j] = qj.T
        k[j] = qk[:, FEAT:].astype(bf16)
        vj = (dot(ain[...], w[j, 1, :, 0:FEAT]) + slots[j, 3:4, :]).astype(bf16)
        v[j] = vj
        vt[j] = vj.T
    lse[...] = jnp.zeros_like(lse)
    for j in range(2):
        for h in range(3):
            kh = jnp.where(lane == h, k[j], jnp.zeros((), bf16))
            logits = jnp.where(keep, dot(kh, qt[j]), -1e30)
            top = jnp.max(logits, 0, keepdims=True)
            expo = jnp.exp(logits - top)
            total = jnp.sum(expo, 0, keepdims=True)
            chance = (expo * (1.0 / total)).astype(bf16)
            rows = slice(h * HEAD_DIM, (h + 1) * HEAD_DIM)
            mt[j, rows, :] = dot(vt[j, rows, :], chance)
            lse[3 * j + h : 3 * j + h + 1, :] = top + jnp.log(total)
    total = 0.0
    for j in range(2):
        mj = mt[j].T.astype(bf16)
        mixed[j] = mj
        total += dot(mj, w[j, 1, :, FEAT:WIDE], 1, 1)
    part[...] = total
    part_low[...] = total.astype(bf16)


def k_norm2(scal, x, part, oth, vec, c1, c2, d1, d2, resid, low, low_t, grad, grad_t, buf):
    r = x[...].astype(f32) + part[...] + oth[...].astype(f32) + vec[4:5, :]
    resid[...] = r
    v = norm(r, vec[5:6, :], vec[6:7, :])[2].astype(bf16)
    low[...] = v
    low_t[...] = v.T
    assemble(scal, c1, c2, d1, d2, buf)
    g = jnp.where(kept_rows(scal), buf[...], 0.0).astype(bf16)
    grad[...] = g
    grad_t[...] = g.T


def gelu_both(v):
    half = 0.5 * (1.0 + lax.erf(v * 0.7071067811865476))
    slope = half + v * jnp.exp(-0.5 * v * v) * 0.3989422804014327
    return v * half, slope


def ffn_kernel(parts, first, last, split, adds):
    n = len({r for r, _ in parts})

    def kernel(scal, *refs):
        refs = list(refs)
        low, low_t, grad, grad_t = refs[:4]
        pieces, refs = refs[4 : 4 + n], refs[4 + n :]
        add_in = add_out = None
        if adds == "in":
            add_in = refs.pop(0)
        if adds == "out":
            add_out = refs.pop(0)
        if not first:
            old_out, old_back = refs.pop(0), refs.pop(0)
        if last:
            keep, give, back, back_low = refs[:4]
            refs = refs[4:]
        else:
            out, back = refs[:2]
            refs = refs[2:]
        if split:
            g_in, g_out = refs[0], refs[1]
            at = 0
            refs = refs[2:]
        else:
            g_in = g_out = refs[0]
            at = D + 16
            refs = refs[1:]
        ein, cout = refs
        z = scal[2]
        for s, (r, i) in enumerate(parts):
            src = pieces[r] if i is None else pieces[r].at[i]
            place = pl.ds(pl.multiple_of(((z - s + 4) % 4) * FEAT, FEAT), FEAT)
            ein[place, :] = src[0:FEAT, :]
            cout[place, :] = src[FEAT:WIDE, :]
            if s == 0:
                bias = src[WIDE:FPIECE, :].astype(f32)[0:1]
        act, slope = gelu_both(dot(low[...], ein[...]) + bias)
        hidden = act.astype(bf16)
        g = (dot(grad[...], cout[...]) * slope).astype(bf16)
        res = dot(hidden, cout[...], 1, 1)
        if not first:
            res = res + old_out[...]
        if last:
            core = scal[0] == 0
            a, b = res[:, :WIDE], res[:, WIDE:]
            keep[...] = jnp.where(core, a, b)
            give[...] = jnp.where(core, b, a).astype(bf16)
        else:
            out[...] = res
        res = dot(g, ein[...], 1, 1)
        if not first:
            res = res + old_back[...]
        back[...] = res
        if last:
            back_low[...] = res.astype(bf16)
        w = dot(low_t[...], g)
        sums = jnp.sum(g.astype(f32), 0, keepdims=True)
        sums = jnp.broadcast_to(sums, (16, WIDE))
        if add_in is not None:
            w = w + add_in[0:D, :].astype(f32)
            sums = sums + add_in[D : D + 16, :].astype(f32)
        g_in[0:D, :] = w.astype(bf16)
        g_in[D : D + 16, :] = sums.astype(bf16)
        w = dot(grad_t[...], hidden)
        if add_out is not None:
            w = w + add_out[...].astype(f32)
        g_out[at : at + D, :] = w.astype(bf16)

    return kernel


def ffn(scal, rows, pieces, parts, acc, split=False, last=False, add_in=None, add_out=None):
    first = acc is None
    adds = "in" if add_in is not None else "out" if add_out is not None else None
    extra = [a for a in (add_in, add_out) if a is not None]
    if last:
        outs = [((ROWS, WIDE), f32), ((ROWS, WIDE), bf16), ((ROWS, D), f32), ((ROWS, D), bf16)]
    else:
        outs = [((ROWS, D), f32), ((ROWS, D), f32)]
    if split:
        outs += [((D + 16, WIDE), bf16), ((D, WIDE), bf16)]
    else:
        outs += [((2 * D + 16, WIDE), bf16)]
    return call(ffn_kernel(parts, first, last, split, adds), outs, scal, *rows, *pieces, *extra, *(acc or ()),
                flops=12 * ROWS * D * WIDE, scratch=[pltpu.VMEM((D, WIDE), bf16)] * 2, name="ffn")


def place_rows(scal, v, out1, out2):
    even = scal[2] % 2 == 0
    q = []
    for i in range(2):
        part = v[:, i * FEAT : (i + 1) * FEAT]
        q.append(jnp.concatenate([part[0:HALF], part[PAD : PAD + HALF]], 1))
    out1[...] = jnp.where(even, q[0], q[1]).astype(bf16)
    out2[...] = jnp.where(even, q[1], q[0]).astype(bf16)


def k_out(scal, resid, keep, got, vec, out1, out2):
    first = scal[0] == 0
    r = jnp.where(first, resid[:, 0:WIDE], resid[:, WIDE:D])
    b = jnp.where(first, vec[7:8, 0:WIDE], vec[7:8, WIDE:D])
    v = r + keep[...] + got[...].astype(f32) + b
    place_rows(scal, jnp.where(kept_rows(scal), v, 0.0), out1, out2)


def k_back(scal, resid, back, back_oth, gml, vec, w, q, k, v, lse, mixed,
           gres, branch, gqk, gv, part, part_low, vrows, bufs, gmt, kt, qt, dqt, dk, dv):
    gnm = back[...] + back_oth[...].astype(f32)
    normed, inverse, _ = norm(resid[...], vec[5:6, :], vec[6:7, :])
    g = gml[...].astype(f32)
    res = g + norm_back(gnm, normed, inverse, vec[5:6, :])
    gres[...] = res
    low = res.astype(bf16)
    branch[...] = low
    vrows[...] = jnp.zeros_like(vrows)
    vrows[4:5, :] = jnp.sum(low.astype(f32), 0, keepdims=True)
    vrows[5:6, :] = jnp.sum(gnm * normed, 0, keepdims=True)
    vrows[6:7, :] = jnp.sum(gnm, 0, keepdims=True)
    vrows[7:8, :] = jnp.sum(g, 0, keepdims=True)
    keep = kept_rows(scal)
    lane = lax.broadcasted_iota(jnp.int32, (1, FEAT), 1) // HEAD_DIM
    none = jnp.zeros((), bf16)
    total = 0.0
    for j in range(2):
        gm = dot(low, w[j, 1, :, FEAT:WIDE])
        gm_low = gm.astype(bf16)
        gmt[...] = gm_low.T
        kt[...] = k[j].T
        qt[...] = q[j].T
        prod = gm_low.astype(f32) * mixed[j].astype(f32)
        prod_t = prod.T
        dk[...] = jnp.zeros_like(dk)
        dv[...] = jnp.zeros_like(dv)
        for h in range(3):
            rows = slice(h * HEAD_DIM, (h + 1) * HEAD_DIM)
            delta = jnp.sum(prod_t[rows, :], 0, keepdims=True)
            logits = jnp.where(keep, dot(jnp.where(lane == h, k[j], none), qt[...]), -1e30)
            chance = jnp.exp(logits - lse[3 * j + h : 3 * j + h + 1, :])
            gchance = dot(jnp.where(lane == h, v[j], none), gmt[...])
            gl = (chance * (gchance - delta)).astype(bf16)
            dv[...] += dot(chance.astype(bf16), jnp.where(lane == h, gm_low, none))
            dk[...] += dot(gl, jnp.where(lane == h, q[j], none))
            dqt[rows, :] = dot(kt[rows, :], gl) * 0.125
        gq = dqt[...].T
        both = jnp.concatenate([gq, dk[...]], 1).astype(bf16)
        gqk[j] = both
        val = dv[...].astype(bf16)
        gv[j] = val
        total += dot(both, w[j, 0], 1, 1) + dot(val, w[j, 1, :, 0:FEAT], 1, 1)
    part[...] = total
    part_low[...] = total.astype(bf16)


def k_front(scal, part, oth, x, vec, gres, branch, gqk, gv, mixed, ain_t, vrows,
            own, gx, gy, gd1, gd2, in1, in2, vfull, wbuf):
    core, hid, z = scal[0], scal[1], scal[2]
    gna = part[...] + oth[...].astype(f32)
    normed, inverse, _ = norm(x[...].astype(f32), vec[0:1, :], vec[1:2, :])
    res = gres[...] + norm_back(gna, normed, inverse, vec[0:1, :])
    place_rows(scal, jnp.where(core == 0, res[:, 0:WIDE], res[:, WIDE:D]), in1, in2)
    vfull[...] = vrows[...]
    vfull[0:1, :] = jnp.sum(gna * normed, 0, keepdims=True)
    vfull[1:2, :] = jnp.sum(gna, 0, keepdims=True)
    branch_t = branch[...].T
    dest = lambda i, p, j: ((own, gx, gy)[i].at[2 * p + j] if i < 3 else (gd1, gd2)[p].at[j])
    for j in range(2):
        wbuf[0] = dot(ain_t[...], gqk[j]).astype(bf16)
        wbuf[1, :, 0:FEAT] = dot(ain_t[...], gv[j]).astype(bf16)
        wbuf[1, :, FEAT:WIDE] = dot(branch_t, mixed[j]).astype(bf16)
        src = (z - 2 * core - j + 8) % 4
        mine = vfull[:, 0:FEAT]
        for i in (1, 2, 3):
            mine = jnp.where(src == i, vfull[:, i * FEAT : (i + 1) * FEAT], mine)
        line = lax.broadcasted_iota(jnp.int32, (8, 1), 0)
        cols_q = jnp.sum(gqk[j].astype(f32), 0, keepdims=True)[:, 0:FEAT]
        cols_v = jnp.sum(gv[j].astype(f32), 0, keepdims=True)
        mine = jnp.where(line == 2, cols_q, jnp.where(line == 3, cols_v, mine))
        mine = jnp.concatenate([mine, jnp.zeros_like(mine)], 1)
        mine = jnp.concatenate([mine, jnp.zeros_like(mine)], 0).astype(bf16)
        for i in range(4):
            for p in range(2):
                at = pl.multiple_of((4 * (core ^ p) + (hid ^ i)) * UNITS, 32)
                to = dest(i, p, j)
                to[0:UNITS, :] = wbuf[0, pl.ds(at, UNITS), :]
                to[UNITS : 2 * UNITS, :] = wbuf[1, pl.ds(at, UNITS), :]
                to[2 * UNITS : APIECE, :] = mine


def plus(a, b):
    return a.astype(f32) + b.astype(f32)


def k_fsum(scal, g, sx, sy, keep, s1, s2, s3):
    z = scal[2]
    for k, to in enumerate((keep, s1, s2, s3)):
        for base, at, n in ((((z + k) % 4) * FEAT, 0, FEAT), (D + 16 + ((z + k) % 4) * FEAT, FEAT, FEAT), (D, WIDE, 16)):
            rows = pl.ds(pl.multiple_of(base, 16), n)
            v = plus(g[rows, :], sx[rows, :]) + sy[rows, :].astype(f32)
            to[at : at + n, :] = v.astype(to.dtype)


def k_ffin(keep, r1, r2, r3, ex, con, bias):
    v = keep[...] + r1[...].astype(f32) + r2[...].astype(f32) + r3[...].astype(f32)
    ex[...] = v[0:FEAT]
    con[...] = v[FEAT:WIDE].T
    bias[...] = v[WIDE : WIDE + 1]


def k_aadd(gx, ry, gy, rx, px, py):
    px[0:2] = gx[0:2]
    px[2:4] = plus(gx[2:4], ry[...]).astype(bf16)
    py[0:2] = plus(gy[0:2], rx[...]).astype(bf16)
    py[2:4] = gy[2:4]


def k_asum(own, sx, sy, keep, give):
    keep[...] = plus(own[0:2], sx[0:2]) + sy[0:2].astype(f32)
    give[...] = (plus(own[2:4], sx[2:4]) + sy[2:4].astype(f32)).astype(bf16)


def k_asel(scal, keep, got, s0, s1, s2, s3):
    first = scal[0] == 0
    a, b = keep[...], got[...].astype(f32)
    lo, hi = jnp.where(first, a, b), jnp.where(first, b, a)
    s0[...] = lo[0]
    s1[...] = lo[1].astype(bf16)
    s2[...] = hi[0].astype(bf16)
    s3[...] = hi[1].astype(bf16)


def k_afin(s0, r1, r2, r3, pin, pout, vec):
    v = s0[...] + r1[...].astype(f32) + r2[...].astype(f32) + r3[...].astype(f32)
    pin[0] = v[0:UNITS, 0:FEAT]
    pin[1] = v[0:UNITS, FEAT:WIDE]
    pin[2] = v[UNITS : 2 * UNITS, 0:FEAT]
    pout[...] = v[UNITS : 2 * UNITS, FEAT:WIDE].T
    vec[...] = v[2 * UNITS : 2 * UNITS + 8, 0:FEAT]


def k_home(scal, b1, b2, out):
    even = scal[2] % 2 == 0
    a, b = b1[...], b2[...]
    s0, s1 = jnp.where(even, a, b), jnp.where(even, b, a)
    t = out.dtype
    out[0 : HALF - 1, 0, :] = s0[0 : HALF - 1].astype(t)
    left = lax.broadcasted_iota(jnp.int32, (1, WIDE), 1) < FEAT
    out[HALF - 1 : HALF, 0, :] = jnp.where(left, s0[HALF - 1 : HALF].astype(f32), s1[0:1].astype(f32)).astype(t)
    out[HALF:L, 0, :] = s1[1:HALF].astype(t)


def body(patches, visible, project_in, project_out, expand, contract, expand_bias, vectors, cotangent):
    n_dp = lax.axis_size("dp")
    more = n_dp // 2
    dp, hid, z = lax.axis_index("dp"), lax.axis_index("hid"), lax.axis_index("mod")
    core = dp % 2
    place = 4 * core + hid
    if more > 1:
        def mine_of(v, dim):
            whole = lax.all_gather(v, ("dp", "hid"), axis=dim, tiled=True)
            size = whole.shape[dim] // 8
            return lax.dynamic_slice_in_dim(whole, place * size, size, dim)

        project_in, project_out = mine_of(project_in, 1), mine_of(project_out, 1)
        expand, contract = mine_of(expand, 1), mine_of(contract, 0)
        expand_bias = mine_of(expand_bias, 0)

    counts = jnp.stack([visible, over_core(visible)])
    counts = jnp.where(core == 0, counts, counts[::-1]).reshape(4)
    scal = jnp.stack([core, hid, z, counts[z]]).astype(jnp.int32)
    where = jnp.stack([core, hid, z, z]).astype(jnp.int32)

    a0, f0 = call(k_pack, [((APIECE, WIDE), bf16), ((FPIECE, WIDE), bf16)], None,
                  project_in, project_out, expand, contract, expand_bias.reshape(1, -1), vectors, name="pack")
    a = [a0] + [over_z(a0, k) for k in (1, 2, 3)]
    block = ((HALF, WIDE), bf16)
    p1, p2, c1, c2 = call(k_in, [block] * 4, where, patches.reshape(L, 1, WIDE), cotangent.reshape(L, 1, WIDE), name="rows_in")
    p1, p2 = rows_there(p1, False), rows_there(p2, True)
    keeps, gives = call(k_give, [((2, 2 * UNITS, WIDE), bf16)] * 2, where, *a, name="give")
    got = over_core(gives)
    here = jnp.concatenate([keeps, got], 0)
    from_x, from_y = over_x(here), over_y(here)
    f = [f0] + [over_z(f0, k) for k in (1, 2, 3)]
    fx, fy = over_x(f0), over_y(f0)
    q1, q2 = over_core(p1), over_core(p2)
    diag_a, diag_b = over_x(from_y[:2]), over_y(from_x[2:])
    c1, c2 = rows_there(c1, False), rows_there(c2, True)
    d1, d2 = over_core(c1), over_core(c2)
    f3 = jnp.stack(f[1:])
    fx3, fy3 = over_x(f3), over_y(f3)
    fd_a, fd_b = over_x(jnp.stack([fy, fy3[0]])), over_y(fx3[1:])

    wide, tall = ((ROWS, D), bf16), ((D, ROWS), bf16)
    rows32 = ((ROWS, D), f32)
    x, ain, ain_t, vec, slots = call(
        k_norm1, [wide, wide, tall, ((8, D), f32), ((2, 8, FEAT), f32)], scal, p1, p2, q1, q2, *a,
        scratch=[pltpu.VMEM((ROWS, D), f32)], name="norm_attn")
    head = ((2, ROWS, FEAT), bf16)
    flip = pltpu.VMEM((2, FEAT, ROWS), bf16)
    w, q, k, v, lse, mixed, part, part_low = call(
        k_attn, [((2, 2, D, WIDE), bf16), head, head, head, ((8, ROWS), f32), head, rows32, wide], scal,
        ain, keeps, got, from_x, from_y, diag_a, diag_b, slots,
        flops=2 * ROWS * D * WIDE * 4 + 24 * ROWS * ROWS * HEAD_DIM,
        scratch=[flip, flip, pltpu.VMEM((2, FEAT, ROWS), f32)], name="attend")
    other = over_core(part_low)
    resid, low, low_t, gml, gml_t = call(
        k_norm2, [rows32, wide, tall, wide, tall], scal, x, part, other, vec, c1, c2, d1, d2,
        scratch=[pltpu.VMEM((ROWS, D), f32)], name="norm_mlp")

    rows = (low, low_t, gml, gml_t)
    o_acc, b_acc, g_own = ffn(scal, rows, f, [(i, None) for i in range(4)], None)
    o_acc, b_acc, gd_in, gd_out = ffn(scal, rows, (fd_a, fd_b), [(0, 0), (0, 1), (1, 0), (1, 1)], (o_acc, b_acc), split=True)
    rx, ry = over_x(gd_in), over_y(gd_out)
    one_three = [(0, None), (1, 0), (1, 1), (1, 2)]
    o_acc, b_acc, g_x = ffn(scal, rows, (fx, fx3), one_three, (o_acc, b_acc), add_out=ry)
    sx = over_x(g_x)
    keep, give, back, back_low, g_y = ffn(scal, rows, (fy, fy3), one_three, (o_acc, b_acc), last=True, add_in=rx)
    back_oth = over_core(back_low)
    sy = over_y(g_y)
    got_out = over_core(give)
    r1, r2 = call(k_out, [block] * 2, scal, resid, keep, got_out, vec, name="result")

    pair = ((2, ROWS, WIDE), bf16)
    side = pltpu.VMEM((FEAT, ROWS), bf16)
    acc = pltpu.VMEM((ROWS, FEAT), f32)
    gres, branch, gqk, gv, part, part_low, vrows = call(
        k_back, [rows32, wide, pair, head, rows32, wide, ((8, D), f32)], scal,
        resid, back, back_oth, gml, vec, w, q, k, v, lse, mixed,
        flops=2 * ROWS * D * WIDE * 4 + 60 * ROWS * ROWS * HEAD_DIM,
        scratch=[pltpu.VMEM((8, ROWS), f32), side, side, side, pltpu.VMEM((FEAT, ROWS), f32), acc, acc], name="attend_back")
    oth = over_core(part_low)
    r1, r2 = rows_back(r1, False), rows_back(r2, True)
    four, two = ((4, APIECE, WIDE), bf16), ((2, APIECE, WIDE), bf16)
    ga_own, ga_x, ga_y, ga_d1, ga_d2, i1, i2 = call(
        k_front, [four, four, four, two, two, block, block], where, part, oth, x, vec, gres, branch, gqk, gv, mixed, ain_t, vrows,
        flops=2 * ROWS * D * WIDE * 4, scratch=[pltpu.VMEM((8, D), f32), pltpu.VMEM((2, D, WIDE), bf16)], name="norm_attn_back")
    ax, ay = over_x(ga_d1), over_y(ga_d2)
    fpart = (FPIECE, WIDE)
    fk, f1, f2, f3 = call(k_fsum, [(fpart, f32)] + [(fpart, bf16)] * 3, where, g_own, sx, sy, name="ffn_sum")
    px, py = call(k_aadd, [four, four], None, ga_x, ay, ga_y, ax, name="attn_add")
    tx, ty = over_x(px), over_y(py)
    f1, f2, f3 = over_z(f1, 1), over_z(f2, 2), over_z(f3, 3)
    i1, i2 = rows_back(i1, False), rows_back(i2, True)
    result = call(k_home, [((L, 1, WIDE), bf16)], where, r1, r2, name="rows_out").reshape(1, L * WIDE)
    expand_grad, contract_grad, bias_grad = call(
        k_ffin, [((FEAT, WIDE), f32), ((WIDE, FEAT), f32), ((1, WIDE), f32)], None, fk, f1, f2, f3, name="ffn_last")
    apart = (APIECE, WIDE)
    ak, give = call(k_asum, [((2,) + apart, f32), ((2,) + apart, bf16)], None, ga_own, tx, ty, name="attn_sum")
    got = over_core(give)
    s0, s1, s2, s3 = call(k_asel, [(apart, f32)] + [(apart, bf16)] * 3, where, ak, got, name="attn_slots")
    s1, s2, s3 = over_z(s1, 3), over_z(s2, 2), over_z(s3, 1)
    grad_input = call(k_home, [((L, 1, WIDE), f32)], where, i1, i2, name="rows_out_grad").reshape(1, L * WIDE)
    in_grad, out_grad, vector_grad = call(
        k_afin, [((3, UNITS, FEAT), f32), ((FEAT, UNITS), f32), ((8, FEAT), f32)], None, s0, s1, s2, s3, name="attn_last")
    bias_grad = bias_grad.reshape(-1)

    if more > 1:
        def spread(v, dim):
            whole = jnp.zeros(v.shape[:dim] + (8 * v.shape[dim],) + v.shape[dim + 1 :], f32)
            whole = lax.dynamic_update_slice_in_dim(whole, v, place * v.shape[dim], dim)
            return lax.psum_scatter(whole, ("dp", "hid"), scatter_dimension=dim, tiled=True)

        in_grad, out_grad = spread(in_grad, 1), spread(out_grad, 1)
        expand_grad, contract_grad, bias_grad = spread(expand_grad, 1), spread(contract_grad, 0), spread(bias_grad, 0)
        vector_grad = lax.psum(vector_grad, "dp") / 2
    return result, grad_input, in_grad, out_grad, expand_grad, contract_grad, bias_grad, vector_grad


def solution(mesh):
    rows = P("mod", ("dp", "hid"))
    in_specs = (rows, P(("dp", "hid")), P(None, ("dp", "hid"), "mod"), rows, rows, P(("dp", "hid"), "mod"),
                P(("dp", "hid")), P(None, "mod"), rows)
    out_specs = (rows, rows, P(None, ("dp", "hid"), "mod"), rows, rows, P(("dp", "hid"), "mod"),
                 P(("dp", "hid")), P(None, "mod"))
    return jax.shard_map(body, mesh=mesh, in_specs=in_specs, out_specs=out_specs, check_vma=False)
```

```python
import jax
import jax.numpy as jnp
from jax import lax
from jax.experimental import pallas as pl
from jax.experimental.pallas import tpu as pltpu
from jax.sharding import PartitionSpec as P

D = 768
HEAD_DIM = 64
L = 529
FEAT = 192
HALF = 265
PAD = 272
ROWS = 2 * PAD
WIDE = 2 * FEAT
UNITS = D // 8
APIECE = 2 * UNITS + 16
FPIECE = 2 * FEAT + 16
eps = 1e-06
bf16 = jnp.bfloat16
f32 = jnp.float32

X = [(0, 1), (1, 0), (2, 3), (3, 2)]
Y = [(0, 2), (2, 0), (1, 3), (3, 1)]


def dot(a, b, ca=1, cb=0):
    return lax.dot_general(a, b, (((ca,), (cb,)), ((), ())), preferred_element_type=f32)


def over_x(v):
    return lax.ppermute(v, "hid", X)


def over_y(v):
    return lax.ppermute(v, "hid", Y)


def over_core(v):
    n = lax.axis_size("dp")
    return lax.ppermute(v, "dp", [(i, i ^ 1) for i in range(n)])


def z_pairs(v, pairs):
    return lax.ppermute(v, "mod", pairs)


def z_one(v):
    return z_pairs(v, [(0, 1), (1, 0), (2, 3), (3, 2)])


def z_three(v):
    return z_pairs(v, [(0, 3), (3, 0), (1, 2), (2, 1)])


def z_two(v):
    return z_pairs(v, [(0, 2), (2, 0), (1, 3), (3, 1)])


def z_all(v):
    return z_one(v), z_two(v), z_three(v)


def after(v, *deps):
    return lax.optimization_barrier((v,) + deps)[0]


def row_pairs(second, back):
    pairs = []
    for dp in range(lax.axis_size("dp")):
        for z in range(4):
            core = dp % 2
            parity = 1 - z % 2 if second else z % 2
            src, dst = dp * 4 + z, (dp - core + z // 2) * 4 + 2 * core + parity
            pairs.append((dst, src) if back else (src, dst))
    return pairs


def rows_there(v, second):
    return lax.ppermute(v, ("dp", "mod"), row_pairs(second, False))


def rows_back(v, second):
    return lax.ppermute(v, ("dp", "mod"), row_pairs(second, True))


VM = pl.BlockSpec(memory_space=pltpu.VMEM)
SM = pl.BlockSpec(memory_space=pltpu.SMEM)


ORDER = []


def call(kernel, outs, scal, *args, limit=20, scratch=(), name=None):
    if ORDER:
        if scal is None:
            args = (after(args[0], ORDER[-1]),) + args[1:]
        else:
            scal = after(scal, ORDER[-1])
    outs = [jax.ShapeDtypeStruct(s, t) for s, t in outs]
    single = len(outs) == 1
    ins = ([] if scal is None else [SM]) + [VM] * len(args)
    if scal is not None:
        args = (scal,) + args
    result = pl.pallas_call(
        kernel,
        out_shape=outs[0] if single else outs,
        in_specs=ins,
        out_specs=VM if single else [VM] * len(outs),
        scratch_shapes=list(scratch),
        cost_estimate=pl.CostEstimate(flops=0, bytes_accessed=500000, transcendentals=0),
        compiler_params=pltpu.CompilerParams(vmem_limit_bytes=limit * 2**20),
        name=name,
    )(*args)
    ORDER.append(result if single else result[0])
    return result


def k_pack_attn(pin, pout, vec, attn):
    u = UNITS
    attn[0:u, 0:FEAT] = pin[0]
    attn[0:u, FEAT:WIDE] = pin[1]
    attn[u : 2 * u, 0:FEAT] = pin[2]
    attn[u : 2 * u, FEAT:WIDE] = pout[...].astype(f32).T.astype(bf16)
    v = vec[...]
    hi = v.astype(bf16)
    lo = (v - hi.astype(f32)).astype(bf16)
    both = jnp.concatenate([hi.astype(f32), lo.astype(f32)], 1)
    attn[2 * u : APIECE, :] = jnp.concatenate([both, jnp.zeros_like(both)], 0).astype(bf16)


def k_pack_ffn(ex, con_t, bias, ffn):
    ffn[0:FEAT, :] = ex[...]
    ffn[FEAT:WIDE, :] = con_t[...]
    ffn[WIDE:FPIECE, :] = jnp.broadcast_to(bias[...].astype(f32)[None], (16, WIDE)).astype(bf16)


def k_scal(where, mine, other, out):
    for i in range(3):
        out[i] = where[i]
    z, core = where[2], where[0]
    here = z // 2 == core
    a, b = jnp.where(here, mine[0], other[0]), jnp.where(here, mine[1], other[1])
    out[3] = jnp.where(z % 2 == 0, a, b)


def k_in(scal, p, c, out1, out2):
    even = scal[2] % 2 == 0

    def fill(a, b):
        for i, src in enumerate((p, c)):
            a[i] = src[0:HALF, 0, :]
            b[i] = src[HALF - 1 : L, 0, :]

    @pl.when(even)
    def _():
        fill(out1, out2)

    @pl.when(jnp.logical_not(even))
    def _():
        fill(out2, out1)


def row_ids(parity, shape, dim):
    place = lax.broadcasted_iota(jnp.int32, shape, dim)
    right = place >= PAD
    slot = jnp.where(right, place - PAD, place)
    ids = 2 * slot - parity + jnp.where(right, 1, 0)
    real = (slot < HALF) & (ids >= 0) & (ids < L)
    return real, ids


def kept_rows(scal, shape=(ROWS, 1), dim=0):
    real, ids = row_ids(scal[2] % 2, shape, dim)
    return real & (ids < scal[3])


def assemble(scal, i, own1, own2, oth1, oth2, out):
    core, even = scal[0], scal[2] % 2 == 0
    a, b, c, d = (r[i].astype(f32) for r in (own1, own2, oth1, oth2))
    own = jnp.where(even, a, b), jnp.where(even, b, a)
    oth = jnp.where(even, c, d), jnp.where(even, d, c)
    first = core == 0
    for q in range(4):
        mine, theirs = (own, oth) if q < 2 else (oth, own)
        v = jnp.where(first, mine[q % 2], theirs[q % 2])
        out[0:HALF, q * FEAT : (q + 1) * FEAT] = v[:, :FEAT]
        out[PAD : PAD + HALF, q * FEAT : (q + 1) * FEAT] = v[:, FEAT:]


def norm(v, gain, shift):
    moved = v - jnp.mean(v, 1, keepdims=True)
    inverse = lax.rsqrt(jnp.mean(moved * moved, 1, keepdims=True) + eps)
    normed = moved * inverse
    return normed, inverse, normed * gain + shift


def norm_back(grad, normed, inverse, gain):
    t = grad * gain
    return inverse * (t - jnp.mean(t, 1, keepdims=True) - normed * jnp.mean(t * normed, 1, keepdims=True))


def vec_block(refs, k):
    v = refs[0][2 * UNITS : APIECE, :].astype(f32)
    for i in (1, 2, 3):
        v = jnp.where(k == i, refs[i][2 * UNITS : APIECE, :].astype(f32), v)
    return v[0:8, :FEAT] + v[0:8, FEAT:]


def k_give(scal, a0, a1, a2, a3, keeps, gives, vec, slots):
    core, z = scal[0], scal[2]
    refs = (a0, a1, a2, a3)
    for j, (lo, hi) in enumerate(((a0, a2), (a1, a3))):
        u, v = lo[0 : 2 * UNITS, :], hi[0 : 2 * UNITS, :]
        keeps[j] = jnp.where(core == 0, u, v)
        gives[j] = jnp.where(core == 0, v, u)
    for q in range(4):
        vec[:, q * FEAT : (q + 1) * FEAT] = vec_block(refs, z ^ q)
    for j in range(2):
        slots[j] = vec_block(refs, 2 * core + j)


def k_join(a, b, out):
    n = a.shape[0]
    out[0:n] = a[...]
    out[n : 2 * n] = b[...]


def k_cross(from_x, from_y, to_x, to_y):
    to_x[...] = from_y[0:2]
    to_y[...] = from_x[2:4]


def k_three(a, b, c, out):
    for i, v in enumerate((a, b, c)):
        out[i] = v[...]


def k_far(y0, y123, x123, to_x, to_y):
    to_x[0] = y0[...]
    to_x[1] = y123[0]
    to_y[...] = x123[1:3]


def k_norm1(scal, own1, own2, oth1, oth2, vec, x, ain, ain_t, buf):
    assemble(scal, 0, own1, own2, oth1, oth2, buf)
    real, _ = row_ids(scal[2] % 2, (ROWS, 1), 0)
    v = jnp.where(real, buf[...], 0.0)
    x[...] = v.astype(bf16)
    low = norm(v, vec[0:1, :], vec[1:2, :])[2].astype(bf16)
    ain[...] = low
    ain_t[...] = low.T


def k_attn(scal, ain, h_own, h_got, fx, fy, da, db, slots, w, q, k, v, lse, mixed, part, low_l, low_r, qt, vt, mt):
    core, hid = scal[0], scal[1]
    for i in range(4):
        for p in range(2):
            for j in range(2):
                src = ((h_own, h_got)[p], None, None, None)[i]
                if i == 0:
                    src = (h_own, h_got)[p][j]
                elif i == 3:
                    src = (da, db)[p][j]
                else:
                    src = (fx, fy)[i - 1][2 * p + j]
                at = pl.multiple_of((4 * (core ^ p) + (hid ^ i)) * UNITS, 32)
                w[j, 0, pl.ds(at, UNITS), :] = src[0:UNITS]
                w[j, 1, pl.ds(at, UNITS), :] = src[UNITS : 2 * UNITS]
    keep = kept_rows(scal)
    lane = lax.broadcasted_iota(jnp.int32, (1, FEAT), 1) // HEAD_DIM
    for j in range(2):
        qk = dot(ain[...], w[j, 0])
        qj = (qk[:, :FEAT] + slots[j, 2:3, :]).astype(bf16) * jnp.asarray(0.125, bf16)
        q[j] = qj
        qt[j] = qj.T
        k[j] = qk[:, FEAT:].astype(bf16)
        vj = (dot(ain[...], w[j, 1, :, 0:FEAT]) + slots[j, 3:4, :]).astype(bf16)
        v[j] = vj
        vt[j] = vj.T
    lse[...] = jnp.zeros_like(lse)
    for j in range(2):
        for h in range(3):
            kh = jnp.where(lane == h, k[j], jnp.zeros((), bf16))
            logits = jnp.where(keep, dot(kh, qt[j]), -1e30)
            top = jnp.max(logits, 0, keepdims=True)
            expo = jnp.exp(logits - top)
            total = jnp.sum(expo, 0, keepdims=True)
            chance = (expo * (1.0 / total)).astype(bf16)
            rows = slice(h * HEAD_DIM, (h + 1) * HEAD_DIM)
            mt[j, rows, :] = dot(vt[j, rows, :], chance)
            lse[3 * j + h : 3 * j + h + 1, :] = top + jnp.log(total)
    total = 0.0
    for j in range(2):
        mj = mt[j].T.astype(bf16)
        mixed[j] = mj
        total += dot(mj, w[j, 1, :, FEAT:WIDE], 1, 1)
    part[...] = total
    low_l[...] = total[:, :WIDE].astype(bf16)
    low_r[...] = total[:, WIDE:].astype(bf16)


def sides(left, right):
    return jnp.concatenate([left[...], right[...]], 1).astype(f32)


def k_norm2(scal, x, part, oth_l, oth_r, vec, c1, c2, d1, d2, resid, low, low_t, grad, grad_t, buf):
    r = x[...].astype(f32) + part[...] + sides(oth_l, oth_r) + vec[4:5, :]
    resid[...] = r
    v = norm(r, vec[5:6, :], vec[6:7, :])[2].astype(bf16)
    low[...] = v
    low_t[...] = v.T
    assemble(scal, 1, c1, c2, d1, d2, buf)
    g = jnp.where(kept_rows(scal), buf[...], 0.0).astype(bf16)
    grad[...] = g
    grad_t[...] = g.T


def gelu_both(v):
    half = 0.5 * (1.0 + lax.erf(v * 0.7071067811865476))
    slope = half + v * jnp.exp(-0.5 * v * v) * 0.3989422804014327
    return v * half, slope


def ffn_kernel(parts, first, last):
    n = len({r for r, _ in parts})

    def kernel(scal, *refs):
        low, low_t, grad, grad_t = refs[:4]
        pieces, refs = refs[4 : 4 + n], refs[4 + n :]
        if not first:
            old_out, old_back, *refs = refs
        if last:
            keep, give, back, low_l, low_r, *refs = refs
        else:
            out, back, *refs = refs
        g_in, g_out, ein, cout = refs
        for s, (r, i) in enumerate(parts):
            src = pieces[r] if i is None else pieces[r].at[i]
            place = pl.ds(pl.multiple_of((scal[2] ^ s) * FEAT, FEAT), FEAT)
            ein[place, :] = src[0:FEAT, :]
            cout[place, :] = src[FEAT:WIDE, :]
            if s == 0:
                bias = src[WIDE:FPIECE, :].astype(f32)[0:1]
        act, slope = gelu_both(dot(low[...], ein[...]) + bias)
        hidden = act.astype(bf16)
        g = (dot(grad[...], cout[...]) * slope).astype(bf16)
        res = dot(hidden, cout[...], 1, 1)
        if not first:
            res = res + old_out[...]
        if last:
            core = scal[0] == 0
            a, b = res[:, :WIDE], res[:, WIDE:]
            keep[...] = jnp.where(core, a, b)
            give[...] = jnp.where(core, b, a).astype(bf16)
        else:
            out[...] = res
        res = dot(g, ein[...], 1, 1)
        if not first:
            res = res + old_back[...]
        back[...] = res
        if last:
            low_l[...] = res[:, :WIDE].astype(bf16)
            low_r[...] = res[:, WIDE:].astype(bf16)
        g_in[0:D, :] = dot(low_t[...], g).astype(bf16)
        sums = jnp.sum(g.astype(f32), 0, keepdims=True)
        g_in[D : D + 16, :] = jnp.broadcast_to(sums, (16, WIDE)).astype(bf16)
        g_out[...] = dot(grad_t[...], hidden).astype(bf16)

    return kernel


def ffn(scal, rows, pieces, parts, acc, last=False):
    if last:
        outs = [((ROWS, WIDE), f32), ((ROWS, WIDE), bf16), ((ROWS, D), f32), ((ROWS, WIDE), bf16), ((ROWS, WIDE), bf16)]
    else:
        outs = [((ROWS, D), f32), ((ROWS, D), f32)]
    outs += [((D + 16, WIDE), bf16), ((D, WIDE), bf16)]
    return call(ffn_kernel(parts, acc is None, last), outs, scal, *rows, *pieces, *(acc or ()),
                scratch=[pltpu.VMEM((D, WIDE), bf16)] * 2, name="ffn")


def place_rows(scal, v, out1, out2):
    even = scal[2] % 2 == 0
    q = []
    for i in range(2):
        part = v[:, i * FEAT : (i + 1) * FEAT]
        q.append(jnp.concatenate([part[0:HALF], part[PAD : PAD + HALF]], 1))
    out1[...] = jnp.where(even, q[0], q[1]).astype(bf16)
    out2[...] = jnp.where(even, q[1], q[0]).astype(bf16)


def k_back(scal, resid, back, oth_l, oth_r, gml, vec, gres, branch, vrows):
    gnm = back[...] + sides(oth_l, oth_r)
    normed, inverse, _ = norm(resid[...], vec[5:6, :], vec[6:7, :])
    g = gml[...].astype(f32)
    res = g + norm_back(gnm, normed, inverse, vec[5:6, :])
    gres[...] = res
    low = res.astype(bf16)
    branch[...] = low
    vrows[...] = jnp.zeros_like(vrows)
    vrows[4:5, :] = jnp.sum(low.astype(f32), 0, keepdims=True)
    vrows[5:6, :] = jnp.sum(gnm * normed, 0, keepdims=True)
    vrows[6:7, :] = jnp.sum(gnm, 0, keepdims=True)
    vrows[7:8, :] = jnp.sum(g, 0, keepdims=True)


def heads_back(j, scal, branch, w, q, k, v, lse, mixed, old, gqk, gv, part, lows, gmt, kt, qt, dqt, dk, dv):
    keep = kept_rows(scal)
    lane = lax.broadcasted_iota(jnp.int32, (1, FEAT), 1) // HEAD_DIM
    none = jnp.zeros((), bf16)
    gm_low = dot(branch[...], w[j, 1, :, FEAT:WIDE]).astype(bf16)
    gmt[...] = gm_low.T
    kt[...] = k[j].T
    qt[...] = q[j].T
    prod_t = (gm_low.astype(f32) * mixed[j].astype(f32)).T
    dk[...] = jnp.zeros_like(dk)
    dv[...] = jnp.zeros_like(dv)
    for h in range(3):
        rows = slice(h * HEAD_DIM, (h + 1) * HEAD_DIM)
        delta = jnp.sum(prod_t[rows, :], 0, keepdims=True)
        logits = jnp.where(keep, dot(jnp.where(lane == h, k[j], none), qt[...]), -1e30)
        chance = jnp.exp(logits - lse[3 * j + h : 3 * j + h + 1, :])
        gchance = dot(jnp.where(lane == h, v[j], none), gmt[...])
        gl = (chance * (gchance - delta)).astype(bf16)
        dv[...] += dot(chance.astype(bf16), jnp.where(lane == h, gm_low, none))
        dk[...] += dot(gl, jnp.where(lane == h, q[j], none))
        dqt[rows, :] = dot(kt[rows, :], gl) * 0.125
    gq = dqt[...].T
    both = jnp.concatenate([gq, dk[...]], 1).astype(bf16)
    gqk[...] = both
    val = dv[...].astype(bf16)
    gv[...] = val
    total = dot(both, w[j, 0], 1, 1) + dot(val, w[j, 1, :, 0:FEAT], 1, 1)
    if old is not None:
        total = total + old[...]
        lows[0][...] = total[:, :WIDE].astype(bf16)
        lows[1][...] = total[:, WIDE:].astype(bf16)
    part[...] = total


def k_back0(scal, branch, w, q, k, v, lse, mixed, gqk, gv, part, *scratch):
    heads_back(0, scal, branch, w, q, k, v, lse, mixed, None, gqk, gv, part, None, *scratch)


def k_back1(scal, branch, w, q, k, v, lse, mixed, old, gqk, gv, part, low_l, low_r, *scratch):
    heads_back(1, scal, branch, w, q, k, v, lse, mixed, old, gqk, gv, part, (low_l, low_r), *scratch)


def k_front(scal, part, oth_l, oth_r, resid, keep, got, x, vec, gres, branch, gqk0, gqk1, gv0, gv1, mixed, ain_t, vrows,
            own, gx, gy, gd1, gd2, out1, out2, vfull, wbuf):
    core, hid, z = scal[0], scal[1], scal[2]
    gna = part[...] + sides(oth_l, oth_r)
    normed, inverse, _ = norm(x[...].astype(f32), vec[0:1, :], vec[1:2, :])
    res = gres[...] + norm_back(gna, normed, inverse, vec[0:1, :])
    first = core == 0
    place_rows(scal, jnp.where(first, res[:, 0:WIDE], res[:, WIDE:D]), out1.at[1], out2.at[1])
    r = jnp.where(first, resid[:, 0:WIDE], resid[:, WIDE:D])
    b = jnp.where(first, vec[7:8, 0:WIDE], vec[7:8, WIDE:D])
    r = r + keep[...] + got[...].astype(f32) + b
    place_rows(scal, jnp.where(kept_rows(scal), r, 0.0), out1.at[0], out2.at[0])
    vfull[...] = vrows[...]
    vfull[0:1, :] = jnp.sum(gna * normed, 0, keepdims=True)
    vfull[1:2, :] = jnp.sum(gna, 0, keepdims=True)
    branch_t = branch[...].T
    dest = lambda i, p, j: ((own, gx, gy)[i].at[2 * p + j] if i < 3 else (gd1, gd2)[p].at[j])
    for j in range(2):
        gqk, gv = ((gqk0, gv0), (gqk1, gv1))[j]
        wbuf[0] = dot(ain_t[...], gqk[...]).astype(bf16)
        wbuf[1, :, 0:FEAT] = dot(ain_t[...], gv[...]).astype(bf16)
        wbuf[1, :, FEAT:WIDE] = dot(branch_t, mixed[j]).astype(bf16)
        src = z ^ (2 * core + j)
        mine = vfull[:, 0:FEAT]
        for i in (1, 2, 3):
            mine = jnp.where(src == i, vfull[:, i * FEAT : (i + 1) * FEAT], mine)
        line = lax.broadcasted_iota(jnp.int32, (8, 1), 0)
        cols_q = jnp.sum(gqk[...].astype(f32), 0, keepdims=True)[:, 0:FEAT]
        cols_v = jnp.sum(gv[...].astype(f32), 0, keepdims=True)
        mine = jnp.where(line == 2, cols_q, jnp.where(line == 3, cols_v, mine))
        mine = jnp.concatenate([mine, jnp.zeros_like(mine)], 1)
        mine = jnp.concatenate([mine, jnp.zeros_like(mine)], 0).astype(bf16)
        for i in range(4):
            for p in range(2):
                at = pl.multiple_of((4 * (core ^ p) + (hid ^ i)) * UNITS, 32)
                to = dest(i, p, j)
                to[0:UNITS, :] = wbuf[0, pl.ds(at, UNITS), :]
                to[UNITS : 2 * UNITS, :] = wbuf[1, pl.ds(at, UNITS), :]
                to[2 * UNITS : APIECE, :] = mine


def plus(a, b):
    return a.astype(f32) + b.astype(f32)


def k_plus(a, b, out):
    out[...] = plus(a[...], b[...]).astype(out.dtype)


def k_fsum(scal, near_in, near_out, xb, yb, keep, s1, s2, s3):
    z = scal[2]
    for k, to in enumerate((keep, s1, s2, s3)):
        rows = pl.ds(pl.multiple_of((z ^ k) * FEAT, FEAT), FEAT)
        tail = slice(D, D + 16)
        to[0:FEAT, :] = (near_in[rows, :] + yb[rows, :].astype(f32)).astype(to.dtype)
        to[FEAT:WIDE, :] = (near_out[rows, :] + xb[rows, :].astype(f32)).astype(to.dtype)
        to[WIDE:FPIECE, :] = (near_in[tail, :] + yb[tail, :].astype(f32)).astype(to.dtype)


def k_zadd(s1, inner, s3, edge, t1, t3):
    t1[...] = plus(s1[...], inner[...]).astype(bf16)
    t3[...] = plus(s3[...], edge[...]).astype(bf16)


def z_back(s2):
    return z_pairs(s2, [(0, 1), (3, 2)]), z_pairs(s2, [(1, 2), (2, 1)])


def k_ffin(keep, r1, r3, ex, con_t, bias):
    v = keep[...] + r1[...].astype(f32) + r3[...].astype(f32)
    ex[...] = v[0:FEAT]
    con_t[...] = v[FEAT:WIDE]
    bias[...] = v[WIDE]


def k_aadd(gx, ry, gy, rx, px, py):
    px[0:2] = gx[0:2]
    px[2:4] = plus(gx[2:4], ry[...]).astype(bf16)
    py[0:2] = plus(gy[0:2], rx[...]).astype(bf16)
    py[2:4] = gy[2:4]


def k_asum(own, sx, sy, keep, give):
    keep[...] = plus(own[0:2], sx[0:2]) + sy[0:2].astype(f32)
    give[...] = (plus(own[2:4], sx[2:4]) + sy[2:4].astype(f32)).astype(bf16)


def k_asel(scal, keep, got, s0, s1, s2, s3):
    first = scal[0] == 0
    a, b = keep[...], got[...].astype(f32)
    lo, hi = jnp.where(first, a, b), jnp.where(first, b, a)
    s0[...] = lo[0]
    s1[...] = lo[1].astype(bf16)
    s2[...] = hi[0].astype(bf16)
    s3[...] = hi[1].astype(bf16)


def k_afin(s0, r1, r3, pin, pout, vec):
    v = s0[...] + r1[...].astype(f32) + r3[...].astype(f32)
    pin[0] = v[0:UNITS, 0:FEAT]
    pin[1] = v[0:UNITS, FEAT:WIDE]
    pin[2] = v[UNITS : 2 * UNITS, 0:FEAT]
    pout[...] = v[UNITS : 2 * UNITS, FEAT:WIDE].T
    vec[...] = v[2 * UNITS : 2 * UNITS + 8, 0:FEAT]


def k_home(scal, b1, b2, out, grad):
    even = scal[2] % 2 == 0
    left = lax.broadcasted_iota(jnp.int32, (1, WIDE), 1) < FEAT
    for i, to in enumerate((out, grad)):
        a, b = b1[i], b2[i]
        s0, s1 = jnp.where(even, a, b), jnp.where(even, b, a)
        t = to.dtype
        to[0 : HALF - 1, 0, :] = s0[0 : HALF - 1].astype(t)
        to[HALF - 1 : HALF, 0, :] = jnp.where(left, s0[HALF - 1 : HALF].astype(f32), s1[0:1].astype(f32)).astype(t)
        to[HALF:L, 0, :] = s1[1:HALF].astype(t)


def body(patches, visible, project_in, project_out, expand, contract, expand_bias, vectors, cotangent):
    n_dp = lax.axis_size("dp")
    more = n_dp // 2
    dp, hid, z = lax.axis_index("dp"), lax.axis_index("hid"), lax.axis_index("mod")
    core = dp % 2
    place = 4 * core + hid
    if more > 1:
        def mine_of(v, dim):
            whole = lax.all_gather(v, ("dp", "hid"), axis=dim, tiled=True)
            size = whole.shape[dim] // 8
            return lax.dynamic_slice_in_dim(whole, place * size, size, dim)

        project_in, project_out = mine_of(project_in, 1), mine_of(project_out, 1)
        expand, contract = mine_of(expand, 1), mine_of(contract, 0)
        expand_bias = mine_of(expand_bias, 0)

    where = jnp.stack([core, hid, z, z]).astype(jnp.int32)

    fpart, apart = (FPIECE, WIDE), (APIECE, WIDE)
    del ORDER[:]
    a0 = call(k_pack_attn, [(apart, bf16)], None, project_in, project_out, vectors, name="pack_attn")
    f0 = call(k_pack_ffn, [(fpart, bf16)], None, expand, contract.T, expand_bias, name="pack_ffn")
    a1, a2, a3 = z_all(a0)
    fx, fy = over_x(f0), over_y(f0)
    pair = ((2, HALF, WIDE), bf16)
    p1, p2 = call(k_in, [pair] * 2, where, patches.reshape(L, 1, WIDE), cotangent.reshape(L, 1, WIDE), name="rows_in")
    counts = over_core(after(visible, a1))
    keeps, gives, vec, slots = call(
        k_give, [((2, 2 * UNITS, WIDE), bf16)] * 2 + [((8, D), f32), ((2, 8, FEAT), f32)], where, after(a0, fx, fy, counts), a1, a2, a3, name="give")
    scal = pl.pallas_call(k_scal, out_shape=jax.ShapeDtypeStruct((4,), jnp.int32), in_specs=[SM] * 3, out_specs=SM, name="counts",
                          compiler_params=pltpu.CompilerParams(vmem_limit_bytes=2**20))(where, visible, counts)
    f1, f2, f3 = z_all(after(f0, a1, a2, a3))
    got = over_core(gives)
    here = call(k_join, [((4, 2 * UNITS, WIDE), bf16)], None, keeps, got, name="join_attn")
    from_x, from_y = over_x(here), over_y(here)
    to_x, to_y = call(k_cross, [((2, 2 * UNITS, WIDE), bf16)] * 2, None, from_x, from_y, name="cross_attn")
    diag_a, diag_b = over_x(to_x), over_y(to_y)
    f123 = call(k_three, [((3,) + fpart, bf16)], None, f1, f2, after(f3, diag_a, diag_b), name="join_ffn")
    fx123, fy123 = over_x(f123), over_y(f123)
    p1, p2 = after((p1, p2), f1, f2, f3)
    p1, p2 = rows_there(p1, False), rows_there(p2, True)
    q1, q2 = over_core(p1), over_core(p2)
    wide, tall = ((ROWS, D), bf16), ((D, ROWS), bf16)
    rows32 = ((ROWS, D), f32)
    x, ain, ain_t = call(k_norm1, [wide, wide, tall], where, p1, p2, q1, q2, vec, scratch=[pltpu.VMEM((ROWS, D), f32)], name="norm_attn")

    head, half = ((2, ROWS, FEAT), bf16), ((ROWS, WIDE), bf16)
    flip = pltpu.VMEM((2, FEAT, ROWS), bf16)
    w, q, k, v, lse, mixed, part, low_l, low_r = call(
        k_attn, [((2, 2, D, WIDE), bf16), head, head, head, ((8, ROWS), f32), head, rows32, half, half], scal,
        ain, keeps, got, from_x, from_y, diag_a, diag_b, slots,
        scratch=[flip, flip, pltpu.VMEM((2, FEAT, ROWS), f32)], name="attend")
    oth_l, oth_r = over_core(low_l), over_core(low_r)
    resid, low, low_t, gml, gml_t = call(
        k_norm2, [rows32, wide, tall, wide, tall], scal, x, part, oth_l, oth_r, vec, p1, p2, q1, q2,
        scratch=[pltpu.VMEM((ROWS, D), f32)], name="norm_mlp")

    rows = (low, low_t, gml, gml_t)
    o_acc, b_acc, own_in, own_out = ffn(scal, rows, (f0, f1, f2, f3), [(i, None) for i in range(4)], None)
    near = [(0, None), (1, 0), (1, 1), (1, 2)]
    to_x, to_y = call(k_far, [((2,) + fpart, bf16)] * 2, None, fy, fy123, fx123, name="far_ffn")
    fd_a, fd_b = over_x(to_x), over_y(to_y)
    o_acc, b_acc, x_in, x_out = ffn(scal, rows, (fx, fx123), near, (o_acc, b_acc))
    sxa = over_x(x_in)
    o_acc, b_acc, y_in, y_out = ffn(scal, rows, (fy, fy123), near, (o_acc, b_acc))
    sya = over_y(y_out)
    keep, give, back, low_l, low_r, d_in, d_out = ffn(scal, rows, (fd_a, fd_b), [(0, 0), (0, 1), (1, 0), (1, 1)], (o_acc, b_acc), last=True)
    oth_l, oth_r = over_core(low_l), over_core(low_r)
    rx, ry = over_x(d_in), over_y(d_out)

    side = pltpu.VMEM((FEAT, ROWS), bf16)
    acc = pltpu.VMEM((ROWS, FEAT), f32)
    gres, branch, vrows = call(k_back, [rows32, wide, ((8, D), f32)], scal, resid, back, oth_l, oth_r, gml, vec, name="norm_mlp_back")
    work = [side, side, side, pltpu.VMEM((FEAT, ROWS), f32), acc, acc]
    one, thin = ((ROWS, WIDE), bf16), ((ROWS, FEAT), bf16)
    gqk0, gv0, part = call(k_back0, [one, thin, rows32], scal, branch, w, q, k, v, lse, mixed, scratch=work, name="attend_back")
    in_shape, out_shape = (D + 16, WIDE), (D, WIDE)
    near_in = call(k_plus, [(in_shape, f32)], None, own_in, sxa, name="ffn_sum_x")
    near_out = call(k_plus, [(out_shape, f32)], None, own_out, sya, name="ffn_sum_y")
    got_out = over_core(after(give, near_out))
    gqk1, gv1, part, low_l, low_r = call(k_back1, [one, thin, rows32, half, half], scal, branch, w, q, k, v, lse, mixed, part, scratch=work, name="attend_back")
    oth_l, oth_r = over_core(low_l), over_core(low_r)
    xb = call(k_plus, [(out_shape, bf16)], None, x_out, ry, name="ffn_add_x")
    yb = call(k_plus, [(in_shape, bf16)], None, y_in, rx, name="ffn_add_y")
    sxb, syb = over_x(xb), over_y(yb)
    four, two = ((4, APIECE, WIDE), bf16), ((2, APIECE, WIDE), bf16)
    ga_own, ga_x, ga_y, ga_d1, ga_d2, r1, r2 = call(
        k_front, [four, four, four, two, two, pair, pair], scal, part, oth_l, oth_r, resid, keep, got_out, x, vec, gres, branch,
        gqk0, gqk1, gv0, gv1, mixed, ain_t, vrows, scratch=[pltpu.VMEM((8, D), f32), pltpu.VMEM((2, D, WIDE), bf16)], name="norm_attn_back")
    ax, ay = over_x(ga_d1), over_y(ga_d2)
    px, py = call(k_aadd, [four, four], None, ga_x, ay, ga_y, ax, name="attn_add")
    tx, ty = over_x(px), over_y(py)
    r1, r2 = rows_back(r1, False), rows_back(r2, True)
    result, grad_input = call(k_home, [((L, 1, WIDE), bf16), ((L, 1, WIDE), f32)], where, r1, r2, name="rows_out")
    result, grad_input = result.reshape(1, L * WIDE), grad_input.reshape(1, L * WIDE)
    fk, s1, s2, s3 = call(k_fsum, [(fpart, f32)] + [(fpart, bf16)] * 3, where, near_in, near_out, sxb, syb, name="ffn_sum")
    edge, inner = z_back(s2)
    t1, t3 = call(k_zadd, [(fpart, bf16)] * 2, None, s1, inner, s3, edge, name="ffn_zadd")
    f_one, f_three = z_one(t1), z_three(t3)
    ak, give = call(k_asum, [((2,) + apart, f32), ((2,) + apart, bf16)], None, ga_own, tx, ty, name="attn_sum")
    got = over_core(give)
    s0, s1, s2, s3 = call(k_asel, [(apart, f32)] + [(apart, bf16)] * 3, where, ak, got, name="attn_slots")
    edge, inner = z_back(s2)
    t1, t3 = call(k_zadd, [(apart, bf16)] * 2, None, s1, inner, s3, edge, name="attn_zadd")
    a_one, a_three = z_one(t1), z_three(t3)
    expand_grad, contract_grad, bias_grad = call(
        k_ffin, [((FEAT, WIDE), f32), ((FEAT, WIDE), f32), ((WIDE,), f32)], None, fk, f_one, f_three, name="ffn_last")
    in_grad, out_grad, vector_grad = call(
        k_afin, [((3, UNITS, FEAT), f32), ((FEAT, UNITS), f32), ((8, FEAT), f32)], None, s0, a_one, a_three, name="attn_last")
    contract_grad = contract_grad.T

    if more > 1:
        def spread(v, dim):
            whole = jnp.zeros(v.shape[:dim] + (8 * v.shape[dim],) + v.shape[dim + 1 :], f32)
            whole = lax.dynamic_update_slice_in_dim(whole, v, place * v.shape[dim], dim)
            return lax.psum_scatter(whole, ("dp", "hid"), scatter_dimension=dim, tiled=True)

        in_grad, out_grad = spread(in_grad, 1), spread(out_grad, 1)
        expand_grad, contract_grad, bias_grad = spread(expand_grad, 1), spread(contract_grad, 0), spread(bias_grad, 0)
        vector_grad = lax.psum(vector_grad, "dp") / 2
    return result, grad_input, in_grad, out_grad, expand_grad, contract_grad, bias_grad, vector_grad


def solution(mesh):
    rows = P("mod", ("dp", "hid"))
    in_specs = (rows, P(("dp", "hid")), P(None, ("dp", "hid"), "mod"), rows, rows, P(("dp", "hid"), "mod"),
                P(("dp", "hid")), P(None, "mod"), rows)
    out_specs = (rows, rows, P(None, ("dp", "hid"), "mod"), rows, rows, P(("dp", "hid"), "mod"),
                 P(("dp", "hid")), P(None, "mod"))
    return jax.shard_map(body, mesh=mesh, in_specs=in_specs, out_specs=out_specs, check_vma=False)
```

```python
import jax
import jax.numpy as jnp
from jax import lax
from jax.experimental import pallas as pl
from jax.experimental.pallas import tpu as pltpu
from jax.sharding import PartitionSpec as P

D = 768
HEAD_DIM = 64
L = 529
FEAT = 192
HALF = 265
PAD = 272
ROWS = 2 * PAD
WIDE = 2 * FEAT
UNITS = D // 8
APIECE = 2 * UNITS + 16
FPIECE = 2 * FEAT + 16
eps = 1e-06
bf16 = jnp.bfloat16
f32 = jnp.float32

X = [(0, 1), (1, 0), (2, 3), (3, 2)]
Y = [(0, 2), (2, 0), (1, 3), (3, 1)]


def dot(a, b, ca=1, cb=0):
    return lax.dot_general(a, b, (((ca,), (cb,)), ((), ())), preferred_element_type=f32)


def over_x(v):
    return lax.ppermute(v, "hid", X)


def over_y(v):
    return lax.ppermute(v, "hid", Y)


def over_core(v):
    n = lax.axis_size("dp")
    return lax.ppermute(v, "dp", [(i, i ^ 1) for i in range(n)])


def z_pairs(v, pairs):
    return lax.ppermute(v, "mod", pairs)


def z_one(v):
    return z_pairs(v, [(0, 1), (1, 0), (2, 3), (3, 2)])


def z_three(v):
    return z_pairs(v, [(0, 3), (3, 0), (1, 2), (2, 1)])


def z_two(v):
    return z_pairs(v, [(0, 2), (2, 0), (1, 3), (3, 1)])


def z_all(v):
    return z_one(v), z_two(v), z_three(v)


def exchange(parts):
    return [over_core(p) for p in parts]


def after(v, *deps):
    return lax.optimization_barrier((v,) + deps)[0]


def row_pairs(second, back):
    pairs = []
    for dp in range(lax.axis_size("dp")):
        for z in range(4):
            core = dp % 2
            parity = 1 - z % 2 if second else z % 2
            src, dst = dp * 4 + z, (dp - core + z // 2) * 4 + 2 * core + parity
            pairs.append((dst, src) if back else (src, dst))
    return pairs


def rows_there(v, second):
    return lax.ppermute(v, ("dp", "mod"), row_pairs(second, False))


def rows_back(v, second):
    return lax.ppermute(v, ("dp", "mod"), row_pairs(second, True))


VM = pl.BlockSpec(memory_space=pltpu.VMEM)
SM = pl.BlockSpec(memory_space=pltpu.SMEM)


ORDER = []


def call(kernel, outs, scal, *args, seen=None, limit=20, scratch=(), name=None):
    if ORDER:
        if scal is None:
            args = (after(args[0], ORDER[-1]),) + args[1:]
        else:
            scal = after(scal, ORDER[-1])
    outs = [jax.ShapeDtypeStruct(s, t) for s, t in outs]
    single = len(outs) == 1
    ins = [VM] * len(args)
    for extra in (seen, scal):
        if extra is not None:
            ins, args = [SM] + ins, (extra,) + args
    result = pl.pallas_call(
        kernel,
        out_shape=outs[0] if single else outs,
        in_specs=ins,
        out_specs=VM if single else [VM] * len(outs),
        scratch_shapes=list(scratch),
        cost_estimate=pl.CostEstimate(flops=0, bytes_accessed=500000, transcendentals=0),
        compiler_params=pltpu.CompilerParams(vmem_limit_bytes=limit * 2**20),
        name=name,
    )(*args)
    ORDER.append(result if single else result[0])
    return result


def k_pack_attn(pin, pout, vec, attn):
    u = UNITS
    attn[0:u, 0:FEAT] = pin[0]
    attn[0:u, FEAT:WIDE] = pin[1]
    attn[u : 2 * u, 0:FEAT] = pin[2]
    attn[u : 2 * u, FEAT:WIDE] = pout[...].astype(f32).T.astype(bf16)
    v = vec[...]
    hi = v.astype(bf16)
    lo = (v - hi.astype(f32)).astype(bf16)
    both = jnp.concatenate([hi.astype(f32), lo.astype(f32)], 1)
    attn[2 * u : APIECE, :] = jnp.concatenate([both, jnp.zeros_like(both)], 0).astype(bf16)


def k_pack_ffn(ex, con_t, bias, ffn):
    ffn[0:FEAT, :] = ex[...]
    ffn[FEAT:WIDE, :] = con_t[...]
    ffn[WIDE:FPIECE, :] = jnp.broadcast_to(bias[...].astype(f32)[None], (16, WIDE)).astype(bf16)


def count_row(count):
    lane = lax.broadcasted_iota(jnp.int32, (1, FEAT), 1)
    value = jnp.where(lane == 0, count // 32, jnp.where(lane == 1, count % 32, 0))
    return value.astype(f32).astype(bf16)


def k_in(scal, seen, src, out1, out2):
    even = scal[2] % 2 == 0

    def fill(a, b):
        a[0:HALF, :] = src[0:HALF, 0, :]
        b[0:HALF, :] = src[HALF - 1 : L, 0, :]
        a[HALF - 1 : HALF, FEAT:WIDE] = count_row(seen[0])
        b[0:1, 0:FEAT] = count_row(seen[1])

    @pl.when(even)
    def _():
        fill(out1, out2)

    @pl.when(jnp.logical_not(even))
    def _():
        fill(out2, out1)


def k_in_each(scal, seen, p, c, p1, p2, c1, c2):
    k_in(scal, seen, p, p1, p2)
    k_in(scal, seen, c, c1, c2)


def row_ids(parity, shape, dim):
    place = lax.broadcasted_iota(jnp.int32, shape, dim)
    right = place >= PAD
    slot = jnp.where(right, place - PAD, place)
    ids = 2 * slot - parity + jnp.where(right, 1, 0)
    real = (slot < HALF) & (ids >= 0) & (ids < L)
    return real, ids


def kept_rows(scal, count):
    real, ids = row_ids(scal[2] % 2, (ROWS, 1), 0)
    return real & (ids.astype(f32) < count[0:1, 0:1])


def assemble(scal, own1, own2, oth1, oth2, out):
    core, even = scal[0], scal[2] % 2 == 0
    a, b, c, d = (r[...].astype(f32) for r in (own1, own2, oth1, oth2))
    own = jnp.where(even, a, b), jnp.where(even, b, a)
    oth = jnp.where(even, c, d), jnp.where(even, d, c)
    first = core == 0
    for q in range(4):
        mine, theirs = (own, oth) if q < 2 else (oth, own)
        v = jnp.where(first, mine[q % 2], theirs[q % 2])
        out[0:HALF, q * FEAT : (q + 1) * FEAT] = v[:, :FEAT]
        out[PAD : PAD + HALF, q * FEAT : (q + 1) * FEAT] = v[:, FEAT:]


def norm(v, gain, shift):
    moved = v - jnp.mean(v, 1, keepdims=True)
    inverse = lax.rsqrt(jnp.mean(moved * moved, 1, keepdims=True) + eps)
    normed = moved * inverse
    return normed, inverse, normed * gain + shift


def norm_back(grad, normed, inverse, gain):
    t = grad * gain
    return inverse * (t - jnp.mean(t, 1, keepdims=True) - normed * jnp.mean(t * normed, 1, keepdims=True))


def vec_block(refs, k):
    v = refs[0][2 * UNITS : APIECE, :].astype(f32)
    for i in (1, 2, 3):
        v = jnp.where(k == i, refs[i][2 * UNITS : APIECE, :].astype(f32), v)
    return v[0:8, :FEAT] + v[0:8, FEAT:]


def k_give(scal, a0, a1, a2, a3, keeps, vec, slots, give0, give1):
    core, z = scal[0], scal[2]
    refs = (a0, a1, a2, a3)
    for j, (lo, hi) in enumerate(((a0, a2), (a1, a3))):
        u, v = lo[0 : 2 * UNITS, :], hi[0 : 2 * UNITS, :]
        keeps[j] = jnp.where(core == 0, u, v)
        (give0, give1)[j][...] = jnp.where(core == 0, v, u)
    for q in range(4):
        vec[:, q * FEAT : (q + 1) * FEAT] = vec_block(refs, z ^ q)
    for j in range(2):
        slots[j] = vec_block(refs, 2 * core + j)


def k_join(keeps, got0, got1, out):
    out[0:2] = keeps[...]
    out[2] = got0[...]
    out[3] = got1[...]


def k_cross(from_x, from_y, to_x, to_y):
    to_x[...] = from_y[0:2]
    to_y[...] = from_x[2:4]


def k_three(a, b, c, out):
    for i, v in enumerate((a, b, c)):
        out[i] = v[...]


def k_far(y0, y123, x123, to_x, to_y):
    to_x[0] = y0[...]
    to_x[1] = y123[0]
    to_y[...] = x123[1:3]


def k_norm1(scal, own1, own2, oth1, oth2, vec, x, ain, ain_t, count, buf):
    assemble(scal, own1, own2, oth1, oth2, buf)
    a, b = own1[HALF - 1 : HALF, FEAT : FEAT + 128].astype(f32), own1[0:1, 0:128].astype(f32)
    v = jnp.where(scal[2] % 2 == 0, a, b)
    lane = lax.broadcasted_iota(jnp.int32, (1, 128), 1)
    v = jnp.sum(v * jnp.where(lane == 0, 32.0, jnp.where(lane == 1, 1.0, 0.0)), 1, keepdims=True)
    count[...] = jnp.broadcast_to(v, (8, 128))
    real, _ = row_ids(scal[2] % 2, (ROWS, 1), 0)
    v = jnp.where(real, buf[...], 0.0)
    x[...] = v.astype(bf16)
    low = norm(v, vec[0:1, :], vec[1:2, :])[2].astype(bf16)
    ain[...] = low
    ain_t[...] = low.T


def k_attn(scal, count, ain, here, fx, fy, da, db, slots, w, q, k, v, lse, mixed, part, *rest):
    *lows, qt, vt, mt = rest
    core, hid = scal[0], scal[1]
    for i in range(4):
        for p in range(2):
            for j in range(2):
                src = (da, db)[p][j] if i == 3 else (here, fx, fy)[i][2 * p + j]
                at = pl.multiple_of((4 * (core ^ p) + (hid ^ i)) * UNITS, 32)
                w[j, 0, pl.ds(at, UNITS), :] = src[0:UNITS]
                w[j, 1, pl.ds(at, UNITS), :] = src[UNITS : 2 * UNITS]
    keep = kept_rows(scal, count)
    lane = lax.broadcasted_iota(jnp.int32, (1, FEAT), 1) // HEAD_DIM
    for j in range(2):
        qk = dot(ain[...], w[j, 0])
        qj = (qk[:, :FEAT] + slots[j, 2:3, :]).astype(bf16) * jnp.asarray(0.125, bf16)
        q[j] = qj
        qt[j] = qj.T
        k[j] = qk[:, FEAT:].astype(bf16)
        vj = (dot(ain[...], w[j, 1, :, 0:FEAT]) + slots[j, 3:4, :]).astype(bf16)
        v[j] = vj
        vt[j] = vj.T
    lse[...] = jnp.zeros_like(lse)
    for j in range(2):
        for h in range(3):
            kh = jnp.where(lane == h, k[j], jnp.zeros((), bf16))
            logits = jnp.where(keep, dot(kh, qt[j]), -1e30)
            top = jnp.max(logits, 0, keepdims=True)
            expo = jnp.exp(logits - top)
            total = jnp.sum(expo, 0, keepdims=True)
            chance = (expo * (1.0 / total)).astype(bf16)
            rows = slice(h * HEAD_DIM, (h + 1) * HEAD_DIM)
            mt[j, rows, :] = dot(vt[j, rows, :], chance)
            lse[3 * j + h : 3 * j + h + 1, :] = top + jnp.log(total)
    total = 0.0
    for j in range(2):
        mj = mt[j].T.astype(bf16)
        mixed[j] = mj
        total += dot(mj, w[j, 1, :, FEAT:WIDE], 1, 1)
    part[...] = total
    put_sides(total, lows)


def sides(left, right):
    return jnp.concatenate([left[...], right[...]], 1).astype(f32)


def put_sides(total, parts):
    parts[0][...] = total[:, :WIDE].astype(bf16)
    parts[1][...] = total[:, WIDE:].astype(bf16)


def k_norm2(scal, count, x, part, oth_l, oth_r, vec, c1, c2, d1, d2, resid, low, low_t, grad, grad_t, buf):
    r = x[...].astype(f32) + part[...] + sides(oth_l, oth_r) + vec[4:5, :]
    resid[...] = r
    v = norm(r, vec[5:6, :], vec[6:7, :])[2].astype(bf16)
    low[...] = v
    low_t[...] = v.T
    assemble(scal, c1, c2, d1, d2, buf)
    g = jnp.where(kept_rows(scal, count), buf[...], 0.0).astype(bf16)
    grad[...] = g
    grad_t[...] = g.T


def gelu_both(v):
    half = 0.5 * (1.0 + lax.erf(v * 0.7071067811865476))
    slope = half + v * jnp.exp(-0.5 * v * v) * 0.3989422804014327
    return v * half, slope


def ffn_kernel(parts, first, last):
    n = len({r for r, _ in parts})

    def kernel(scal, *refs):
        low, low_t, grad, grad_t = refs[:4]
        pieces, refs = refs[4 : 4 + n], refs[4 + n :]
        if not first:
            old_out, old_back, *refs = refs
        if last:
            keep, give, back, *refs = refs
            lows, refs = refs[:2], refs[2:]
        else:
            out, back, *refs = refs
        g_in, g_out, ein, cout = refs
        for s, (r, i) in enumerate(parts):
            src = pieces[r] if i is None else pieces[r].at[i]
            place = pl.ds(pl.multiple_of((scal[2] ^ s) * FEAT, FEAT), FEAT)
            ein[place, :] = src[0:FEAT, :]
            cout[place, :] = src[FEAT:WIDE, :]
            if s == 0:
                bias = src[WIDE:FPIECE, :].astype(f32)[0:1]
        act, slope = gelu_both(dot(low[...], ein[...]) + bias)
        hidden = act.astype(bf16)
        g = (dot(grad[...], cout[...]) * slope).astype(bf16)
        res = dot(hidden, cout[...], 1, 1)
        if not first:
            res = res + old_out[...]
        if last:
            core = scal[0] == 0
            a, b = res[:, :WIDE], res[:, WIDE:]
            keep[...] = jnp.where(core, a, b)
            give[...] = jnp.where(core, b, a).astype(bf16)
        else:
            out[...] = res
        res = dot(g, ein[...], 1, 1)
        if not first:
            res = res + old_back[...]
        back[...] = res
        if last:
            put_sides(res, lows)
        g_in[0:D, :] = dot(low_t[...], g).astype(bf16)
        sums = jnp.sum(g.astype(f32), 0, keepdims=True)
        g_in[D : D + 16, :] = jnp.broadcast_to(sums, (16, WIDE)).astype(bf16)
        g_out[...] = dot(grad_t[...], hidden).astype(bf16)

    return kernel


def ffn(scal, rows, pieces, parts, acc, last=False):
    if last:
        outs = [((ROWS, WIDE), f32), ((ROWS, WIDE), bf16), ((ROWS, D), f32)] + [((ROWS, WIDE), bf16)] * 2
    else:
        outs = [((ROWS, D), f32), ((ROWS, D), f32)]
    outs += [((D + 16, WIDE), bf16), ((D, WIDE), bf16)]
    return call(ffn_kernel(parts, acc is None, last), outs, scal, *rows, *pieces, *(acc or ()),
                scratch=[pltpu.VMEM((D, WIDE), bf16)] * 2, name="ffn")


def place_rows(scal, v, out1, out2):
    even = scal[2] % 2 == 0
    q = []
    for i in range(2):
        part = v[:, i * FEAT : (i + 1) * FEAT]
        q.append(jnp.concatenate([part[0:HALF], part[PAD : PAD + HALF]], 1))
    out1[...] = jnp.where(even, q[0], q[1]).astype(bf16)
    out2[...] = jnp.where(even, q[1], q[0]).astype(bf16)


def k_back(scal, resid, back, oth_l, oth_r, gml, vec, gres, branch, vrows):
    gnm = back[...] + sides(oth_l, oth_r)
    normed, inverse, _ = norm(resid[...], vec[5:6, :], vec[6:7, :])
    g = gml[...].astype(f32)
    res = g + norm_back(gnm, normed, inverse, vec[5:6, :])
    gres[...] = res
    low = res.astype(bf16)
    branch[...] = low
    vrows[...] = jnp.zeros_like(vrows)
    vrows[4:5, :] = jnp.sum(low.astype(f32), 0, keepdims=True)
    vrows[5:6, :] = jnp.sum(gnm * normed, 0, keepdims=True)
    vrows[6:7, :] = jnp.sum(gnm, 0, keepdims=True)
    vrows[7:8, :] = jnp.sum(g, 0, keepdims=True)


def heads_back(j, scal, count, branch, w, q, k, v, lse, mixed, old, gqk, gv, part, lows, gmt, kt, qt, dqt, dk, dv):
    keep = kept_rows(scal, count)
    lane = lax.broadcasted_iota(jnp.int32, (1, FEAT), 1) // HEAD_DIM
    none = jnp.zeros((), bf16)
    gm_low = dot(branch[...], w[j, 1, :, FEAT:WIDE]).astype(bf16)
    gmt[...] = gm_low.T
    kt[...] = k[j].T
    qt[...] = q[j].T
    prod_t = (gm_low.astype(f32) * mixed[j].astype(f32)).T
    dk[...] = jnp.zeros_like(dk)
    dv[...] = jnp.zeros_like(dv)
    for h in range(3):
        rows = slice(h * HEAD_DIM, (h + 1) * HEAD_DIM)
        delta = jnp.sum(prod_t[rows, :], 0, keepdims=True)
        logits = jnp.where(keep, dot(jnp.where(lane == h, k[j], none), qt[...]), -1e30)
        chance = jnp.exp(logits - lse[3 * j + h : 3 * j + h + 1, :])
        gchance = dot(jnp.where(lane == h, v[j], none), gmt[...])
        gl = (chance * (gchance - delta)).astype(bf16)
        dv[...] += dot(chance.astype(bf16), jnp.where(lane == h, gm_low, none))
        dk[...] += dot(gl, jnp.where(lane == h, q[j], none))
        dqt[rows, :] = dot(kt[rows, :], gl) * 0.125
    gq = dqt[...].T
    both = jnp.concatenate([gq, dk[...]], 1).astype(bf16)
    gqk[...] = both
    val = dv[...].astype(bf16)
    gv[...] = val
    total = dot(both, w[j, 0], 1, 1) + dot(val, w[j, 1, :, 0:FEAT], 1, 1)
    if old is not None:
        total = total + old[...]
        put_sides(total, lows)
    part[...] = total


def k_back0(scal, count, branch, w, q, k, v, lse, mixed, gqk, gv, part, *scratch):
    heads_back(0, scal, count, branch, w, q, k, v, lse, mixed, None, gqk, gv, part, None, *scratch)


def k_back1(scal, count, branch, w, q, k, v, lse, mixed, old, gqk, gv, part, *refs):
    heads_back(1, scal, count, branch, w, q, k, v, lse, mixed, old, gqk, gv, part, refs[:2], *refs[2:])


def rows_result(scal, count, resid, keep, got, vec, out1, out2):
    first = scal[0] == 0
    r = jnp.where(first, resid[:, 0:WIDE], resid[:, WIDE:D])
    b = jnp.where(first, vec[7:8, 0:WIDE], vec[7:8, WIDE:D])
    r = r + keep[...] + got[...].astype(f32) + b
    place_rows(scal, jnp.where(kept_rows(scal, count), r, 0.0), out1, out2)


def k_front(scal, count, resid, keep, got, part, oth_l, oth_r, x, vec, gres, branch, gqk0, gqk1, gv0, gv1, mixed, ain_t, vrows,
            own, gx, gy, gd1, gd2, out1, out2, vfull, wbuf):
    core, hid, z = scal[0], scal[1], scal[2]
    gna = part[...] + sides(oth_l, oth_r)
    normed, inverse, _ = norm(x[...].astype(f32), vec[0:1, :], vec[1:2, :])
    res = gres[...] + norm_back(gna, normed, inverse, vec[0:1, :])
    first = core == 0
    rows_result(scal, count, resid, keep, got, vec, out1.at[0], out2.at[0])
    place_rows(scal, jnp.where(first, res[:, 0:WIDE], res[:, WIDE:D]), out1.at[1], out2.at[1])
    vfull[...] = vrows[...]
    vfull[0:1, :] = jnp.sum(gna * normed, 0, keepdims=True)
    vfull[1:2, :] = jnp.sum(gna, 0, keepdims=True)
    branch_t = branch[...].T
    dest = lambda i, p, j: ((own, gx, gy)[i].at[2 * p + j] if i < 3 else (gd1, gd2)[p].at[j])
    for j in range(2):
        gqk, gv = ((gqk0, gv0), (gqk1, gv1))[j]
        wbuf[0] = dot(ain_t[...], gqk[...]).astype(bf16)
        wbuf[1, :, 0:FEAT] = dot(ain_t[...], gv[...]).astype(bf16)
        wbuf[1, :, FEAT:WIDE] = dot(branch_t, mixed[j]).astype(bf16)
        src = z ^ (2 * core + j)
        mine = vfull[:, 0:FEAT]
        for i in (1, 2, 3):
            mine = jnp.where(src == i, vfull[:, i * FEAT : (i + 1) * FEAT], mine)
        line = lax.broadcasted_iota(jnp.int32, (8, 1), 0)
        cols_q = jnp.sum(gqk[...].astype(f32), 0, keepdims=True)[:, 0:FEAT]
        cols_v = jnp.sum(gv[...].astype(f32), 0, keepdims=True)
        mine = jnp.where(line == 2, cols_q, jnp.where(line == 3, cols_v, mine))
        mine = jnp.concatenate([mine, jnp.zeros_like(mine)], 1)
        mine = jnp.concatenate([mine, jnp.zeros_like(mine)], 0).astype(bf16)
        for i in range(4):
            for p in range(2):
                at = pl.multiple_of((4 * (core ^ p) + (hid ^ i)) * UNITS, 32)
                to = dest(i, p, j)
                to[0:UNITS, :] = wbuf[0, pl.ds(at, UNITS), :]
                to[UNITS : 2 * UNITS, :] = wbuf[1, pl.ds(at, UNITS), :]
                to[2 * UNITS : APIECE, :] = mine


def plus(a, b):
    return a.astype(f32) + b.astype(f32)


def k_plus(a, b, out):
    out[...] = plus(a[...], b[...]).astype(out.dtype)


def k_fsum(scal, near_in, near_out, xb, yb, keep, s1, s2, s3):
    z = scal[2]
    for k, to in enumerate((keep, s1, s2, s3)):
        rows = pl.ds(pl.multiple_of((z ^ k) * FEAT, FEAT), FEAT)
        tail = slice(D, D + 16)
        to[0:FEAT, :] = (near_in[rows, :] + yb[rows, :].astype(f32)).astype(to.dtype)
        to[FEAT:WIDE, :] = (near_out[rows, :] + xb[rows, :].astype(f32)).astype(to.dtype)
        to[WIDE:FPIECE, :] = (near_in[tail, :] + yb[tail, :].astype(f32)).astype(to.dtype)


def k_zadd(s3, *refs):
    *r2, t3 = refs
    n = s3.shape[0] // len(r2)
    for i, r in enumerate(r2):
        rows = slice(i * n, (i + 1) * n)
        t3[rows, :] = plus(s3[rows, :], r[...]).astype(bf16)


def k_ffin(keep, r1, r3, ex, con_t, bias):
    v = keep[...] + r1[...].astype(f32) + r3[...].astype(f32)
    ex[...] = v[0:FEAT]
    con_t[...] = v[FEAT:WIDE]
    bias[...] = v[WIDE]


def k_aadd(gx, ry, gy, rx, px, py):
    px[0:2] = gx[0:2]
    px[2:4] = plus(gx[2:4], ry[...]).astype(bf16)
    py[0:2] = plus(gy[0:2], rx[...]).astype(bf16)
    py[2:4] = gy[2:4]


def k_asum(own, sx, sy, keep, give0, give1):
    keep[...] = plus(own[0:2], sx[0:2]) + sy[0:2].astype(f32)
    give = (plus(own[2:4], sx[2:4]) + sy[2:4].astype(f32)).astype(bf16)
    give0[...] = give[0]
    give1[...] = give[1]


def k_asel(scal, keep, got0, got1, s0, s1, s3, s2a, s2b):
    first = scal[0] == 0
    a, b = keep[0], got0[...].astype(f32)
    s0[...] = jnp.where(first, a, b)
    hi = jnp.where(first, b, a).astype(bf16)
    n = APIECE // 2
    s2a[...] = hi[0:n]
    s2b[...] = hi[n:APIECE]
    a, b = keep[1], got1[...].astype(f32)
    s1[...] = jnp.where(first, a, b).astype(bf16)
    s3[...] = jnp.where(first, b, a).astype(bf16)


def k_afin(s0, r1, r3, pin, pout, vec):
    v = s0[...] + r1[...].astype(f32) + r3[...].astype(f32)
    pin[0] = v[0:UNITS, 0:FEAT]
    pin[1] = v[0:UNITS, FEAT:WIDE]
    pin[2] = v[UNITS : 2 * UNITS, 0:FEAT]
    pout[...] = v[UNITS : 2 * UNITS, FEAT:WIDE].T
    vec[...] = v[2 * UNITS : 2 * UNITS + 8, 0:FEAT]


def k_home(scal, b1, b2, to):
    even = scal[2] % 2 == 0
    left = lax.broadcasted_iota(jnp.int32, (1, WIDE), 1) < FEAT
    a, b = b1[...], b2[...]
    s0, s1 = jnp.where(even, a, b), jnp.where(even, b, a)
    t = to.dtype
    to[0 : HALF - 1, 0, :] = s0[0 : HALF - 1].astype(t)
    to[HALF - 1 : HALF, 0, :] = jnp.where(left, s0[HALF - 1 : HALF].astype(f32), s1[0:1].astype(f32)).astype(t)
    to[HALF:L, 0, :] = s1[1:HALF].astype(t)


def k_home_both(scal, b1, b2, out, grad):
    k_home(scal, b1.at[0], b2.at[0], out)
    k_home(scal, b1.at[1], b2.at[1], grad)


def body(patches, visible, project_in, project_out, expand, contract, expand_bias, vectors, cotangent):
    n_dp = lax.axis_size("dp")
    more = n_dp // 2
    dp, hid, z = lax.axis_index("dp"), lax.axis_index("hid"), lax.axis_index("mod")
    core = dp % 2
    place = 4 * core + hid
    if more > 1:
        def mine_of(v, dim):
            whole = lax.all_gather(v, ("dp", "hid"), axis=dim, tiled=True)
            size = whole.shape[dim] // 8
            return lax.dynamic_slice_in_dim(whole, place * size, size, dim)

        project_in, project_out = mine_of(project_in, 1), mine_of(project_out, 1)
        expand, contract = mine_of(expand, 1), mine_of(contract, 0)
        expand_bias = mine_of(expand_bias, 0)

    where = jnp.stack([core, hid, z]).astype(jnp.int32)
    fpart, apart = (FPIECE, WIDE), (APIECE, WIDE)
    del ORDER[:]
    block, pair = ((HALF, WIDE), bf16), ((2, HALF, WIDE), bf16)
    wide, tall = ((ROWS, D), bf16), ((D, ROWS), bf16)
    rows32, half = ((ROWS, D), f32), ((ROWS, WIDE), bf16)
    head = ((2, ROWS, FEAT), bf16)
    four, two = ((4, APIECE, WIDE), bf16), ((2, APIECE, WIDE), bf16)
    in_shape, out_shape = (D + 16, WIDE), (D, WIDE)

    a0 = call(k_pack_attn, [(apart, bf16)], None, project_in, project_out, vectors, name="pack_attn")
    f0 = call(k_pack_ffn, [(fpart, bf16)], None, expand, contract.T, expand_bias, name="pack_ffn")
    a1, a2, a3 = z_all(a0)
    fx, fy = over_x(f0), over_y(f0)
    p1, p2, c1, c2 = call(
        k_in_each, [block] * 4, where, patches.reshape(L, 1, WIDE), cotangent.reshape(L, 1, WIDE), seen=visible, name="rows_in")
    fz = after(f0, a1, a2, a3)
    f1, f3 = z_one(fz), z_three(fz)
    f2 = z_one(f3)
    keeps, vec, slots, *gives = call(
        k_give, [((2, 2 * UNITS, WIDE), bf16), ((8, D), f32), ((2, 8, FEAT), f32)] + [((2 * UNITS, WIDE), bf16)] * 2,
        where, a0, a1, a2, a3, name="give")
    got = exchange(gives)
    got[0] = after(got[0], fx, fy)
    here = call(k_join, [((4, 2 * UNITS, WIDE), bf16)], None, keeps, *got, name="join_attn")
    from_x, from_y = over_x(here), over_y(here)
    to_x, to_y = call(k_cross, [((2, 2 * UNITS, WIDE), bf16)] * 2, None, from_x, from_y, name="cross_attn")
    diag_a, diag_b = over_x(to_x), over_y(to_y)
    p1, p2 = after((p1, p2), f1, f3, to_x)
    p1, p2 = rows_there(p1, False), rows_there(p2, True)
    c1, c2 = after((c1, c2), f1, f3)
    c1, c2 = rows_there(c1, False), rows_there(c2, True)
    d1, d2 = exchange([c1, c2])
    f123 = call(k_three, [((3,) + fpart, bf16)], None, f1, f2, after(f3, diag_a, diag_b), name="join_ffn")
    fx123, fy123 = over_x(f123), over_y(f123)
    q1, q2 = exchange([p1, p2])

    x, ain, ain_t, count = call(
        k_norm1, [wide, wide, tall, ((8, 128), f32)], where, p1, p2, q1, q2, vec, scratch=[pltpu.VMEM((ROWS, D), f32)], name="norm_attn")
    flip = (2, FEAT, ROWS)
    w, q, k, v, lse, mixed, part, *lows = call(
        k_attn, [((2, 2, D, WIDE), bf16), head, head, head, ((8, ROWS), f32), head, rows32, half, half], where,
        count, ain, here, from_x, from_y, diag_a, diag_b, slots,
        scratch=[pltpu.VMEM(flip, bf16), pltpu.VMEM(flip, bf16), pltpu.VMEM(flip, f32)], name="attend")
    oths = exchange(lows)
    resid, low, low_t, gml, gml_t = call(
        k_norm2, [rows32, wide, tall, wide, tall], where, count, x, part, *oths, vec, c1, c2, d1, d2,
        scratch=[pltpu.VMEM((ROWS, D), f32)], name="norm_mlp")

    rows = (low, low_t, gml, gml_t)
    to_x, to_y = call(k_far, [((2,) + fpart, bf16)] * 2, None, fy, fy123, fx123, name="far_ffn")
    fd_a, fd_b = over_x(to_x), over_y(to_y)
    near = [(0, None), (1, 0), (1, 1), (1, 2)]
    out, back, x_in, x_out = ffn(where, rows, (fx, fx123), near, None)
    sxa = over_x(x_in)
    out, back, y_in, y_out = ffn(where, rows, (fy, fy123), near, (out, back))
    sya = over_y(y_out)
    out, back, own_in, own_out = ffn(where, rows, (f0, f123), near, (out, back))
    keep, give, back, low_l, low_r, d_in, d_out = ffn(
        where, rows, (fd_a, fd_b), [(0, 0), (0, 1), (1, 0), (1, 1)], (out, back), last=True)
    oths = exchange([low_l, low_r])
    rx, ry = over_x(d_in), over_y(d_out)

    gres, branch, vrows = call(k_back, [rows32, wide, ((8, D), f32)], where, resid, back, *oths, gml, vec, name="norm_mlp_back")
    side, acc = pltpu.VMEM((FEAT, ROWS), bf16), pltpu.VMEM((ROWS, FEAT), f32)
    work = [side, side, side, pltpu.VMEM((FEAT, ROWS), f32), acc, acc]
    one, thin = ((ROWS, WIDE), bf16), ((ROWS, FEAT), bf16)
    kept = (count, branch, w, q, k, v, lse, mixed)
    gqk0, gv0, part = call(k_back0, [one, thin, rows32], where, *kept, scratch=work, name="attend_back")
    gqk1, gv1, part, *lows = call(k_back1, [one, thin, rows32, half, half], where, *kept, part, scratch=work, name="attend_back")
    oths = exchange(lows)
    got_out = over_core(after(give, lows[0]))
    near_in = call(k_plus, [(in_shape, f32)], None, own_in, sxa, name="sum_x")
    near_out = call(k_plus, [(out_shape, f32)], None, own_out, sya, name="sum_y")
    ga_own, ga_x, ga_y, ga_d1, ga_d2, r1, r2 = call(
        k_front, [four, four, four, two, two, pair, pair], where, count, resid, keep, got_out, part, *oths, x, vec, gres, branch,
        gqk0, gqk1, gv0, gv1, mixed, ain_t, vrows, scratch=[pltpu.VMEM((8, D), f32), pltpu.VMEM((2, D, WIDE), bf16)], name="norm_attn_back")

    ax, ay = over_x(ga_d1), over_y(ga_d2)
    xb = call(k_plus, [(out_shape, bf16)], None, x_out, ry, name="add_x")
    yb = call(k_plus, [(in_shape, bf16)], None, y_in, rx, name="add_y")
    sxb, syb = over_x(xb), over_y(yb)
    px, py = call(k_aadd, [four, four], None, ga_x, ay, ga_y, ax, name="attn_add")
    tx, ty = over_x(px), over_y(py)
    r1, r2 = rows_back(r1, False), rows_back(after(r2, px), True)
    result, grad_input = call(k_home_both, [((L, 1, WIDE), bf16), ((L, 1, WIDE), f32)], where, r1, r2, name="rows_out")
    result, grad_input = result.reshape(1, L * WIDE), grad_input.reshape(1, L * WIDE)
    fk, s1, s2, s3 = call(k_fsum, [(fpart, f32)] + [(fpart, bf16)] * 3, where, near_in, near_out, sxb, syb, name="ffn_sum")
    g2, g1 = z_one(s2), z_one(s1)
    g3 = z_three(call(k_zadd, [(fpart, bf16)], None, s3, g2, name="ffn_zadd"))
    ak, *gives = call(k_asum, [((2,) + apart, f32), (apart, bf16), (apart, bf16)], None, ga_own, tx, ty, name="attn_sum")
    got = exchange(gives)
    cut = ((APIECE // 2, WIDE), bf16)
    s0, s1, s3, *s2 = call(k_asel, [(apart, f32), (apart, bf16), (apart, bf16), cut, cut], where, ak, *got, name="attn_slots")
    t2, t1 = [z_one(s) for s in s2], z_one(s1)
    expand_grad, contract_grad, bias_grad = call(
        k_ffin, [((FEAT, WIDE), f32), ((FEAT, WIDE), f32), ((WIDE,), f32)], None, fk, g1, g3, name="ffn_last")
    t3 = z_three(call(k_zadd, [(apart, bf16)], None, s3, *t2, name="attn_zadd"))
    in_grad, out_grad, vector_grad = call(
        k_afin, [((3, UNITS, FEAT), f32), ((FEAT, UNITS), f32), ((8, FEAT), f32)], None, s0, t1, t3, name="attn_last")
    contract_grad = contract_grad.T

    if more > 1:
        def spread(v, dim):
            whole = jnp.zeros(v.shape[:dim] + (8 * v.shape[dim],) + v.shape[dim + 1 :], f32)
            whole = lax.dynamic_update_slice_in_dim(whole, v, place * v.shape[dim], dim)
            return lax.psum_scatter(whole, ("dp", "hid"), scatter_dimension=dim, tiled=True)

        in_grad, out_grad = spread(in_grad, 1), spread(out_grad, 1)
        expand_grad, contract_grad, bias_grad = spread(expand_grad, 1), spread(contract_grad, 0), spread(bias_grad, 0)
        vector_grad = lax.psum(vector_grad, "dp") / 2
    return result, grad_input, in_grad, out_grad, expand_grad, contract_grad, bias_grad, vector_grad


def solution(mesh):
    rows = P("mod", ("dp", "hid"))
    in_specs = (rows, P(("dp", "hid")), P(None, ("dp", "hid"), "mod"), rows, rows, P(("dp", "hid"), "mod"),
                P(("dp", "hid")), P(None, "mod"), rows)
    out_specs = (rows, rows, P(None, ("dp", "hid"), "mod"), rows, rows, P(("dp", "hid"), "mod"),
                 P(("dp", "hid")), P(None, "mod"))
    return jax.shard_map(body, mesh=mesh, in_specs=in_specs, out_specs=out_specs, check_vma=False)
```

```python
import jax
import jax.numpy as jnp
from jax import lax
from jax.experimental import pallas as pl
from jax.experimental.pallas import tpu as pltpu
from jax.sharding import PartitionSpec as P

D = 768
HEAD_DIM = 64
L = 529
FEAT = 192
HALF = 265
PAD = 272
ROWS = 2 * PAD
WIDE = 2 * FEAT
UNITS = D // 8
APIECE = 2 * UNITS + 16
FPIECE = 2 * FEAT + 16
eps = 1e-06
bf16 = jnp.bfloat16
f32 = jnp.float32

X = [(0, 1), (1, 0), (2, 3), (3, 2)]
Y = [(0, 2), (2, 0), (1, 3), (3, 1)]


def dot(a, b, ca=1, cb=0):
    return lax.dot_general(a, b, (((ca,), (cb,)), ((), ())), preferred_element_type=f32)


def over_x(v):
    return lax.ppermute(v, "hid", X)


def over_y(v):
    return lax.ppermute(v, "hid", Y)


def over_core(v):
    n = lax.axis_size("dp")
    return lax.ppermute(v, "dp", [(i, i ^ 1) for i in range(n)])


def z_pairs(v, pairs):
    return lax.ppermute(v, "mod", pairs)


def z_one(v):
    return z_pairs(v, [(0, 1), (1, 0), (2, 3), (3, 2)])


def z_three(v):
    return z_pairs(v, [(0, 3), (3, 0), (1, 2), (2, 1)])


def z_two(v):
    return z_pairs(v, [(0, 2), (2, 0), (1, 3), (3, 1)])


def z_all(v):
    return z_one(v), z_two(v), z_three(v)


def exchange(parts):
    return [over_core(p) for p in parts]


def after(v, *deps):
    return lax.optimization_barrier((v,) + deps)[0]


def row_pairs(second, back):
    pairs = []
    for dp in range(lax.axis_size("dp")):
        for z in range(4):
            core = dp % 2
            parity = 1 - z % 2 if second else z % 2
            src, dst = dp * 4 + z, (dp - core + z // 2) * 4 + 2 * core + parity
            pairs.append((dst, src) if back else (src, dst))
    return pairs


def rows_there(v, second):
    return lax.ppermute(v, ("dp", "mod"), row_pairs(second, False))


def rows_back(v, second):
    return lax.ppermute(v, ("dp", "mod"), row_pairs(second, True))


VM = pl.BlockSpec(memory_space=pltpu.VMEM)
SM = pl.BlockSpec(memory_space=pltpu.SMEM)


ORDER = []


def call(kernel, outs, scal, *args, seen=None, limit=20, scratch=(), name=None):
    if ORDER:
        if scal is None:
            args = (after(args[0], ORDER[-1]),) + args[1:]
        else:
            scal = after(scal, ORDER[-1])
    outs = [jax.ShapeDtypeStruct(s, t) for s, t in outs]
    single = len(outs) == 1
    ins = [VM] * len(args)
    for extra in (seen, scal):
        if extra is not None:
            ins, args = [SM] + ins, (extra,) + args
    result = pl.pallas_call(
        kernel,
        out_shape=outs[0] if single else outs,
        in_specs=ins,
        out_specs=VM if single else [VM] * len(outs),
        scratch_shapes=list(scratch),
        cost_estimate=pl.CostEstimate(flops=0, bytes_accessed=500000, transcendentals=0),
        compiler_params=pltpu.CompilerParams(vmem_limit_bytes=limit * 2**20),
        name=name,
    )(*args)
    ORDER.append(result if single else result[0])
    return result


def k_pack_attn(pin, pout, vec, attn):
    u = UNITS
    attn[0:u, 0:FEAT] = pin[0]
    attn[0:u, FEAT:WIDE] = pin[1]
    attn[u : 2 * u, 0:FEAT] = pin[2]
    attn[u : 2 * u, FEAT:WIDE] = pout[...].astype(f32).T.astype(bf16)
    v = vec[...]
    hi = v.astype(bf16)
    lo = (v - hi.astype(f32)).astype(bf16)
    both = jnp.concatenate([hi.astype(f32), lo.astype(f32)], 1)
    attn[2 * u : APIECE, :] = jnp.concatenate([both, jnp.zeros_like(both)], 0).astype(bf16)


def k_pack_ffn(ex, con_t, bias, ffn):
    ffn[0:FEAT, :] = ex[...]
    ffn[FEAT:WIDE, :] = con_t[...]
    ffn[WIDE:FPIECE, :] = jnp.broadcast_to(bias[...].astype(f32)[None], (16, WIDE)).astype(bf16)


def count_row(count):
    lane = lax.broadcasted_iota(jnp.int32, (1, FEAT), 1)
    value = jnp.where(lane == 0, count // 32, jnp.where(lane == 1, count % 32, 0))
    return value.astype(f32).astype(bf16)


def k_in(scal, seen, src, out1, out2):
    even = scal[2] % 2 == 0

    def fill(a, b):
        a[0:HALF, :] = src[0:HALF, 0, :]
        b[0:HALF, :] = src[HALF - 1 : L, 0, :]
        a[HALF - 1 : HALF, FEAT:WIDE] = count_row(seen[0])
        b[0:1, 0:FEAT] = count_row(seen[1])

    @pl.when(even)
    def _():
        fill(out1, out2)

    @pl.when(jnp.logical_not(even))
    def _():
        fill(out2, out1)


def k_in_each(scal, seen, p, c, p1, p2, c1, c2):
    k_in(scal, seen, p, p1, p2)
    k_in(scal, seen, c, c1, c2)


def row_ids(parity, shape, dim):
    place = lax.broadcasted_iota(jnp.int32, shape, dim)
    right = place >= PAD
    slot = jnp.where(right, place - PAD, place)
    ids = 2 * slot - parity + jnp.where(right, 1, 0)
    real = (slot < HALF) & (ids >= 0) & (ids < L)
    return real, ids


def kept_rows(scal, count):
    real, ids = row_ids(scal[2] % 2, (ROWS, 1), 0)
    return real & (ids.astype(f32) < count[0:1, 0:1])


def assemble(scal, own1, own2, oth1, oth2, out):
    core, even = scal[0], scal[2] % 2 == 0
    a, b, c, d = (r[...].astype(f32) for r in (own1, own2, oth1, oth2))
    own = jnp.where(even, a, b), jnp.where(even, b, a)
    oth = jnp.where(even, c, d), jnp.where(even, d, c)
    first = core == 0
    for q in range(4):
        mine, theirs = (own, oth) if q < 2 else (oth, own)
        v = jnp.where(first, mine[q % 2], theirs[q % 2])
        out[0:HALF, q * FEAT : (q + 1) * FEAT] = v[:, :FEAT]
        out[PAD : PAD + HALF, q * FEAT : (q + 1) * FEAT] = v[:, FEAT:]


def norm(v, gain, shift):
    moved = v - jnp.mean(v, 1, keepdims=True)
    inverse = lax.rsqrt(jnp.mean(moved * moved, 1, keepdims=True) + eps)
    normed = moved * inverse
    return normed, inverse, normed * gain + shift


def norm_back(grad, normed, inverse, gain):
    t = grad * gain
    return inverse * (t - jnp.mean(t, 1, keepdims=True) - normed * jnp.mean(t * normed, 1, keepdims=True))


def vec_block(refs, k):
    v = refs[0][2 * UNITS : APIECE, :].astype(f32)
    for i in (1, 2, 3):
        v = jnp.where(k == i, refs[i][2 * UNITS : APIECE, :].astype(f32), v)
    return v[0:8, :FEAT] + v[0:8, FEAT:]


def k_give(scal, a0, a1, a2, a3, keeps, vec, slots, give0, give1):
    core, z = scal[0], scal[2]
    refs = (a0, a1, a2, a3)
    for j, (lo, hi) in enumerate(((a0, a2), (a1, a3))):
        u, v = lo[0 : 2 * UNITS, :], hi[0 : 2 * UNITS, :]
        keeps[j] = jnp.where(core == 0, u, v)
        (give0, give1)[j][...] = jnp.where(core == 0, v, u)
    for q in range(4):
        vec[:, q * FEAT : (q + 1) * FEAT] = vec_block(refs, z ^ q)
    for j in range(2):
        slots[j] = vec_block(refs, 2 * core + j)


def k_join(keeps, got0, got1, out):
    out[0:2] = keeps[...]
    out[2] = got0[...]
    out[3] = got1[...]


def k_cross(from_x, from_y, to_x, to_y):
    to_x[...] = from_y[0:2]
    to_y[...] = from_x[2:4]


def k_three(a, b, c, out):
    for i, v in enumerate((a, b, c)):
        out[i] = v[...]


def k_far(y0, y123, x123, to_x, to_y):
    to_x[0] = y0[...]
    to_x[1] = y123[0]
    to_y[...] = x123[1:3]


def k_norm1(scal, own1, own2, oth1, oth2, vec, x, ain, ain_t, count, buf):
    assemble(scal, own1, own2, oth1, oth2, buf)
    a, b = own1[HALF - 1 : HALF, FEAT : FEAT + 128].astype(f32), own1[0:1, 0:128].astype(f32)
    v = jnp.where(scal[2] % 2 == 0, a, b)
    lane = lax.broadcasted_iota(jnp.int32, (1, 128), 1)
    v = jnp.sum(v * jnp.where(lane == 0, 32.0, jnp.where(lane == 1, 1.0, 0.0)), 1, keepdims=True)
    count[...] = jnp.broadcast_to(v, (8, 128))
    real, _ = row_ids(scal[2] % 2, (ROWS, 1), 0)
    v = jnp.where(real, buf[...], 0.0)
    x[...] = v.astype(bf16)
    low = norm(v, vec[0:1, :], vec[1:2, :])[2].astype(bf16)
    ain[...] = low
    ain_t[...] = low.T


def k_attn(scal, count, ain, here, fx, fy, da, db, slots, w, q, k, v, lse, mixed, part, *rest):
    *lows, qt, vt, mt = rest
    core, hid = scal[0], scal[1]
    for i in range(4):
        for p in range(2):
            for j in range(2):
                src = (da, db)[p][j] if i == 3 else (here, fx, fy)[i][2 * p + j]
                at = pl.multiple_of((4 * (core ^ p) + (hid ^ i)) * UNITS, 32)
                w[j, 0, pl.ds(at, UNITS), :] = src[0:UNITS]
                w[j, 1, pl.ds(at, UNITS), :] = src[UNITS : 2 * UNITS]
    keep = kept_rows(scal, count)
    lane = lax.broadcasted_iota(jnp.int32, (1, FEAT), 1) // HEAD_DIM
    for j in range(2):
        qk = dot(ain[...], w[j, 0])
        qj = (qk[:, :FEAT] + slots[j, 2:3, :]).astype(bf16) * jnp.asarray(0.125, bf16)
        q[j] = qj
        qt[j] = qj.T
        k[j] = qk[:, FEAT:].astype(bf16)
        vj = (dot(ain[...], w[j, 1, :, 0:FEAT]) + slots[j, 3:4, :]).astype(bf16)
        v[j] = vj
        vt[j] = vj.T
    lse[...] = jnp.zeros_like(lse)
    for j in range(2):
        for h in range(3):
            kh = jnp.where(lane == h, k[j], jnp.zeros((), bf16))
            logits = jnp.where(keep, dot(kh, qt[j]), -1e30)
            top = jnp.max(logits, 0, keepdims=True)
            expo = jnp.exp(logits - top)
            total = jnp.sum(expo, 0, keepdims=True)
            chance = (expo * (1.0 / total)).astype(bf16)
            rows = slice(h * HEAD_DIM, (h + 1) * HEAD_DIM)
            mt[j, rows, :] = dot(vt[j, rows, :], chance)
            lse[3 * j + h : 3 * j + h + 1, :] = top + jnp.log(total)
    total = 0.0
    for j in range(2):
        mj = mt[j].T.astype(bf16)
        mixed[j] = mj
        total += dot(mj, w[j, 1, :, FEAT:WIDE], 1, 1)
    part[...] = total
    put_sides(total, lows)


def sides(left, right):
    return jnp.concatenate([left[...], right[...]], 1).astype(f32)


def put_sides(total, parts):
    parts[0][...] = total[:, :WIDE].astype(bf16)
    parts[1][...] = total[:, WIDE:].astype(bf16)


def k_norm2(scal, count, x, part, oth_l, oth_r, vec, c1, c2, d1, d2, resid, low, low_t, grad, grad_t, buf):
    r = x[...].astype(f32) + part[...] + sides(oth_l, oth_r) + vec[4:5, :]
    resid[...] = r
    v = norm(r, vec[5:6, :], vec[6:7, :])[2].astype(bf16)
    low[...] = v
    low_t[...] = v.T
    assemble(scal, c1, c2, d1, d2, buf)
    g = jnp.where(kept_rows(scal, count), buf[...], 0.0).astype(bf16)
    grad[...] = g
    grad_t[...] = g.T


def gelu_both(v):
    half = 0.5 * (1.0 + lax.erf(v * 0.7071067811865476))
    slope = half + v * jnp.exp(-0.5 * v * v) * 0.3989422804014327
    return v * half, slope


def ffn_kernel(parts, first, last):
    n = len({r for r, _ in parts})

    def kernel(scal, *refs):
        low, low_t, grad, grad_t = refs[:4]
        pieces, refs = refs[4 : 4 + n], refs[4 + n :]
        if not first:
            old_out, old_back, *refs = refs
        if last:
            keep, give, back, *refs = refs
            lows, refs = refs[:2], refs[2:]
        else:
            out, back, *refs = refs
        g_in, g_out, ein, cout = refs
        for s, (r, i) in enumerate(parts):
            src = pieces[r] if i is None else pieces[r].at[i]
            place = pl.ds(pl.multiple_of((scal[2] ^ s) * FEAT, FEAT), FEAT)
            ein[place, :] = src[0:FEAT, :]
            cout[place, :] = src[FEAT:WIDE, :]
            if s == 0:
                bias = src[WIDE:FPIECE, :].astype(f32)[0:1]
        act, slope = gelu_both(dot(low[...], ein[...]) + bias)
        hidden = act.astype(bf16)
        g = (dot(grad[...], cout[...]) * slope).astype(bf16)
        res = dot(hidden, cout[...], 1, 1)
        if not first:
            res = res + old_out[...]
        if last:
            core = scal[0] == 0
            a, b = res[:, :WIDE], res[:, WIDE:]
            keep[...] = jnp.where(core, a, b)
            give[...] = jnp.where(core, b, a).astype(bf16)
        else:
            out[...] = res
        res = dot(g, ein[...], 1, 1)
        if not first:
            res = res + old_back[...]
        back[...] = res
        if last:
            put_sides(res, lows)
        g_in[0:D, :] = dot(low_t[...], g).astype(bf16)
        sums = jnp.sum(g.astype(f32), 0, keepdims=True)
        g_in[D : D + 16, :] = jnp.broadcast_to(sums, (16, WIDE)).astype(bf16)
        g_out[...] = dot(grad_t[...], hidden).astype(bf16)

    return kernel


def ffn(scal, rows, pieces, parts, acc, last=False):
    if last:
        outs = [((ROWS, WIDE), f32), ((ROWS, WIDE), bf16), ((ROWS, D), f32)] + [((ROWS, WIDE), bf16)] * 2
    else:
        outs = [((ROWS, D), f32), ((ROWS, D), f32)]
    outs += [((D + 16, WIDE), bf16), ((D, WIDE), bf16)]
    return call(ffn_kernel(parts, acc is None, last), outs, scal, *rows, *pieces, *(acc or ()),
                scratch=[pltpu.VMEM((D, WIDE), bf16)] * 2, name="ffn")


def place_rows(scal, v, out1, out2):
    even = scal[2] % 2 == 0
    q = []
    for i in range(2):
        part = v[:, i * FEAT : (i + 1) * FEAT]
        q.append(jnp.concatenate([part[0:HALF], part[PAD : PAD + HALF]], 1))
    out1[...] = jnp.where(even, q[0], q[1]).astype(bf16)
    out2[...] = jnp.where(even, q[1], q[0]).astype(bf16)


def k_back(scal, resid, back, oth_l, oth_r, gml, vec, gres, branch, vrows):
    gnm = back[...] + sides(oth_l, oth_r)
    normed, inverse, _ = norm(resid[...], vec[5:6, :], vec[6:7, :])
    g = gml[...].astype(f32)
    res = g + norm_back(gnm, normed, inverse, vec[5:6, :])
    gres[...] = res
    low = res.astype(bf16)
    branch[...] = low
    vrows[...] = jnp.zeros_like(vrows)
    vrows[4:5, :] = jnp.sum(low.astype(f32), 0, keepdims=True)
    vrows[5:6, :] = jnp.sum(gnm * normed, 0, keepdims=True)
    vrows[6:7, :] = jnp.sum(gnm, 0, keepdims=True)
    vrows[7:8, :] = jnp.sum(g, 0, keepdims=True)


def heads_back(j, scal, count, branch, w, q, k, v, lse, mixed, old, gqk, gv, part, lows, gmt, kt, qt, dqt):
    keep = kept_rows(scal, count)
    lane = lax.broadcasted_iota(jnp.int32, (1, FEAT), 1) // HEAD_DIM
    none = jnp.zeros((), bf16)
    gm_low = dot(branch[...], w[j, 1, :, FEAT:WIDE]).astype(bf16)
    gmt[...] = gm_low.T
    kt[...] = k[j].T
    qt[...] = q[j].T
    prod_t = (gm_low.astype(f32) * mixed[j].astype(f32)).T
    dks, dvs = [], []
    for h in range(3):
        rows = slice(h * HEAD_DIM, (h + 1) * HEAD_DIM)
        delta = jnp.sum(prod_t[rows, :], 0, keepdims=True)
        logits = jnp.where(keep, dot(jnp.where(lane == h, k[j], none), qt[...]), -1e30)
        chance = jnp.exp(logits - lse[3 * j + h : 3 * j + h + 1, :])
        gchance = dot(jnp.where(lane == h, v[j], none), gmt[...])
        gl = (chance * (gchance - delta)).astype(bf16)
        dvs.append(dot(chance.astype(bf16), gm_low[:, rows]))
        dks.append(dot(gl, q[j][:, rows]))
        dqt[rows, :] = dot(kt[rows, :], gl) * 0.125
    gq = dqt[...].T
    both = jnp.concatenate([gq] + dks, 1).astype(bf16)
    gqk[...] = both
    val = jnp.concatenate(dvs, 1).astype(bf16)
    gv[...] = val
    total = dot(both, w[j, 0], 1, 1) + dot(val, w[j, 1, :, 0:FEAT], 1, 1)
    if old is not None:
        total = total + old[...]
        put_sides(total, lows)
    part[...] = total


def k_back0(scal, count, branch, w, q, k, v, lse, mixed, gqk, gv, part, *scratch):
    heads_back(0, scal, count, branch, w, q, k, v, lse, mixed, None, gqk, gv, part, None, *scratch)


def k_back1(scal, count, branch, w, q, k, v, lse, mixed, old, gqk, gv, part, *refs):
    heads_back(1, scal, count, branch, w, q, k, v, lse, mixed, old, gqk, gv, part, refs[:2], *refs[2:])


def rows_result(scal, count, resid, keep, got, vec, out1, out2):
    first = scal[0] == 0
    r = jnp.where(first, resid[:, 0:WIDE], resid[:, WIDE:D])
    b = jnp.where(first, vec[7:8, 0:WIDE], vec[7:8, WIDE:D])
    r = r + keep[...] + got[...].astype(f32) + b
    place_rows(scal, jnp.where(kept_rows(scal, count), r, 0.0), out1, out2)


def k_front(scal, count, resid, keep, got, part, oth_l, oth_r, x, vec, gres, branch, gqk0, gqk1, gv0, gv1, mixed, ain_t, vrows,
            own, gx, gy, gd1, gd2, out1, out2, vfull, wbuf):
    core, hid, z = scal[0], scal[1], scal[2]
    gna = part[...] + sides(oth_l, oth_r)
    normed, inverse, _ = norm(x[...].astype(f32), vec[0:1, :], vec[1:2, :])
    res = gres[...] + norm_back(gna, normed, inverse, vec[0:1, :])
    first = core == 0
    rows_result(scal, count, resid, keep, got, vec, out1.at[0], out2.at[0])
    place_rows(scal, jnp.where(first, res[:, 0:WIDE], res[:, WIDE:D]), out1.at[1], out2.at[1])
    vfull[...] = vrows[...]
    vfull[0:1, :] = jnp.sum(gna * normed, 0, keepdims=True)
    vfull[1:2, :] = jnp.sum(gna, 0, keepdims=True)
    branch_t = branch[...].T
    dest = lambda i, p, j: ((own, gx, gy)[i].at[2 * p + j] if i < 3 else (gd1, gd2)[p].at[j])
    for j in range(2):
        gqk, gv = ((gqk0, gv0), (gqk1, gv1))[j]
        wbuf[0] = dot(ain_t[...], gqk[...]).astype(bf16)
        wbuf[1, :, 0:FEAT] = dot(ain_t[...], gv[...]).astype(bf16)
        wbuf[1, :, FEAT:WIDE] = dot(branch_t, mixed[j]).astype(bf16)
        src = z ^ (2 * core + j)
        mine = vfull[:, 0:FEAT]
        for i in (1, 2, 3):
            mine = jnp.where(src == i, vfull[:, i * FEAT : (i + 1) * FEAT], mine)
        line = lax.broadcasted_iota(jnp.int32, (8, 1), 0)
        cols_q = jnp.sum(gqk[...].astype(f32), 0, keepdims=True)[:, 0:FEAT]
        cols_v = jnp.sum(gv[...].astype(f32), 0, keepdims=True)
        mine = jnp.where(line == 2, cols_q, jnp.where(line == 3, cols_v, mine))
        mine = jnp.concatenate([mine, jnp.zeros_like(mine)], 1)
        mine = jnp.concatenate([mine, jnp.zeros_like(mine)], 0).astype(bf16)
        for i in range(4):
            for p in range(2):
                at = pl.multiple_of((4 * (core ^ p) + (hid ^ i)) * UNITS, 32)
                to = dest(i, p, j)
                to[0:UNITS, :] = wbuf[0, pl.ds(at, UNITS), :]
                to[UNITS : 2 * UNITS, :] = wbuf[1, pl.ds(at, UNITS), :]
                to[2 * UNITS : APIECE, :] = mine


def plus(a, b):
    return a.astype(f32) + b.astype(f32)


def k_plus(a, b, out):
    out[...] = plus(a[...], b[...]).astype(out.dtype)


def k_fsum(scal, near_in, near_out, xb, yb, keep, s1, s2, s3):
    z = scal[2]
    for k, to in enumerate((keep, s1, s2, s3)):
        rows = pl.ds(pl.multiple_of((z ^ k) * FEAT, FEAT), FEAT)
        tail = slice(D, D + 16)
        to[0:FEAT, :] = (near_in[rows, :] + yb[rows, :].astype(f32)).astype(to.dtype)
        to[FEAT:WIDE, :] = (near_out[rows, :] + xb[rows, :].astype(f32)).astype(to.dtype)
        to[WIDE:FPIECE, :] = (near_in[tail, :] + yb[tail, :].astype(f32)).astype(to.dtype)


def k_zadd(s3, *refs):
    *r2, t3 = refs
    n = s3.shape[0] // len(r2)
    for i, r in enumerate(r2):
        rows = slice(i * n, (i + 1) * n)
        t3[rows, :] = plus(s3[rows, :], r[...]).astype(bf16)


def k_ffin(keep, r1, r3, ex, con_t, bias):
    v = keep[...] + r1[...].astype(f32) + r3[...].astype(f32)
    ex[...] = v[0:FEAT]
    con_t[...] = v[FEAT:WIDE]
    bias[...] = v[WIDE]


def k_aadd(gx, ry, gy, rx, px, py):
    px[0:2] = gx[0:2]
    px[2:4] = plus(gx[2:4], ry[...]).astype(bf16)
    py[0:2] = plus(gy[0:2], rx[...]).astype(bf16)
    py[2:4] = gy[2:4]


def k_asum(own, sx, sy, keep, give0, give1):
    keep[...] = plus(own[0:2], sx[0:2]) + sy[0:2].astype(f32)
    give = (plus(own[2:4], sx[2:4]) + sy[2:4].astype(f32)).astype(bf16)
    give0[...] = give[0]
    give1[...] = give[1]


def k_asel(scal, keep, got0, got1, s0, s1, s3, s2a, s2b):
    first = scal[0] == 0
    a, b = keep[0], got0[...].astype(f32)
    s0[...] = jnp.where(first, a, b)
    hi = jnp.where(first, b, a).astype(bf16)
    n = APIECE // 2
    s2a[...] = hi[0:n]
    s2b[...] = hi[n:APIECE]
    a, b = keep[1], got1[...].astype(f32)
    s1[...] = jnp.where(first, a, b).astype(bf16)
    s3[...] = jnp.where(first, b, a).astype(bf16)


def k_afin(s0, r1, r3, pin, pout, vec):
    v = s0[...] + r1[...].astype(f32) + r3[...].astype(f32)
    pin[0] = v[0:UNITS, 0:FEAT]
    pin[1] = v[0:UNITS, FEAT:WIDE]
    pin[2] = v[UNITS : 2 * UNITS, 0:FEAT]
    pout[...] = v[UNITS : 2 * UNITS, FEAT:WIDE].T
    vec[...] = v[2 * UNITS : 2 * UNITS + 8, 0:FEAT]


def k_home(scal, b1, b2, to):
    even = scal[2] % 2 == 0
    left = lax.broadcasted_iota(jnp.int32, (1, WIDE), 1) < FEAT
    a, b = b1[...], b2[...]
    s0, s1 = jnp.where(even, a, b), jnp.where(even, b, a)
    t = to.dtype
    to[0 : HALF - 1, 0, :] = s0[0 : HALF - 1].astype(t)
    to[HALF - 1 : HALF, 0, :] = jnp.where(left, s0[HALF - 1 : HALF].astype(f32), s1[0:1].astype(f32)).astype(t)
    to[HALF:L, 0, :] = s1[1:HALF].astype(t)


def k_home_both(scal, b1, b2, out, grad):
    k_home(scal, b1.at[0], b2.at[0], out)
    k_home(scal, b1.at[1], b2.at[1], grad)


def body(patches, visible, project_in, project_out, expand, contract, expand_bias, vectors, cotangent):
    n_dp = lax.axis_size("dp")
    more = n_dp // 2
    dp, hid, z = lax.axis_index("dp"), lax.axis_index("hid"), lax.axis_index("mod")
    core = dp % 2
    place = 4 * core + hid
    if more > 1:
        def mine_of(v, dim):
            whole = lax.all_gather(v, ("dp", "hid"), axis=dim, tiled=True)
            size = whole.shape[dim] // 8
            return lax.dynamic_slice_in_dim(whole, place * size, size, dim)

        project_in, project_out = mine_of(project_in, 1), mine_of(project_out, 1)
        expand, contract = mine_of(expand, 1), mine_of(contract, 0)
        expand_bias = mine_of(expand_bias, 0)

    where = jnp.stack([core, hid, z]).astype(jnp.int32)
    fpart, apart = (FPIECE, WIDE), (APIECE, WIDE)
    del ORDER[:]
    block, pair = ((HALF, WIDE), bf16), ((2, HALF, WIDE), bf16)
    wide, tall = ((ROWS, D), bf16), ((D, ROWS), bf16)
    rows32, half = ((ROWS, D), f32), ((ROWS, WIDE), bf16)
    head = ((2, ROWS, FEAT), bf16)
    four, two = ((4, APIECE, WIDE), bf16), ((2, APIECE, WIDE), bf16)
    in_shape, out_shape = (D + 16, WIDE), (D, WIDE)

    a0 = call(k_pack_attn, [(apart, bf16)], None, project_in, project_out, vectors, name="pack_attn")
    f0 = call(k_pack_ffn, [(fpart, bf16)], None, expand, contract.T, expand_bias, name="pack_ffn")
    a1, a2, a3 = z_all(a0)
    fx, fy = over_x(f0), over_y(f0)
    p1, p2, c1, c2 = call(
        k_in_each, [block] * 4, where, patches.reshape(L, 1, WIDE), cotangent.reshape(L, 1, WIDE), seen=visible, name="rows_in")
    f1, f3 = z_one(f0), z_three(f0)
    f2 = z_one(f3)
    keeps, vec, slots, *gives = call(
        k_give, [((2, 2 * UNITS, WIDE), bf16), ((8, D), f32), ((2, 8, FEAT), f32)] + [((2 * UNITS, WIDE), bf16)] * 2,
        where, a0, a1, a2, a3, name="give")
    got = exchange(gives)
    got[0] = after(got[0], fx, fy)
    here = call(k_join, [((4, 2 * UNITS, WIDE), bf16)], None, keeps, *got, name="join_attn")
    from_x, from_y = over_x(here), over_y(here)
    to_x, to_y = call(k_cross, [((2, 2 * UNITS, WIDE), bf16)] * 2, None, from_x, from_y, name="cross_attn")
    diag_a, diag_b = over_x(to_x), over_y(to_y)
    p1, p2 = after((p1, p2), f1, f3, to_x)
    p1, p2 = rows_there(p1, False), rows_there(p2, True)
    c1, c2 = after((c1, c2), f1, f3)
    c1, c2 = rows_there(c1, False), rows_there(c2, True)
    d1, d2 = exchange([c1, c2])
    f123 = call(k_three, [((3,) + fpart, bf16)], None, f1, f2, after(f3, diag_a, diag_b), name="join_ffn")
    fx123, fy123 = over_x(f123), over_y(f123)
    q1, q2 = exchange([p1, p2])

    x, ain, ain_t, count = call(
        k_norm1, [wide, wide, tall, ((8, 128), f32)], where, p1, p2, q1, q2, vec, scratch=[pltpu.VMEM((ROWS, D), f32)], name="norm_attn")
    flip = (2, FEAT, ROWS)
    w, q, k, v, lse, mixed, part, *lows = call(
        k_attn, [((2, 2, D, WIDE), bf16), head, head, head, ((8, ROWS), f32), head, rows32, half, half], where,
        count, ain, here, from_x, from_y, diag_a, diag_b, slots,
        scratch=[pltpu.VMEM(flip, bf16), pltpu.VMEM(flip, bf16), pltpu.VMEM(flip, f32)], name="attend")
    oths = exchange(lows)
    resid, low, low_t, gml, gml_t = call(
        k_norm2, [rows32, wide, tall, wide, tall], where, count, x, part, *oths, vec, c1, c2, d1, d2,
        scratch=[pltpu.VMEM((ROWS, D), f32)], name="norm_mlp")

    rows = (low, low_t, gml, gml_t)
    to_x, to_y = call(k_far, [((2,) + fpart, bf16)] * 2, None, fy, fy123, fx123, name="far_ffn")
    fd_a, fd_b = over_x(to_x), over_y(to_y)
    near = [(0, None), (1, 0), (1, 1), (1, 2)]
    out, back, x_in, x_out = ffn(where, rows, (fx, fx123), near, None)
    sxa = over_x(x_in)
    out, back, y_in, y_out = ffn(where, rows, (fy, fy123), near, (out, back))
    sya = over_y(y_out)
    out, back, own_in, own_out = ffn(where, rows, (f0, f123), near, (out, back))
    keep, give, back, low_l, low_r, d_in, d_out = ffn(
        where, rows, (fd_a, fd_b), [(0, 0), (0, 1), (1, 0), (1, 1)], (out, back), last=True)
    oths = exchange([low_l, low_r])
    rx, ry = over_x(d_in), over_y(d_out)

    gres, branch, vrows = call(k_back, [rows32, wide, ((8, D), f32)], where, resid, back, *oths, gml, vec, name="norm_mlp_back")
    side = pltpu.VMEM((FEAT, ROWS), bf16)
    work = [side, side, side, pltpu.VMEM((FEAT, ROWS), f32)]
    one, thin = ((ROWS, WIDE), bf16), ((ROWS, FEAT), bf16)
    kept = (count, branch, w, q, k, v, lse, mixed)
    gqk0, gv0, part = call(k_back0, [one, thin, rows32], where, *kept, scratch=work, name="attend_back")
    gqk1, gv1, part, *lows = call(k_back1, [one, thin, rows32, half, half], where, *kept, part, scratch=work, name="attend_back")
    oths = exchange(lows)
    got_out = over_core(after(give, lows[0]))
    near_in = call(k_plus, [(in_shape, f32)], None, own_in, sxa, name="sum_x")
    near_out = call(k_plus, [(out_shape, f32)], None, own_out, sya, name="sum_y")
    ga_own, ga_x, ga_y, ga_d1, ga_d2, r1, r2 = call(
        k_front, [four, four, four, two, two, pair, pair], where, count, resid, keep, got_out, part, *oths, x, vec, gres, branch,
        gqk0, gqk1, gv0, gv1, mixed, ain_t, vrows, scratch=[pltpu.VMEM((8, D), f32), pltpu.VMEM((2, D, WIDE), bf16)], name="norm_attn_back")

    ax, ay = over_x(ga_d1), over_y(ga_d2)
    xb = call(k_plus, [(out_shape, bf16)], None, x_out, ry, name="add_x")
    yb = call(k_plus, [(in_shape, bf16)], None, y_in, rx, name="add_y")
    sxb, syb = over_x(xb), over_y(yb)
    px, py = call(k_aadd, [four, four], None, ga_x, ay, ga_y, ax, name="attn_add")
    tx, ty = over_x(px), over_y(py)
    r1, r2 = rows_back(after(r1, px), False), rows_back(r2, True)
    result, grad_input = call(k_home_both, [((L, 1, WIDE), bf16), ((L, 1, WIDE), f32)], where, r1, r2, name="rows_out")
    result, grad_input = result.reshape(1, L * WIDE), grad_input.reshape(1, L * WIDE)
    fk, s1, s2, s3 = call(k_fsum, [(fpart, f32)] + [(fpart, bf16)] * 3, where, near_in, near_out, sxb, syb, name="ffn_sum")
    g2, g1 = z_one(s2), z_one(s1)
    g3 = z_three(call(k_zadd, [(fpart, bf16)], None, s3, g2, name="ffn_zadd"))
    ak, *gives = call(k_asum, [((2,) + apart, f32), (apart, bf16), (apart, bf16)], None, ga_own, tx, ty, name="attn_sum")
    got = exchange(gives)
    cut = ((APIECE // 2, WIDE), bf16)
    s0, s1, s3, *s2 = call(k_asel, [(apart, f32), (apart, bf16), (apart, bf16), cut, cut], where, ak, *got, name="attn_slots")
    t2, t1 = [z_one(s) for s in s2], z_one(s1)
    expand_grad, contract_grad, bias_grad = call(
        k_ffin, [((FEAT, WIDE), f32), ((FEAT, WIDE), f32), ((WIDE,), f32)], None, fk, g1, g3, name="ffn_last")
    t3 = z_three(call(k_zadd, [(apart, bf16)], None, s3, *t2, name="attn_zadd"))
    in_grad, out_grad, vector_grad = call(
        k_afin, [((3, UNITS, FEAT), f32), ((FEAT, UNITS), f32), ((8, FEAT), f32)], None, s0, t1, t3, name="attn_last")
    contract_grad = contract_grad.T

    if more > 1:
        def spread(v, dim):
            whole = jnp.zeros(v.shape[:dim] + (8 * v.shape[dim],) + v.shape[dim + 1 :], f32)
            whole = lax.dynamic_update_slice_in_dim(whole, v, place * v.shape[dim], dim)
            return lax.psum_scatter(whole, ("dp", "hid"), scatter_dimension=dim, tiled=True)

        in_grad, out_grad = spread(in_grad, 1), spread(out_grad, 1)
        expand_grad, contract_grad, bias_grad = spread(expand_grad, 1), spread(contract_grad, 0), spread(bias_grad, 0)
        vector_grad = lax.psum(vector_grad, "dp") / 2
    return result, grad_input, in_grad, out_grad, expand_grad, contract_grad, bias_grad, vector_grad


def solution(mesh):
    rows = P("mod", ("dp", "hid"))
    in_specs = (rows, P(("dp", "hid")), P(None, ("dp", "hid"), "mod"), rows, rows, P(("dp", "hid"), "mod"),
                P(("dp", "hid")), P(None, "mod"), rows)
    out_specs = (rows, rows, P(None, ("dp", "hid"), "mod"), rows, rows, P(("dp", "hid"), "mod"),
                 P(("dp", "hid")), P(None, "mod"))
    return jax.shard_map(body, mesh=mesh, in_specs=in_specs, out_specs=out_specs, check_vma=False)
```

```python
import jax
import jax.numpy as jnp
from jax import lax
from jax.experimental import pallas as pl
from jax.experimental.pallas import tpu as pltpu
from jax.sharding import PartitionSpec as P

D = 768
HEAD_DIM = 64
L = 529
FEAT = 192
HALF = 265
PAD = 272
ROWS = 2 * PAD
WIDE = 2 * FEAT
UNITS = D // 8
APIECE = 2 * UNITS + 16
FPIECE = 2 * FEAT + 16
eps = 1e-06
bf16 = jnp.bfloat16
f32 = jnp.float32

X = [(0, 1), (1, 0), (2, 3), (3, 2)]
Y = [(0, 2), (2, 0), (1, 3), (3, 1)]


def dot(a, b, ca=1, cb=0):
    return lax.dot_general(a, b, (((ca,), (cb,)), ((), ())), preferred_element_type=f32)


def over_x(v):
    return lax.ppermute(v, "hid", X)


def over_y(v):
    return lax.ppermute(v, "hid", Y)


def over_core(v):
    n = lax.axis_size("dp")
    return lax.ppermute(v, "dp", [(i, i ^ 1) for i in range(n)])


def z_pairs(v, pairs):
    return lax.ppermute(v, "mod", pairs)


def z_one(v):
    return z_pairs(v, [(0, 1), (1, 0), (2, 3), (3, 2)])


def z_three(v):
    return z_pairs(v, [(0, 3), (3, 0), (1, 2), (2, 1)])


def z_two(v):
    return z_pairs(v, [(0, 2), (2, 0), (1, 3), (3, 1)])


def z_all(v):
    return z_one(v), z_two(v), z_three(v)


def exchange(parts):
    return [over_core(p) for p in parts]


def after(v, *deps):
    return lax.optimization_barrier((v,) + deps)[0]


def row_pairs(second, back):
    pairs = []
    for dp in range(lax.axis_size("dp")):
        for z in range(4):
            core = dp % 2
            parity = 1 - z % 2 if second else z % 2
            src, dst = dp * 4 + z, (dp - core + z // 2) * 4 + 2 * core + parity
            pairs.append((dst, src) if back else (src, dst))
    return pairs


def rows_there(v, second):
    return lax.ppermute(v, ("dp", "mod"), row_pairs(second, False))


def rows_back(v, second):
    return lax.ppermute(v, ("dp", "mod"), row_pairs(second, True))


VM = pl.BlockSpec(memory_space=pltpu.VMEM)
SM = pl.BlockSpec(memory_space=pltpu.SMEM)


ORDER = []


def call(kernel, outs, scal, *args, seen=None, limit=20, scratch=(), name=None):
    if ORDER:
        if scal is None:
            args = (after(args[0], ORDER[-1]),) + args[1:]
        else:
            scal = after(scal, ORDER[-1])
    outs = [jax.ShapeDtypeStruct(s, t) for s, t in outs]
    single = len(outs) == 1
    ins = [VM] * len(args)
    for extra in (seen, scal):
        if extra is not None:
            ins, args = [SM] + ins, (extra,) + args
    result = pl.pallas_call(
        kernel,
        out_shape=outs[0] if single else outs,
        in_specs=ins,
        out_specs=VM if single else [VM] * len(outs),
        scratch_shapes=list(scratch),
        cost_estimate=pl.CostEstimate(flops=0, bytes_accessed=500000, transcendentals=0),
        compiler_params=pltpu.CompilerParams(vmem_limit_bytes=limit * 2**20),
        name=name,
    )(*args)
    ORDER.append(result if single else result[0])
    return result


def k_pack_attn(pin, pout, vec, attn):
    u = UNITS
    attn[0:u, 0:FEAT] = pin[0]
    attn[0:u, FEAT:WIDE] = pin[1]
    attn[u : 2 * u, 0:FEAT] = pin[2]
    attn[u : 2 * u, FEAT:WIDE] = pout[...].astype(f32).T.astype(bf16)
    v = vec[...]
    hi = v.astype(bf16)
    lo = (v - hi.astype(f32)).astype(bf16)
    both = jnp.concatenate([hi.astype(f32), lo.astype(f32)], 1)
    attn[2 * u : APIECE, :] = jnp.concatenate([both, jnp.zeros_like(both)], 0).astype(bf16)


def k_pack_ffn(ex, con_t, bias, ffn):
    ffn[0:FEAT, :] = ex[...]
    ffn[FEAT:WIDE, :] = con_t[...]
    ffn[WIDE:FPIECE, :] = jnp.broadcast_to(bias[...].astype(f32)[None], (16, WIDE)).astype(bf16)


def count_row(count):
    lane = lax.broadcasted_iota(jnp.int32, (1, FEAT), 1)
    value = jnp.where(lane == 0, count // 32, jnp.where(lane == 1, count % 32, 0))
    return value.astype(f32).astype(bf16)


def k_in(scal, seen, src, out1, out2):
    even = scal[2] % 2 == 0

    def fill(a, b):
        a[0:HALF, :] = src[0:HALF, 0, :]
        b[0:HALF, :] = src[HALF - 1 : L, 0, :]
        a[HALF - 1 : HALF, FEAT:WIDE] = count_row(seen[0])
        b[0:1, 0:FEAT] = count_row(seen[1])

    @pl.when(even)
    def _():
        fill(out1, out2)

    @pl.when(jnp.logical_not(even))
    def _():
        fill(out2, out1)


def k_in_each(scal, seen, p, c, p1, p2, c1, c2):
    k_in(scal, seen, p, p1, p2)
    k_in(scal, seen, c, c1, c2)


def row_ids(parity, shape, dim):
    place = lax.broadcasted_iota(jnp.int32, shape, dim)
    right = place >= PAD
    slot = jnp.where(right, place - PAD, place)
    ids = 2 * slot - parity + jnp.where(right, 1, 0)
    real = (slot < HALF) & (ids >= 0) & (ids < L)
    return real, ids


def kept_rows(scal, count):
    real, ids = row_ids(scal[2] % 2, (ROWS, 1), 0)
    return real & (ids.astype(f32) < count[0:1, 0:1])


def assemble(scal, own1, own2, oth1, oth2, out):
    core, even = scal[0], scal[2] % 2 == 0
    a, b, c, d = (r[...].astype(f32) for r in (own1, own2, oth1, oth2))
    own = jnp.where(even, a, b), jnp.where(even, b, a)
    oth = jnp.where(even, c, d), jnp.where(even, d, c)
    first = core == 0
    for q in range(4):
        mine, theirs = (own, oth) if q < 2 else (oth, own)
        v = jnp.where(first, mine[q % 2], theirs[q % 2])
        out[0:HALF, q * FEAT : (q + 1) * FEAT] = v[:, :FEAT]
        out[PAD : PAD + HALF, q * FEAT : (q + 1) * FEAT] = v[:, FEAT:]


def norm(v, gain, shift):
    moved = v - jnp.mean(v, 1, keepdims=True)
    inverse = lax.rsqrt(jnp.mean(moved * moved, 1, keepdims=True) + eps)
    normed = moved * inverse
    return normed, inverse, normed * gain + shift


def norm_back(grad, normed, inverse, gain):
    t = grad * gain
    return inverse * (t - jnp.mean(t, 1, keepdims=True) - normed * jnp.mean(t * normed, 1, keepdims=True))


def vec_block(refs, k):
    v = refs[0][2 * UNITS : APIECE, :].astype(f32)
    for i in (1, 2, 3):
        v = jnp.where(k == i, refs[i][2 * UNITS : APIECE, :].astype(f32), v)
    return v[0:8, :FEAT] + v[0:8, FEAT:]


def k_give(scal, a0, a1, a2, a3, keeps, vec, slots, give0, give1):
    core, z = scal[0], scal[2]
    refs = (a0, a1, a2, a3)
    for j, (lo, hi) in enumerate(((a0, a2), (a1, a3))):
        u, v = lo[0 : 2 * UNITS, :], hi[0 : 2 * UNITS, :]
        keeps[j] = jnp.where(core == 0, u, v)
        (give0, give1)[j][...] = jnp.where(core == 0, v, u)
    for q in range(4):
        vec[:, q * FEAT : (q + 1) * FEAT] = vec_block(refs, z ^ q)
    for j in range(2):
        slots[j] = vec_block(refs, 2 * core + j)


def k_join(keeps, got0, got1, out):
    out[0:2] = keeps[...]
    out[2] = got0[...]
    out[3] = got1[...]


def k_cross(from_x, from_y, to_x, to_y):
    to_x[...] = from_y[0:2]
    to_y[...] = from_x[2:4]


def k_pair(a, b, out):
    out[0] = a[...]
    out[1] = b[...]


def k_three(a, b, c, out):
    for i, v in enumerate((a, b, c)):
        out[i] = v[...]


def k_far(y0, y123, x123, to_x, to_y):
    to_x[0] = y0[...]
    to_x[1] = y123[0]
    to_y[...] = x123[1:3]


def k_norm1(scal, own1, own2, oth1, oth2, vec, x, ain, ain_t, count, buf):
    assemble(scal, own1, own2, oth1, oth2, buf)
    a, b = own1[HALF - 1 : HALF, FEAT : FEAT + 128].astype(f32), own1[0:1, 0:128].astype(f32)
    v = jnp.where(scal[2] % 2 == 0, a, b)
    lane = lax.broadcasted_iota(jnp.int32, (1, 128), 1)
    v = jnp.sum(v * jnp.where(lane == 0, 32.0, jnp.where(lane == 1, 1.0, 0.0)), 1, keepdims=True)
    count[...] = jnp.broadcast_to(v, (8, 128))
    real, _ = row_ids(scal[2] % 2, (ROWS, 1), 0)
    v = jnp.where(real, buf[...], 0.0)
    x[...] = v.astype(bf16)
    low = norm(v, vec[0:1, :], vec[1:2, :])[2].astype(bf16)
    ain[...] = low
    ain_t[...] = low.T


def k_attn(scal, count, ain, here, fx, fy, da, db, slots, w, q, k, v, lse, mixed, part, *rest):
    *lows, qt, vt, mt = rest
    core, hid = scal[0], scal[1]
    for i in range(4):
        for p in range(2):
            for j in range(2):
                src = (da, db)[p][j] if i == 3 else (here, fx, fy)[i][2 * p + j]
                at = pl.multiple_of((4 * (core ^ p) + (hid ^ i)) * UNITS, 32)
                w[j, 0, pl.ds(at, UNITS), :] = src[0:UNITS]
                w[j, 1, pl.ds(at, UNITS), :] = src[UNITS : 2 * UNITS]
    keep = kept_rows(scal, count)
    lane = lax.broadcasted_iota(jnp.int32, (1, FEAT), 1) // HEAD_DIM
    for j in range(2):
        qk = dot(ain[...], w[j, 0])
        qj = (qk[:, :FEAT] + slots[j, 2:3, :]).astype(bf16) * jnp.asarray(0.125, bf16)
        q[j] = qj
        qt[j] = qj.T
        k[j] = qk[:, FEAT:].astype(bf16)
        vj = (dot(ain[...], w[j, 1, :, 0:FEAT]) + slots[j, 3:4, :]).astype(bf16)
        v[j] = vj
        vt[j] = vj.T
    lse[...] = jnp.zeros_like(lse)
    for j in range(2):
        for h in range(3):
            kh = jnp.where(lane == h, k[j], jnp.zeros((), bf16))
            logits = jnp.where(keep, dot(kh, qt[j]), -1e30)
            top = jnp.max(logits, 0, keepdims=True)
            expo = jnp.exp(logits - top)
            total = jnp.sum(expo, 0, keepdims=True)
            chance = (expo * (1.0 / total)).astype(bf16)
            rows = slice(h * HEAD_DIM, (h + 1) * HEAD_DIM)
            mt[j, rows, :] = dot(vt[j, rows, :], chance)
            lse[3 * j + h : 3 * j + h + 1, :] = top + jnp.log(total)
    total = 0.0
    for j in range(2):
        mj = mt[j].T.astype(bf16)
        mixed[j] = mj
        total += dot(mj, w[j, 1, :, FEAT:WIDE], 1, 1)
    part[...] = total
    put_sides(total, lows)


def sides(left, right):
    return jnp.concatenate([left[...], right[...]], 1).astype(f32)


def put_sides(total, parts):
    parts[0][...] = total[:, :WIDE].astype(bf16)
    parts[1][...] = total[:, WIDE:].astype(bf16)


def k_norm2(scal, count, x, part, oth_l, oth_r, vec, c, d, resid, low, low_t, grad, grad_t, buf):
    r = x[...].astype(f32) + part[...] + sides(oth_l, oth_r) + vec[4:5, :]
    resid[...] = r
    v = norm(r, vec[5:6, :], vec[6:7, :])[2].astype(bf16)
    low[...] = v
    low_t[...] = v.T
    assemble(scal, c.at[0], c.at[1], d.at[0], d.at[1], buf)
    g = jnp.where(kept_rows(scal, count), buf[...], 0.0).astype(bf16)
    grad[...] = g
    grad_t[...] = g.T


def gelu_both(v):
    half = 0.5 * (1.0 + lax.erf(v * 0.7071067811865476))
    slope = half + v * jnp.exp(-0.5 * v * v) * 0.3989422804014327
    return v * half, slope


def ffn_kernel(parts, first, last):
    n = len({r for r, _ in parts})

    def kernel(scal, *refs):
        low, low_t, grad, grad_t = refs[:4]
        pieces, refs = refs[4 : 4 + n], refs[4 + n :]
        if not first:
            old_out, old_back, *refs = refs
        if last:
            keep, give, back, *refs = refs
            lows, refs = refs[:2], refs[2:]
        else:
            out, back, *refs = refs
        g_in, g_out, ein, cout = refs
        for s, (r, i) in enumerate(parts):
            src = pieces[r] if i is None else pieces[r].at[i]
            place = pl.ds(pl.multiple_of((scal[2] ^ s) * FEAT, FEAT), FEAT)
            ein[place, :] = src[0:FEAT, :]
            cout[place, :] = src[FEAT:WIDE, :]
            if s == 0:
                bias = src[WIDE:FPIECE, :].astype(f32)[0:1]
        act, slope = gelu_both(dot(low[...], ein[...]) + bias)
        hidden = act.astype(bf16)
        g = (dot(grad[...], cout[...]) * slope).astype(bf16)
        res = dot(hidden, cout[...], 1, 1)
        if not first:
            res = res + old_out[...]
        if last:
            core = scal[0] == 0
            a, b = res[:, :WIDE], res[:, WIDE:]
            keep[...] = jnp.where(core, a, b)
            give[...] = jnp.where(core, b, a).astype(bf16)
        else:
            out[...] = res
        res = dot(g, ein[...], 1, 1)
        if not first:
            res = res + old_back[...]
        back[...] = res
        if last:
            put_sides(res, lows)
        g_in[0:D, :] = dot(low_t[...], g).astype(bf16)
        sums = jnp.sum(g.astype(f32), 0, keepdims=True)
        g_in[D : D + 16, :] = jnp.broadcast_to(sums, (16, WIDE)).astype(bf16)
        g_out[...] = dot(grad_t[...], hidden).astype(bf16)

    return kernel


def ffn(scal, rows, pieces, parts, acc, last=False):
    if last:
        outs = [((ROWS, WIDE), f32), ((ROWS, WIDE), bf16), ((ROWS, D), f32)] + [((ROWS, WIDE), bf16)] * 2
    else:
        outs = [((ROWS, D), f32), ((ROWS, D), f32)]
    outs += [((D + 16, WIDE), bf16), ((D, WIDE), bf16)]
    return call(ffn_kernel(parts, acc is None, last), outs, scal, *rows, *pieces, *(acc or ()),
                scratch=[pltpu.VMEM((D, WIDE), bf16)] * 2, name="ffn")


def place_rows(scal, v, out1, out2):
    even = scal[2] % 2 == 0
    q = []
    for i in range(2):
        part = v[:, i * FEAT : (i + 1) * FEAT]
        q.append(jnp.concatenate([part[0:HALF], part[PAD : PAD + HALF]], 1))
    out1[...] = jnp.where(even, q[0], q[1]).astype(bf16)
    out2[...] = jnp.where(even, q[1], q[0]).astype(bf16)


def k_back(scal, resid, back, oth_l, oth_r, gml, vec, gres, branch, vrows):
    gnm = back[...] + sides(oth_l, oth_r)
    normed, inverse, _ = norm(resid[...], vec[5:6, :], vec[6:7, :])
    g = gml[...].astype(f32)
    res = g + norm_back(gnm, normed, inverse, vec[5:6, :])
    gres[...] = res
    low = res.astype(bf16)
    branch[...] = low
    vrows[...] = jnp.zeros_like(vrows)
    vrows[4:5, :] = jnp.sum(low.astype(f32), 0, keepdims=True)
    vrows[5:6, :] = jnp.sum(gnm * normed, 0, keepdims=True)
    vrows[6:7, :] = jnp.sum(gnm, 0, keepdims=True)
    vrows[7:8, :] = jnp.sum(g, 0, keepdims=True)


def heads_back(j, scal, count, branch, w, q, k, v, lse, mixed, old, gqk, gv, part, lows, gmt, kt, qt, dqt):
    keep = kept_rows(scal, count)
    lane = lax.broadcasted_iota(jnp.int32, (1, FEAT), 1) // HEAD_DIM
    none = jnp.zeros((), bf16)
    gm_low = dot(branch[...], w[j, 1, :, FEAT:WIDE]).astype(bf16)
    gmt[...] = gm_low.T
    kt[...] = k[j].T
    qt[...] = q[j].T
    prod_t = (gm_low.astype(f32) * mixed[j].astype(f32)).T
    dks, dvs = [], []
    for h in range(3):
        rows = slice(h * HEAD_DIM, (h + 1) * HEAD_DIM)
        delta = jnp.sum(prod_t[rows, :], 0, keepdims=True)
        logits = jnp.where(keep, dot(jnp.where(lane == h, k[j], none), qt[...]), -1e30)
        chance = jnp.exp(logits - lse[3 * j + h : 3 * j + h + 1, :])
        gchance = dot(jnp.where(lane == h, v[j], none), gmt[...])
        gl = (chance * (gchance - delta)).astype(bf16)
        dvs.append(dot(chance.astype(bf16), gm_low[:, rows]))
        dks.append(dot(gl, q[j][:, rows]))
        dqt[rows, :] = dot(kt[rows, :], gl) * 0.125
    gq = dqt[...].T
    both = jnp.concatenate([gq] + dks, 1).astype(bf16)
    gqk[...] = both
    val = jnp.concatenate(dvs, 1).astype(bf16)
    gv[...] = val
    total = dot(both, w[j, 0], 1, 1) + dot(val, w[j, 1, :, 0:FEAT], 1, 1)
    if old is not None:
        total = total + old[...]
        put_sides(total, lows)
    part[...] = total


def k_back0(scal, count, branch, w, q, k, v, lse, mixed, gqk, gv, part, *scratch):
    heads_back(0, scal, count, branch, w, q, k, v, lse, mixed, None, gqk, gv, part, None, *scratch)


def k_back1(scal, count, branch, w, q, k, v, lse, mixed, old, gqk, gv, part, *refs):
    heads_back(1, scal, count, branch, w, q, k, v, lse, mixed, old, gqk, gv, part, refs[:2], *refs[2:])


def rows_result(scal, count, resid, keep, got, vec, out1, out2):
    first = scal[0] == 0
    r = jnp.where(first, resid[:, 0:WIDE], resid[:, WIDE:D])
    b = jnp.where(first, vec[7:8, 0:WIDE], vec[7:8, WIDE:D])
    r = r + keep[...] + got[...].astype(f32) + b
    place_rows(scal, jnp.where(kept_rows(scal, count), r, 0.0), out1, out2)


def k_front(scal, count, resid, keep, got, part, oth_l, oth_r, x, vec, gres, branch, gqk0, gqk1, gv0, gv1, mixed, ain_t, vrows,
            own, gx, gy, gd1, gd2, out1, out2, vfull, wbuf):
    core, hid, z = scal[0], scal[1], scal[2]
    gna = part[...] + sides(oth_l, oth_r)
    normed, inverse, _ = norm(x[...].astype(f32), vec[0:1, :], vec[1:2, :])
    res = gres[...] + norm_back(gna, normed, inverse, vec[0:1, :])
    first = core == 0
    rows_result(scal, count, resid, keep, got, vec, out1.at[0], out2.at[0])
    place_rows(scal, jnp.where(first, res[:, 0:WIDE], res[:, WIDE:D]), out1.at[1], out2.at[1])
    vfull[...] = vrows[...]
    vfull[0:1, :] = jnp.sum(gna * normed, 0, keepdims=True)
    vfull[1:2, :] = jnp.sum(gna, 0, keepdims=True)
    branch_t = branch[...].T
    dest = lambda i, p, j: ((own, gx, gy)[i].at[2 * p + j] if i < 3 else (gd1, gd2)[p].at[j])
    for j in range(2):
        gqk, gv = ((gqk0, gv0), (gqk1, gv1))[j]
        wbuf[0] = dot(ain_t[...], gqk[...]).astype(bf16)
        wbuf[1, :, 0:FEAT] = dot(ain_t[...], gv[...]).astype(bf16)
        wbuf[1, :, FEAT:WIDE] = dot(branch_t, mixed[j]).astype(bf16)
        src = z ^ (2 * core + j)
        mine = vfull[:, 0:FEAT]
        for i in (1, 2, 3):
            mine = jnp.where(src == i, vfull[:, i * FEAT : (i + 1) * FEAT], mine)
        line = lax.broadcasted_iota(jnp.int32, (8, 1), 0)
        cols_q = jnp.sum(gqk[...].astype(f32), 0, keepdims=True)[:, 0:FEAT]
        cols_v = jnp.sum(gv[...].astype(f32), 0, keepdims=True)
        mine = jnp.where(line == 2, cols_q, jnp.where(line == 3, cols_v, mine))
        mine = jnp.concatenate([mine, jnp.zeros_like(mine)], 1)
        mine = jnp.concatenate([mine, jnp.zeros_like(mine)], 0).astype(bf16)
        for i in range(4):
            for p in range(2):
                at = pl.multiple_of((4 * (core ^ p) + (hid ^ i)) * UNITS, 32)
                to = dest(i, p, j)
                to[0:UNITS, :] = wbuf[0, pl.ds(at, UNITS), :]
                to[UNITS : 2 * UNITS, :] = wbuf[1, pl.ds(at, UNITS), :]
                to[2 * UNITS : APIECE, :] = mine


def plus(a, b):
    return a.astype(f32) + b.astype(f32)


def k_plus(a, b, out):
    out[...] = plus(a[...], b[...]).astype(out.dtype)


def k_fsum(scal, near_in, near_out, xb, yb, keep, s1, s2, s3):
    z = scal[2]
    for k, to in enumerate((keep, s1, s2, s3)):
        rows = pl.ds(pl.multiple_of((z ^ k) * FEAT, FEAT), FEAT)
        tail = slice(D, D + 16)
        to[0:FEAT, :] = (near_in[rows, :] + yb[rows, :].astype(f32)).astype(to.dtype)
        to[FEAT:WIDE, :] = (near_out[rows, :] + xb[rows, :].astype(f32)).astype(to.dtype)
        to[WIDE:FPIECE, :] = (near_in[tail, :] + yb[tail, :].astype(f32)).astype(to.dtype)


def k_zadd(s3, *refs):
    *r2, t3 = refs
    n = s3.shape[0] // len(r2)
    for i, r in enumerate(r2):
        rows = slice(i * n, (i + 1) * n)
        t3[rows, :] = plus(s3[rows, :], r[...]).astype(bf16)


def k_ffin(keep, r1, r3, ex, con_t, bias):
    v = keep[...] + r1[...].astype(f32) + r3[...].astype(f32)
    ex[...] = v[0:FEAT]
    con_t[...] = v[FEAT:WIDE]
    bias[...] = v[WIDE]


def k_aadd(gx, ry, gy, rx, px, py):
    px[0:2] = gx[0:2]
    px[2:4] = plus(gx[2:4], ry[...]).astype(bf16)
    py[0:2] = plus(gy[0:2], rx[...]).astype(bf16)
    py[2:4] = gy[2:4]


def k_asum(own, sx, sy, keep, give0, give1):
    keep[...] = plus(own[0:2], sx[0:2]) + sy[0:2].astype(f32)
    give = (plus(own[2:4], sx[2:4]) + sy[2:4].astype(f32)).astype(bf16)
    give0[...] = give[0]
    give1[...] = give[1]


def k_asel(scal, keep, got0, got1, s0, s1, s3, s2a, s2b):
    first = scal[0] == 0
    a, b = keep[0], got0[...].astype(f32)
    s0[...] = jnp.where(first, a, b)
    hi = jnp.where(first, b, a).astype(bf16)
    n = APIECE // 2
    s2a[...] = hi[0:n]
    s2b[...] = hi[n:APIECE]
    a, b = keep[1], got1[...].astype(f32)
    s1[...] = jnp.where(first, a, b).astype(bf16)
    s3[...] = jnp.where(first, b, a).astype(bf16)


def k_afin(s0, r1, r3, pin, pout, vec):
    v = s0[...] + r1[...].astype(f32) + r3[...].astype(f32)
    pin[0] = v[0:UNITS, 0:FEAT]
    pin[1] = v[0:UNITS, FEAT:WIDE]
    pin[2] = v[UNITS : 2 * UNITS, 0:FEAT]
    pout[...] = v[UNITS : 2 * UNITS, FEAT:WIDE].T
    vec[...] = v[2 * UNITS : 2 * UNITS + 8, 0:FEAT]


def k_home(scal, b1, b2, to):
    even = scal[2] % 2 == 0
    left = lax.broadcasted_iota(jnp.int32, (1, WIDE), 1) < FEAT
    a, b = b1[...], b2[...]
    s0, s1 = jnp.where(even, a, b), jnp.where(even, b, a)
    t = to.dtype
    to[0 : HALF - 1, 0, :] = s0[0 : HALF - 1].astype(t)
    to[HALF - 1 : HALF, 0, :] = jnp.where(left, s0[HALF - 1 : HALF].astype(f32), s1[0:1].astype(f32)).astype(t)
    to[HALF:L, 0, :] = s1[1:HALF].astype(t)


def k_home_both(scal, b1, b2, out, grad):
    k_home(scal, b1.at[0], b2.at[0], out)
    k_home(scal, b1.at[1], b2.at[1], grad)


def body(patches, visible, project_in, project_out, expand, contract, expand_bias, vectors, cotangent):
    n_dp = lax.axis_size("dp")
    more = n_dp // 2
    dp, hid, z = lax.axis_index("dp"), lax.axis_index("hid"), lax.axis_index("mod")
    core = dp % 2
    place = 4 * core + hid
    if more > 1:
        def mine_of(v, dim):
            whole = lax.all_gather(v, ("dp", "hid"), axis=dim, tiled=True)
            size = whole.shape[dim] // 8
            return lax.dynamic_slice_in_dim(whole, place * size, size, dim)

        project_in, project_out = mine_of(project_in, 1), mine_of(project_out, 1)
        expand, contract = mine_of(expand, 1), mine_of(contract, 0)
        expand_bias = mine_of(expand_bias, 0)

    where = jnp.stack([core, hid, z]).astype(jnp.int32)
    fpart, apart = (FPIECE, WIDE), (APIECE, WIDE)
    del ORDER[:]
    block, pair = ((HALF, WIDE), bf16), ((2, HALF, WIDE), bf16)
    wide, tall = ((ROWS, D), bf16), ((D, ROWS), bf16)
    rows32, half = ((ROWS, D), f32), ((ROWS, WIDE), bf16)
    head = ((2, ROWS, FEAT), bf16)
    four, two = ((4, APIECE, WIDE), bf16), ((2, APIECE, WIDE), bf16)
    in_shape, out_shape = (D + 16, WIDE), (D, WIDE)

    a0 = call(k_pack_attn, [(apart, bf16)], None, project_in, project_out, vectors, name="pack_attn")
    f0 = call(k_pack_ffn, [(fpart, bf16)], None, expand, contract.T, expand_bias, name="pack_ffn")
    a1, a2, a3 = z_all(a0)
    fx, fy = over_x(f0), over_y(f0)
    p1, p2, c1, c2 = call(
        k_in_each, [block] * 4, where, patches.reshape(L, 1, WIDE), cotangent.reshape(L, 1, WIDE), seen=visible, name="rows_in")
    f1, f3 = z_one(f0), z_three(f0)
    f2 = z_one(f3)
    keeps, vec, slots, *gives = call(
        k_give, [((2, 2 * UNITS, WIDE), bf16), ((8, D), f32), ((2, 8, FEAT), f32)] + [((2 * UNITS, WIDE), bf16)] * 2,
        where, a0, a1, a2, a3, name="give")
    got = exchange(gives)
    got[0] = after(got[0], fx, fy)
    here = call(k_join, [((4, 2 * UNITS, WIDE), bf16)], None, keeps, *got, name="join_attn")
    from_x, from_y = over_x(here), over_y(here)
    to_x, to_y = call(k_cross, [((2, 2 * UNITS, WIDE), bf16)] * 2, None, from_x, from_y, name="cross_attn")
    diag_a, diag_b = over_x(to_x), over_y(to_y)
    p1, p2 = after((p1, p2), f1, f3, to_x)
    p1, p2 = rows_there(p1, False), rows_there(p2, True)
    c1, c2 = after((c1, c2), f1, f3)
    c1, c2 = rows_there(c1, False), rows_there(c2, True)
    f123 = call(k_three, [((3,) + fpart, bf16)], None, f1, f2, after(f3, diag_a, diag_b), name="join_ffn")
    fx123, fy123 = over_x(f123), over_y(f123)
    q1, q2 = exchange([p1, p2])

    x, ain, ain_t, count = call(
        k_norm1, [wide, wide, tall, ((8, 128), f32)], where, p1, p2, q1, q2, vec, scratch=[pltpu.VMEM((ROWS, D), f32)], name="norm_attn")
    flip = (2, FEAT, ROWS)
    w, q, k, v, lse, mixed, part, *lows = call(
        k_attn, [((2, 2, D, WIDE), bf16), head, head, head, ((8, ROWS), f32), head, rows32, half, half], where,
        count, ain, here, from_x, from_y, diag_a, diag_b, slots,
        scratch=[pltpu.VMEM(flip, bf16), pltpu.VMEM(flip, bf16), pltpu.VMEM(flip, f32)], name="attend")
    oths = exchange(lows)
    c = call(k_pair, [pair], None, c1, c2, name="join_rows")
    d = over_core(c)
    resid, low, low_t, gml, gml_t = call(
        k_norm2, [rows32, wide, tall, wide, tall], where, count, x, part, *oths, vec, c, d,
        scratch=[pltpu.VMEM((ROWS, D), f32)], name="norm_mlp")

    rows = (low, low_t, gml, gml_t)
    to_x, to_y = call(k_far, [((2,) + fpart, bf16)] * 2, None, fy, fy123, fx123, name="far_ffn")
    fd_a, fd_b = over_x(to_x), over_y(to_y)
    near = [(0, None), (1, 0), (1, 1), (1, 2)]
    out, back, x_in, x_out = ffn(where, rows, (fx, fx123), near, None)
    sxa = over_x(x_in)
    out, back, y_in, y_out = ffn(where, rows, (fy, fy123), near, (out, back))
    sya = over_y(y_out)
    out, back, own_in, own_out = ffn(where, rows, (f0, f123), near, (out, back))
    keep, give, back, low_l, low_r, d_in, d_out = ffn(
        where, rows, (fd_a, fd_b), [(0, 0), (0, 1), (1, 0), (1, 1)], (out, back), last=True)
    oths = exchange([low_l, low_r])
    rx, ry = over_x(d_in), over_y(d_out)

    gres, branch, vrows = call(k_back, [rows32, wide, ((8, D), f32)], where, resid, back, *oths, gml, vec, name="norm_mlp_back")
    side = pltpu.VMEM((FEAT, ROWS), bf16)
    work = [side, side, side, pltpu.VMEM((FEAT, ROWS), f32)]
    one, thin = ((ROWS, WIDE), bf16), ((ROWS, FEAT), bf16)
    kept = (count, branch, w, q, k, v, lse, mixed)
    gqk0, gv0, part = call(k_back0, [one, thin, rows32], where, *kept, scratch=work, name="attend_back")
    gqk1, gv1, part, *lows = call(k_back1, [one, thin, rows32, half, half], where, *kept, part, scratch=work, name="attend_back")
    oths = exchange(lows)
    got_out = over_core(after(give, lows[0]))
    near_in = call(k_plus, [(in_shape, f32)], None, own_in, sxa, name="sum_x")
    near_out = call(k_plus, [(out_shape, f32)], None, own_out, sya, name="sum_y")
    ga_own, ga_x, ga_y, ga_d1, ga_d2, r1, r2 = call(
        k_front, [four, four, four, two, two, pair, pair], where, count, resid, keep, got_out, part, *oths, x, vec, gres, branch,
        gqk0, gqk1, gv0, gv1, mixed, ain_t, vrows, scratch=[pltpu.VMEM((8, D), f32), pltpu.VMEM((2, D, WIDE), bf16)], name="norm_attn_back")

    ax, ay = over_x(ga_d1), over_y(ga_d2)
    xb = call(k_plus, [(out_shape, bf16)], None, x_out, ry, name="add_x")
    yb = call(k_plus, [(in_shape, bf16)], None, y_in, rx, name="add_y")
    sxb, syb = over_x(xb), over_y(yb)
    px, py = call(k_aadd, [four, four], None, ga_x, ay, ga_y, ax, name="attn_add")
    tx, ty = over_x(px), over_y(py)
    r1, r2 = rows_back(after(r1, px), False), rows_back(r2, True)
    result, grad_input = call(k_home_both, [((L, 1, WIDE), bf16), ((L, 1, WIDE), f32)], where, r1, r2, name="rows_out")
    result, grad_input = result.reshape(1, L * WIDE), grad_input.reshape(1, L * WIDE)
    fk, s1, s2, s3 = call(k_fsum, [(fpart, f32)] + [(fpart, bf16)] * 3, where, near_in, near_out, sxb, syb, name="ffn_sum")
    g2, g1 = z_one(s2), z_one(s1)
    g3 = z_three(call(k_zadd, [(fpart, bf16)], None, s3, g2, name="ffn_zadd"))
    ak, *gives = call(k_asum, [((2,) + apart, f32), (apart, bf16), (apart, bf16)], None, ga_own, tx, ty, name="attn_sum")
    got = exchange(gives)
    cut = ((APIECE // 2, WIDE), bf16)
    s0, s1, s3, *s2 = call(k_asel, [(apart, f32), (apart, bf16), (apart, bf16), cut, cut], where, ak, *got, name="attn_slots")
    t2, t1 = [z_one(s) for s in s2], z_one(s1)
    expand_grad, contract_grad, bias_grad = call(
        k_ffin, [((FEAT, WIDE), f32), ((FEAT, WIDE), f32), ((WIDE,), f32)], None, fk, g1, g3, name="ffn_last")
    t3 = z_three(call(k_zadd, [(apart, bf16)], None, s3, *t2, name="attn_zadd"))
    in_grad, out_grad, vector_grad = call(
        k_afin, [((3, UNITS, FEAT), f32), ((FEAT, UNITS), f32), ((8, FEAT), f32)], None, s0, t1, t3, name="attn_last")
    contract_grad = contract_grad.T

    if more > 1:
        def spread(v, dim):
            whole = jnp.zeros(v.shape[:dim] + (8 * v.shape[dim],) + v.shape[dim + 1 :], f32)
            whole = lax.dynamic_update_slice_in_dim(whole, v, place * v.shape[dim], dim)
            return lax.psum_scatter(whole, ("dp", "hid"), scatter_dimension=dim, tiled=True)

        in_grad, out_grad = spread(in_grad, 1), spread(out_grad, 1)
        expand_grad, contract_grad, bias_grad = spread(expand_grad, 1), spread(contract_grad, 0), spread(bias_grad, 0)
        vector_grad = lax.psum(vector_grad, "dp") / 2
    return result, grad_input, in_grad, out_grad, expand_grad, contract_grad, bias_grad, vector_grad


def solution(mesh):
    rows = P("mod", ("dp", "hid"))
    in_specs = (rows, P(("dp", "hid")), P(None, ("dp", "hid"), "mod"), rows, rows, P(("dp", "hid"), "mod"),
                P(("dp", "hid")), P(None, "mod"), rows)
    out_specs = (rows, rows, P(None, ("dp", "hid"), "mod"), rows, rows, P(("dp", "hid"), "mod"),
                 P(("dp", "hid")), P(None, "mod"))
    return jax.shard_map(body, mesh=mesh, in_specs=in_specs, out_specs=out_specs, check_vma=False)
```

```python
import jax
import jax.numpy as jnp
from jax import lax
from jax.experimental import pallas as pl
from jax.experimental.pallas import tpu as pltpu
from jax.sharding import PartitionSpec as P

D = 768
HEAD_DIM = 64
L = 529
FEAT = 192
HALF = 265
PAD = 272
ROWS = 2 * PAD
WIDE = 2 * FEAT
UNITS = D // 8
APIECE = 2 * UNITS + 16
FPIECE = 2 * FEAT + 16
eps = 1e-06
bf16 = jnp.bfloat16
f32 = jnp.float32

X = [(0, 1), (1, 0), (2, 3), (3, 2)]
Y = [(0, 2), (2, 0), (1, 3), (3, 1)]


def dot(a, b, ca=1, cb=0):
    return lax.dot_general(a, b, (((ca,), (cb,)), ((), ())), preferred_element_type=f32)


def over_x(v):
    return lax.ppermute(v, "hid", X)


def over_y(v):
    return lax.ppermute(v, "hid", Y)


def over_core(v):
    n = lax.axis_size("dp")
    return lax.ppermute(v, "dp", [(i, i ^ 1) for i in range(n)])


def z_pairs(v, pairs):
    return lax.ppermute(v, "mod", pairs)


def z_one(v):
    return z_pairs(v, [(0, 1), (1, 0), (2, 3), (3, 2)])


def z_three(v):
    return z_pairs(v, [(0, 3), (3, 0), (1, 2), (2, 1)])


def z_two(v):
    return z_pairs(v, [(0, 2), (2, 0), (1, 3), (3, 1)])


def z_all(v):
    return z_one(v), z_two(v), z_three(v)


def exchange(parts):
    return [over_core(p) for p in parts]


def after(v, *deps):
    return lax.optimization_barrier((v,) + deps)[0]


def row_pairs(second, back):
    pairs = []
    for dp in range(lax.axis_size("dp")):
        for z in range(4):
            core = dp % 2
            parity = 1 - z % 2 if second else z % 2
            src, dst = dp * 4 + z, (dp - core + z // 2) * 4 + 2 * core + parity
            pairs.append((dst, src) if back else (src, dst))
    return pairs


def rows_there(v, second):
    return lax.ppermute(v, ("dp", "mod"), row_pairs(second, False))


def rows_back(v, second):
    return lax.ppermute(v, ("dp", "mod"), row_pairs(second, True))


VM = pl.BlockSpec(memory_space=pltpu.VMEM)
SM = pl.BlockSpec(memory_space=pltpu.SMEM)


ORDER = []


def call(kernel, outs, scal, *args, seen=None, limit=20, scratch=(), name=None):
    if ORDER:
        if scal is None:
            args = (after(args[0], ORDER[-1]),) + args[1:]
        else:
            scal = after(scal, ORDER[-1])
    outs = [jax.ShapeDtypeStruct(s, t) for s, t in outs]
    single = len(outs) == 1
    ins = [VM] * len(args)
    for extra in (seen, scal):
        if extra is not None:
            ins, args = [SM] + ins, (extra,) + args
    result = pl.pallas_call(
        kernel,
        out_shape=outs[0] if single else outs,
        in_specs=ins,
        out_specs=VM if single else [VM] * len(outs),
        scratch_shapes=list(scratch),
        cost_estimate=pl.CostEstimate(flops=0, bytes_accessed=500000, transcendentals=0),
        compiler_params=pltpu.CompilerParams(vmem_limit_bytes=limit * 2**20),
        name=name,
    )(*args)
    ORDER.append(result if single else result[0])
    return result


def k_pack_attn(pin, pout, vec, attn):
    u = UNITS
    attn[0:u, 0:FEAT] = pin[0]
    attn[0:u, FEAT:WIDE] = pin[1]
    attn[u : 2 * u, 0:FEAT] = pin[2]
    attn[u : 2 * u, FEAT:WIDE] = pout[...].astype(f32).T.astype(bf16)
    v = vec[...]
    hi = v.astype(bf16)
    lo = (v - hi.astype(f32)).astype(bf16)
    both = jnp.concatenate([hi.astype(f32), lo.astype(f32)], 1)
    attn[2 * u : APIECE, :] = jnp.concatenate([both, jnp.zeros_like(both)], 0).astype(bf16)


def k_pack_ffn(ex, con_t, bias, ffn):
    ffn[0:FEAT, :] = ex[...]
    ffn[FEAT:WIDE, :] = con_t[...]
    ffn[WIDE:FPIECE, :] = jnp.broadcast_to(bias[...].astype(f32)[None], (16, WIDE)).astype(bf16)


def count_row(count):
    lane = lax.broadcasted_iota(jnp.int32, (1, FEAT), 1)
    value = jnp.where(lane == 0, count // 32, jnp.where(lane == 1, count % 32, 0))
    return value.astype(f32).astype(bf16)


def k_in(scal, seen, src, out1, out2):
    even = scal[2] % 2 == 0

    def fill(a, b):
        a[0:HALF, :] = src[0:HALF, 0, :]
        b[0:HALF, :] = src[HALF - 1 : L, 0, :]
        a[HALF - 1 : HALF, FEAT:WIDE] = count_row(seen[0])
        b[0:1, 0:FEAT] = count_row(seen[1])

    @pl.when(even)
    def _():
        fill(out1, out2)

    @pl.when(jnp.logical_not(even))
    def _():
        fill(out2, out1)


def k_in_each(scal, seen, p, c, p1, p2, c1, c2):
    k_in(scal, seen, p, p1, p2)
    k_in(scal, seen, c, c1, c2)


def row_ids(parity, shape, dim):
    place = lax.broadcasted_iota(jnp.int32, shape, dim)
    right = place >= PAD
    slot = jnp.where(right, place - PAD, place)
    ids = 2 * slot - parity + jnp.where(right, 1, 0)
    real = (slot < HALF) & (ids >= 0) & (ids < L)
    return real, ids


def kept_rows(scal, count):
    real, ids = row_ids(scal[2] % 2, (ROWS, 1), 0)
    return real & (ids.astype(f32) < count[0:1, 0:1])


def assemble(scal, own1, own2, oth1, oth2, out):
    core, even = scal[0], scal[2] % 2 == 0
    a, b, c, d = (r[...].astype(f32) for r in (own1, own2, oth1, oth2))
    own = jnp.where(even, a, b), jnp.where(even, b, a)
    oth = jnp.where(even, c, d), jnp.where(even, d, c)
    first = core == 0
    for q in range(4):
        mine, theirs = (own, oth) if q < 2 else (oth, own)
        v = jnp.where(first, mine[q % 2], theirs[q % 2])
        out[0:HALF, q * FEAT : (q + 1) * FEAT] = v[:, :FEAT]
        out[PAD : PAD + HALF, q * FEAT : (q + 1) * FEAT] = v[:, FEAT:]


def norm(v, gain, shift):
    moved = v - jnp.mean(v, 1, keepdims=True)
    inverse = lax.rsqrt(jnp.mean(moved * moved, 1, keepdims=True) + eps)
    normed = moved * inverse
    return normed, inverse, normed * gain + shift


def norm_back(grad, normed, inverse, gain):
    t = grad * gain
    return inverse * (t - jnp.mean(t, 1, keepdims=True) - normed * jnp.mean(t * normed, 1, keepdims=True))


def vec_block(refs, k):
    v = refs[0][2 * UNITS : APIECE, :].astype(f32)
    for i in (1, 2, 3):
        v = jnp.where(k == i, refs[i][2 * UNITS : APIECE, :].astype(f32), v)
    return v[0:8, :FEAT] + v[0:8, FEAT:]


def k_give(scal, a0, a1, a2, a3, keeps, vec, slots, give0, give1):
    core, z = scal[0], scal[2]
    refs = (a0, a1, a2, a3)
    for j, (lo, hi) in enumerate(((a0, a2), (a1, a3))):
        u, v = lo[0 : 2 * UNITS, :], hi[0 : 2 * UNITS, :]
        keeps[j] = jnp.where(core == 0, u, v)
        (give0, give1)[j][...] = jnp.where(core == 0, v, u)
    for q in range(4):
        vec[:, q * FEAT : (q + 1) * FEAT] = vec_block(refs, z ^ q)
    for j in range(2):
        slots[j] = vec_block(refs, 2 * core + j)


def k_join(keeps, got0, got1, out):
    out[0:2] = keeps[...]
    out[2] = got0[...]
    out[3] = got1[...]


def k_cross(from_x, from_y, to_x, to_y):
    to_x[...] = from_y[0:2]
    to_y[...] = from_x[2:4]


def k_pair(a, b, out):
    out[0] = a[...]
    out[1] = b[...]


def k_three(a, b, c, out):
    for i, v in enumerate((a, b, c)):
        out[i] = v[...]


def k_far(y0, y123, x123, to_x, to_y):
    to_x[0] = y0[...]
    to_x[1] = y123[0]
    to_y[...] = x123[1:3]


def k_norm1(scal, own1, own2, oth1, oth2, vec, x, ain, ain_t, count, buf):
    assemble(scal, own1, own2, oth1, oth2, buf)
    a, b = own1[HALF - 1 : HALF, FEAT : FEAT + 128].astype(f32), own1[0:1, 0:128].astype(f32)
    v = jnp.where(scal[2] % 2 == 0, a, b)
    lane = lax.broadcasted_iota(jnp.int32, (1, 128), 1)
    v = jnp.sum(v * jnp.where(lane == 0, 32.0, jnp.where(lane == 1, 1.0, 0.0)), 1, keepdims=True)
    count[...] = jnp.broadcast_to(v, (8, 128))
    real, _ = row_ids(scal[2] % 2, (ROWS, 1), 0)
    v = jnp.where(real, buf[...], 0.0)
    x[...] = v.astype(bf16)
    low = norm(v, vec[0:1, :], vec[1:2, :])[2].astype(bf16)
    ain[...] = low
    ain_t[...] = low.T


def k_attn(scal, count, ain, here, fx, fy, da, db, slots, w, q, k, v, lse, mixed, part, *rest):
    *lows, qt, vt, mt = rest
    core, hid = scal[0], scal[1]
    for i in range(4):
        for p in range(2):
            for j in range(2):
                src = (da, db)[p][j] if i == 3 else (here, fx, fy)[i][2 * p + j]
                at = pl.multiple_of((4 * (core ^ p) + (hid ^ i)) * UNITS, 32)
                w[j, 0, pl.ds(at, UNITS), :] = src[0:UNITS]
                w[j, 1, pl.ds(at, UNITS), :] = src[UNITS : 2 * UNITS]
    keep = kept_rows(scal, count)
    lane = lax.broadcasted_iota(jnp.int32, (1, FEAT), 1) // HEAD_DIM
    for j in range(2):
        qk = dot(ain[...], w[j, 0])
        qj = (qk[:, :FEAT] + slots[j, 2:3, :]).astype(bf16) * jnp.asarray(0.125, bf16)
        q[j] = qj
        qt[j] = qj.T
        k[j] = qk[:, FEAT:].astype(bf16)
        vj = (dot(ain[...], w[j, 1, :, 0:FEAT]) + slots[j, 3:4, :]).astype(bf16)
        v[j] = vj
        vt[j] = vj.T
    lse[...] = jnp.zeros_like(lse)
    for j in range(2):
        for h in range(3):
            kh = jnp.where(lane == h, k[j], jnp.zeros((), bf16))
            logits = jnp.where(keep, dot(kh, qt[j]), -1e30)
            top = jnp.max(logits, 0, keepdims=True)
            expo = jnp.exp(logits - top)
            total = jnp.sum(expo, 0, keepdims=True)
            chance = (expo * (1.0 / total)).astype(bf16)
            rows = slice(h * HEAD_DIM, (h + 1) * HEAD_DIM)
            mt[j, rows, :] = dot(vt[j, rows, :], chance)
            lse[3 * j + h : 3 * j + h + 1, :] = top + jnp.log(total)
    total = 0.0
    for j in range(2):
        mj = mt[j].T.astype(bf16)
        mixed[j] = mj
        total += dot(mj, w[j, 1, :, FEAT:WIDE], 1, 1)
    part[...] = total
    put_sides(total, lows)


def sides(left, right):
    return jnp.concatenate([left[...], right[...]], 1).astype(f32)


def put_sides(total, parts):
    parts[0][...] = total[:, :WIDE].astype(bf16)
    parts[1][...] = total[:, WIDE:].astype(bf16)


def k_norm2(scal, count, x, part, oth_l, oth_r, vec, c, d, resid, low, low_t, grad, grad_t, buf):
    r = x[...].astype(f32) + part[...] + sides(oth_l, oth_r) + vec[4:5, :]
    resid[...] = r
    v = norm(r, vec[5:6, :], vec[6:7, :])[2].astype(bf16)
    low[...] = v
    low_t[...] = v.T
    assemble(scal, c.at[0], c.at[1], d.at[0], d.at[1], buf)
    g = jnp.where(kept_rows(scal, count), buf[...], 0.0).astype(bf16)
    grad[...] = g
    grad_t[...] = g.T


def gelu_both(v):
    half = 0.5 * (1.0 + lax.erf(v * 0.7071067811865476))
    slope = half + v * jnp.exp(-0.5 * v * v) * 0.3989422804014327
    return v * half, slope


def ffn_kernel(parts, first, last):
    n = len({r for r, _ in parts})

    def kernel(scal, *refs):
        low, low_t, grad, grad_t = refs[:4]
        pieces, refs = refs[4 : 4 + n], refs[4 + n :]
        if not first:
            old_out, old_back, *refs = refs
        if last:
            keep, give, back, *refs = refs
            lows, refs = refs[:2], refs[2:]
        else:
            out, back, *refs = refs
        g_in, g_out, ein, cout = refs
        for s, (r, i) in enumerate(parts):
            src = pieces[r] if i is None else pieces[r].at[i]
            place = pl.ds(pl.multiple_of((scal[2] ^ s) * FEAT, FEAT), FEAT)
            ein[place, :] = src[0:FEAT, :]
            cout[place, :] = src[FEAT:WIDE, :]
            if s == 0:
                bias = src[WIDE:FPIECE, :].astype(f32)[0:1]
        act, slope = gelu_both(dot(low[...], ein[...]) + bias)
        hidden = act.astype(bf16)
        g = (dot(grad[...], cout[...]) * slope).astype(bf16)
        res = dot(hidden, cout[...], 1, 1)
        if not first:
            res = res + old_out[...]
        if last:
            core = scal[0] == 0
            a, b = res[:, :WIDE], res[:, WIDE:]
            keep[...] = jnp.where(core, a, b)
            give[...] = jnp.where(core, b, a).astype(bf16)
        else:
            out[...] = res
        res = dot(g, ein[...], 1, 1)
        if not first:
            res = res + old_back[...]
        back[...] = res
        if last:
            put_sides(res, lows)
        g_in[0:D, :] = dot(low_t[...], g).astype(bf16)
        sums = jnp.sum(g.astype(f32), 0, keepdims=True)
        g_in[D : D + 16, :] = jnp.broadcast_to(sums, (16, WIDE)).astype(bf16)
        g_out[...] = dot(grad_t[...], hidden).astype(bf16)

    return kernel


def ffn(scal, rows, pieces, parts, acc, last=False):
    if last:
        outs = [((ROWS, WIDE), f32), ((ROWS, WIDE), bf16), ((ROWS, D), f32)] + [((ROWS, WIDE), bf16)] * 2
    else:
        outs = [((ROWS, D), f32), ((ROWS, D), f32)]
    outs += [((D + 16, WIDE), bf16), ((D, WIDE), bf16)]
    return call(ffn_kernel(parts, acc is None, last), outs, scal, *rows, *pieces, *(acc or ()),
                scratch=[pltpu.VMEM((D, WIDE), bf16)] * 2, name="ffn")


def place_rows(scal, v, out1, out2):
    even = scal[2] % 2 == 0
    q = []
    for i in range(2):
        part = v[:, i * FEAT : (i + 1) * FEAT]
        q.append(jnp.concatenate([part[0:HALF], part[PAD : PAD + HALF]], 1))
    out1[...] = jnp.where(even, q[0], q[1]).astype(bf16)
    out2[...] = jnp.where(even, q[1], q[0]).astype(bf16)


def k_back(scal, resid, back, oth_l, oth_r, gml, vec, gres, branch, vrows):
    gnm = back[...] + sides(oth_l, oth_r)
    normed, inverse, _ = norm(resid[...], vec[5:6, :], vec[6:7, :])
    g = gml[...].astype(f32)
    res = g + norm_back(gnm, normed, inverse, vec[5:6, :])
    gres[...] = res
    low = res.astype(bf16)
    branch[...] = low
    vrows[...] = jnp.zeros_like(vrows)
    vrows[4:5, :] = jnp.sum(low.astype(f32), 0, keepdims=True)
    vrows[5:6, :] = jnp.sum(gnm * normed, 0, keepdims=True)
    vrows[6:7, :] = jnp.sum(gnm, 0, keepdims=True)
    vrows[7:8, :] = jnp.sum(g, 0, keepdims=True)


def heads_back(j, scal, count, branch, w, q, k, v, lse, mixed, old, gqk, gv, part, lows, gmt, kt, qt, dqt):
    keep = kept_rows(scal, count)
    lane = lax.broadcasted_iota(jnp.int32, (1, FEAT), 1) // HEAD_DIM
    none = jnp.zeros((), bf16)
    gm_low = dot(branch[...], w[j, 1, :, FEAT:WIDE]).astype(bf16)
    gmt[...] = gm_low.T
    kt[...] = k[j].T
    qt[...] = q[j].T
    prod_t = (gm_low.astype(f32) * mixed[j].astype(f32)).T
    dks, dvs = [], []
    for h in range(3):
        rows = slice(h * HEAD_DIM, (h + 1) * HEAD_DIM)
        delta = jnp.sum(prod_t[rows, :], 0, keepdims=True)
        logits = jnp.where(keep, dot(jnp.where(lane == h, k[j], none), qt[...]), -1e30)
        chance = jnp.exp(logits - lse[3 * j + h : 3 * j + h + 1, :])
        gchance = dot(jnp.where(lane == h, v[j], none), gmt[...])
        gl = (chance * (gchance - delta)).astype(bf16)
        dvs.append(dot(chance.astype(bf16), gm_low[:, rows]))
        dks.append(dot(gl, q[j][:, rows]))
        dqt[rows, :] = dot(kt[rows, :], gl) * 0.125
    gq = dqt[...].T
    both = jnp.concatenate([gq] + dks, 1).astype(bf16)
    gqk[...] = both
    val = jnp.concatenate(dvs, 1).astype(bf16)
    gv[...] = val
    total = dot(both, w[j, 0], 1, 1) + dot(val, w[j, 1, :, 0:FEAT], 1, 1)
    if old is not None:
        total = total + old[...]
        put_sides(total, lows)
    part[...] = total


def k_back0(scal, count, branch, w, q, k, v, lse, mixed, gqk, gv, part, *scratch):
    heads_back(0, scal, count, branch, w, q, k, v, lse, mixed, None, gqk, gv, part, None, *scratch)


def k_back1(scal, count, branch, w, q, k, v, lse, mixed, old, gqk, gv, part, *refs):
    heads_back(1, scal, count, branch, w, q, k, v, lse, mixed, old, gqk, gv, part, refs[:2], *refs[2:])


def rows_result(scal, count, resid, keep, got, vec, out1, out2):
    first = scal[0] == 0
    r = jnp.where(first, resid[:, 0:WIDE], resid[:, WIDE:D])
    b = jnp.where(first, vec[7:8, 0:WIDE], vec[7:8, WIDE:D])
    r = r + keep[...] + got[...].astype(f32) + b
    place_rows(scal, jnp.where(kept_rows(scal, count), r, 0.0), out1, out2)


def k_front(scal, count, resid, keep, got, part, oth_l, oth_r, x, vec, gres, branch, gqk0, gqk1, gv0, gv1, mixed, ain_t, vrows,
            own, gx, gy, gd1, gd2, out1, out2, vfull, wbuf):
    core, hid, z = scal[0], scal[1], scal[2]
    gna = part[...] + sides(oth_l, oth_r)
    normed, inverse, _ = norm(x[...].astype(f32), vec[0:1, :], vec[1:2, :])
    res = gres[...] + norm_back(gna, normed, inverse, vec[0:1, :])
    first = core == 0
    rows_result(scal, count, resid, keep, got, vec, out1.at[0], out2.at[0])
    place_rows(scal, jnp.where(first, res[:, 0:WIDE], res[:, WIDE:D]), out1.at[1], out2.at[1])
    vfull[...] = vrows[...]
    vfull[0:1, :] = jnp.sum(gna * normed, 0, keepdims=True)
    vfull[1:2, :] = jnp.sum(gna, 0, keepdims=True)
    branch_t = branch[...].T
    dest = lambda i, p, j: ((own, gx, gy)[i].at[2 * p + j] if i < 3 else (gd1, gd2)[p].at[j])
    for j in range(2):
        gqk, gv = ((gqk0, gv0), (gqk1, gv1))[j]
        wbuf[0] = dot(ain_t[...], gqk[...]).astype(bf16)
        wbuf[1, :, 0:FEAT] = dot(ain_t[...], gv[...]).astype(bf16)
        wbuf[1, :, FEAT:WIDE] = dot(branch_t, mixed[j]).astype(bf16)
        src = z ^ (2 * core + j)
        mine = vfull[:, 0:FEAT]
        for i in (1, 2, 3):
            mine = jnp.where(src == i, vfull[:, i * FEAT : (i + 1) * FEAT], mine)
        line = lax.broadcasted_iota(jnp.int32, (8, 1), 0)
        cols_q = jnp.sum(gqk[...].astype(f32), 0, keepdims=True)[:, 0:FEAT]
        cols_v = jnp.sum(gv[...].astype(f32), 0, keepdims=True)
        mine = jnp.where(line == 2, cols_q, jnp.where(line == 3, cols_v, mine))
        mine = jnp.concatenate([mine, jnp.zeros_like(mine)], 1)
        mine = jnp.concatenate([mine, jnp.zeros_like(mine)], 0).astype(bf16)
        for i in range(4):
            for p in range(2):
                at = pl.multiple_of((4 * (core ^ p) + (hid ^ i)) * UNITS, 32)
                to = dest(i, p, j)
                to[0:UNITS, :] = wbuf[0, pl.ds(at, UNITS), :]
                to[UNITS : 2 * UNITS, :] = wbuf[1, pl.ds(at, UNITS), :]
                to[2 * UNITS : APIECE, :] = mine


def plus(a, b):
    return a.astype(f32) + b.astype(f32)


def k_plus(a, b, out):
    out[...] = plus(a[...], b[...]).astype(out.dtype)


def k_fsum(scal, near_in, near_out, xb, yb, keep, s1, s2, s3):
    z = scal[2]
    for k, to in enumerate((keep, s1, s2, s3)):
        rows = pl.ds(pl.multiple_of((z ^ k) * FEAT, FEAT), FEAT)
        tail = slice(D, D + 16)
        to[0:FEAT, :] = (near_in[rows, :] + yb[rows, :].astype(f32)).astype(to.dtype)
        to[FEAT:WIDE, :] = (near_out[rows, :] + xb[rows, :].astype(f32)).astype(to.dtype)
        to[WIDE:FPIECE, :] = (near_in[tail, :] + yb[tail, :].astype(f32)).astype(to.dtype)


def k_zadd(s3, *refs):
    *r2, t3 = refs
    n = s3.shape[0] // len(r2)
    for i, r in enumerate(r2):
        rows = slice(i * n, (i + 1) * n)
        t3[rows, :] = plus(s3[rows, :], r[...]).astype(bf16)


def k_ffin(keep, r1, r3, ex, con_t, bias):
    v = keep[...] + r1[...].astype(f32) + r3[...].astype(f32)
    ex[...] = v[0:FEAT]
    con_t[...] = v[FEAT:WIDE]
    bias[...] = v[WIDE]


def k_aadd(gx, ry, gy, rx, px, py):
    px[0:2] = gx[0:2]
    px[2:4] = plus(gx[2:4], ry[...]).astype(bf16)
    py[0:2] = plus(gy[0:2], rx[...]).astype(bf16)
    py[2:4] = gy[2:4]


def k_asum(own, sx, sy, keep, give0, give1):
    keep[...] = plus(own[0:2], sx[0:2]) + sy[0:2].astype(f32)
    give = (plus(own[2:4], sx[2:4]) + sy[2:4].astype(f32)).astype(bf16)
    give0[...] = give[0]
    give1[...] = give[1]


def k_asel(scal, keep, got0, got1, s0, s1, s3, s2a, s2b):
    first = scal[0] == 0
    a, b = keep[0], got0[...].astype(f32)
    s0[...] = jnp.where(first, a, b)
    hi = jnp.where(first, b, a).astype(bf16)
    n = APIECE // 2
    s2a[...] = hi[0:n]
    s2b[...] = hi[n:APIECE]
    a, b = keep[1], got1[...].astype(f32)
    s1[...] = jnp.where(first, a, b).astype(bf16)
    s3[...] = jnp.where(first, b, a).astype(bf16)


def k_afin(s0, r1, r3, pin, pout, vec):
    v = s0[...] + r1[...].astype(f32) + r3[...].astype(f32)
    pin[0] = v[0:UNITS, 0:FEAT]
    pin[1] = v[0:UNITS, FEAT:WIDE]
    pin[2] = v[UNITS : 2 * UNITS, 0:FEAT]
    pout[...] = v[UNITS : 2 * UNITS, FEAT:WIDE].T
    vec[...] = v[2 * UNITS : 2 * UNITS + 8, 0:FEAT]


def k_home(scal, b1, b2, to):
    even = scal[2] % 2 == 0
    left = lax.broadcasted_iota(jnp.int32, (1, WIDE), 1) < FEAT
    a, b = b1[...], b2[...]
    s0, s1 = jnp.where(even, a, b), jnp.where(even, b, a)
    t = to.dtype
    to[0 : HALF - 1, 0, :] = s0[0 : HALF - 1].astype(t)
    to[HALF - 1 : HALF, 0, :] = jnp.where(left, s0[HALF - 1 : HALF].astype(f32), s1[0:1].astype(f32)).astype(t)
    to[HALF:L, 0, :] = s1[1:HALF].astype(t)


def k_home_both(scal, b1, b2, out, grad):
    k_home(scal, b1.at[0], b2.at[0], out)
    k_home(scal, b1.at[1], b2.at[1], grad)


def body(patches, visible, project_in, project_out, expand, contract, expand_bias, vectors, cotangent):
    n_dp = lax.axis_size("dp")
    more = n_dp // 2
    dp, hid, z = lax.axis_index("dp"), lax.axis_index("hid"), lax.axis_index("mod")
    core = dp % 2
    place = 4 * core + hid
    if more > 1:
        def mine_of(v, dim):
            whole = lax.all_gather(v, ("dp", "hid"), axis=dim, tiled=True)
            size = whole.shape[dim] // 8
            return lax.dynamic_slice_in_dim(whole, place * size, size, dim)

        project_in, project_out = mine_of(project_in, 1), mine_of(project_out, 1)
        expand, contract = mine_of(expand, 1), mine_of(contract, 0)
        expand_bias = mine_of(expand_bias, 0)

    where = jnp.stack([core, hid, z]).astype(jnp.int32)
    fpart, apart = (FPIECE, WIDE), (APIECE, WIDE)
    del ORDER[:]
    block, pair = ((HALF, WIDE), bf16), ((2, HALF, WIDE), bf16)
    wide, tall = ((ROWS, D), bf16), ((D, ROWS), bf16)
    rows32, half = ((ROWS, D), f32), ((ROWS, WIDE), bf16)
    head = ((2, ROWS, FEAT), bf16)
    four, two = ((4, APIECE, WIDE), bf16), ((2, APIECE, WIDE), bf16)
    in_shape, out_shape = (D + 16, WIDE), (D, WIDE)

    a0 = call(k_pack_attn, [(apart, bf16)], None, project_in, project_out, vectors, name="pack_attn")
    f0 = call(k_pack_ffn, [(fpart, bf16)], None, expand, contract.T, expand_bias, name="pack_ffn")
    a1, a2, a3 = z_all(a0)
    fx, fy = over_x(f0), over_y(f0)
    p1, p2, c1, c2 = call(
        k_in_each, [block] * 4, where, patches.reshape(L, 1, WIDE), cotangent.reshape(L, 1, WIDE), seen=visible, name="rows_in")
    f1, f3 = z_one(f0), z_three(f0)
    f2 = z_one(f3)
    keeps, vec, slots, *gives = call(
        k_give, [((2, 2 * UNITS, WIDE), bf16), ((8, D), f32), ((2, 8, FEAT), f32)] + [((2 * UNITS, WIDE), bf16)] * 2,
        where, a0, a1, a2, a3, name="give")
    got = exchange(gives)
    got[0] = after(got[0], fx, fy)
    here = call(k_join, [((4, 2 * UNITS, WIDE), bf16)], None, keeps, *got, name="join_attn")
    from_x, from_y = over_x(here), over_y(here)
    to_x, to_y = call(k_cross, [((2, 2 * UNITS, WIDE), bf16)] * 2, None, from_x, from_y, name="cross_attn")
    diag_a, diag_b = over_x(to_x), over_y(to_y)
    p1, p2 = after((p1, p2), f1, f3, to_x)
    p1, p2 = rows_there(p1, False), rows_there(p2, True)
    c1, c2 = after((c1, c2), f1, f3)
    c1, c2 = rows_there(c1, False), rows_there(c2, True)
    f123 = call(k_three, [((3,) + fpart, bf16)], None, f1, f2, after(f3, diag_a, diag_b), name="join_ffn")
    fx123, fy123 = over_x(f123), over_y(f123)
    q1, q2 = exchange([p1, p2])

    x, ain, ain_t, count = call(
        k_norm1, [wide, wide, tall, ((8, 128), f32)], where, p1, p2, q1, q2, vec, scratch=[pltpu.VMEM((ROWS, D), f32)], name="norm_attn")
    flip = (2, FEAT, ROWS)
    w, q, k, v, lse, mixed, part, *lows = call(
        k_attn, [((2, 2, D, WIDE), bf16), head, head, head, ((8, ROWS), f32), head, rows32, half, half], where,
        count, ain, here, from_x, from_y, diag_a, diag_b, slots,
        scratch=[pltpu.VMEM(flip, bf16), pltpu.VMEM(flip, bf16), pltpu.VMEM(flip, f32)], name="attend")
    oths = exchange(lows)
    c = call(k_pair, [pair], None, c1, c2, name="join_rows")
    d = over_core(c)
    resid, low, low_t, gml, gml_t = call(
        k_norm2, [rows32, wide, tall, wide, tall], where, count, x, part, *oths, vec, c, d,
        scratch=[pltpu.VMEM((ROWS, D), f32)], name="norm_mlp")

    rows = (low, low_t, gml, gml_t)
    to_x, to_y = call(k_far, [((2,) + fpart, bf16)] * 2, None, fy, fy123, fx123, name="far_ffn")
    fd_a, fd_b = over_x(to_x), over_y(to_y)
    near = [(0, None), (1, 0), (1, 1), (1, 2)]
    out, back, x_in, x_out = ffn(where, rows, (fx, fx123), near, None)
    sxa = over_x(x_in)
    out, back, y_in, y_out = ffn(where, rows, (fy, fy123), near, (out, back))
    sya = over_y(y_out)
    out, back, own_in, own_out = ffn(where, rows, (f0, f123), near, (out, back))
    keep, give, back, low_l, low_r, d_in, d_out = ffn(
        where, rows, (fd_a, fd_b), [(0, 0), (0, 1), (1, 0), (1, 1)], (out, back), last=True)
    oths = exchange([low_l, low_r])
    rx, ry = over_x(d_in), over_y(d_out)
    got_out = over_core(give)

    gres, branch, vrows = call(k_back, [rows32, wide, ((8, D), f32)], where, resid, back, *oths, gml, vec, name="norm_mlp_back")
    side = pltpu.VMEM((FEAT, ROWS), bf16)
    work = [side, side, side, pltpu.VMEM((FEAT, ROWS), f32)]
    one, thin = ((ROWS, WIDE), bf16), ((ROWS, FEAT), bf16)
    kept = (count, branch, w, q, k, v, lse, mixed)
    gqk0, gv0, part = call(k_back0, [one, thin, rows32], where, *kept, scratch=work, name="attend_back")
    gqk1, gv1, part, *lows = call(k_back1, [one, thin, rows32, half, half], where, *kept, part, scratch=work, name="attend_back")
    oths = exchange(lows)
    near_in = call(k_plus, [(in_shape, f32)], None, own_in, sxa, name="sum_x")
    near_out = call(k_plus, [(out_shape, f32)], None, own_out, sya, name="sum_y")
    ga_own, ga_x, ga_y, ga_d1, ga_d2, r1, r2 = call(
        k_front, [four, four, four, two, two, pair, pair], where, count, resid, keep, got_out, part, *oths, x, vec, gres, branch,
        gqk0, gqk1, gv0, gv1, mixed, ain_t, vrows, scratch=[pltpu.VMEM((8, D), f32), pltpu.VMEM((2, D, WIDE), bf16)], name="norm_attn_back")

    ax, ay = over_x(ga_d1), over_y(ga_d2)
    xb = call(k_plus, [(out_shape, bf16)], None, x_out, ry, name="add_x")
    yb = call(k_plus, [(in_shape, bf16)], None, y_in, rx, name="add_y")
    sxb, syb = over_x(xb), over_y(yb)
    px, py = call(k_aadd, [four, four], None, ga_x, ay, ga_y, ax, name="attn_add")
    tx, ty = over_x(px), over_y(py)
    r1, r2 = rows_back(after(r1, px), False), rows_back(r2, True)
    result, grad_input = call(k_home_both, [((L, 1, WIDE), bf16), ((L, 1, WIDE), f32)], where, r1, r2, name="rows_out")
    result, grad_input = result.reshape(1, L * WIDE), grad_input.reshape(1, L * WIDE)
    fk, s1, s2, s3 = call(k_fsum, [(fpart, f32)] + [(fpart, bf16)] * 3, where, near_in, near_out, sxb, syb, name="ffn_sum")
    g2, g1 = z_one(s2), z_one(s1)
    g3 = z_three(call(k_zadd, [(fpart, bf16)], None, s3, g2, name="ffn_zadd"))
    ak, *gives = call(k_asum, [((2,) + apart, f32), (apart, bf16), (apart, bf16)], None, ga_own, tx, ty, name="attn_sum")
    got = exchange(gives)
    cut = ((APIECE // 2, WIDE), bf16)
    s0, s1, s3, *s2 = call(k_asel, [(apart, f32), (apart, bf16), (apart, bf16), cut, cut], where, ak, *got, name="attn_slots")
    t2, t1 = [z_one(s) for s in s2], z_one(s1)
    expand_grad, contract_grad, bias_grad = call(
        k_ffin, [((FEAT, WIDE), f32), ((FEAT, WIDE), f32), ((WIDE,), f32)], None, fk, g1, g3, name="ffn_last")
    t3 = z_three(call(k_zadd, [(apart, bf16)], None, s3, *t2, name="attn_zadd"))
    in_grad, out_grad, vector_grad = call(
        k_afin, [((3, UNITS, FEAT), f32), ((FEAT, UNITS), f32), ((8, FEAT), f32)], None, s0, t1, t3, name="attn_last")
    contract_grad = contract_grad.T

    if more > 1:
        def spread(v, dim):
            whole = jnp.zeros(v.shape[:dim] + (8 * v.shape[dim],) + v.shape[dim + 1 :], f32)
            whole = lax.dynamic_update_slice_in_dim(whole, v, place * v.shape[dim], dim)
            return lax.psum_scatter(whole, ("dp", "hid"), scatter_dimension=dim, tiled=True)

        in_grad, out_grad = spread(in_grad, 1), spread(out_grad, 1)
        expand_grad, contract_grad, bias_grad = spread(expand_grad, 1), spread(contract_grad, 0), spread(bias_grad, 0)
        vector_grad = lax.psum(vector_grad, "dp") / 2
    return result, grad_input, in_grad, out_grad, expand_grad, contract_grad, bias_grad, vector_grad


def solution(mesh):
    rows = P("mod", ("dp", "hid"))
    in_specs = (rows, P(("dp", "hid")), P(None, ("dp", "hid"), "mod"), rows, rows, P(("dp", "hid"), "mod"),
                P(("dp", "hid")), P(None, "mod"), rows)
    out_specs = (rows, rows, P(None, ("dp", "hid"), "mod"), rows, rows, P(("dp", "hid"), "mod"),
                 P(("dp", "hid")), P(None, "mod"))
    return jax.shard_map(body, mesh=mesh, in_specs=in_specs, out_specs=out_specs, check_vma=False)
```
